512 devices in a mesh: wide: 64 (over y, z_hi, x), narrow: 8 (over z_lo, core).
Axes of the slice: x: 4, y: 8, z: 8 (z_hi: 2, z_lo: 4; z = z_hi * 4 + z_lo), core: 2. Of those that a mesh axis runs over, the one named last changes fastest.
Arguments:
- eta_modes: float32 [2, 2048, 2048], P(None, 'wide', 'narrow'), may hold values from -6 to 6
- phi_modes: float32 [2, 2048, 2048], P(None, 'wide', 'narrow'), may hold values from -6 to 6
- zone_field: float32 [4096, 128], P('wide'), may hold values from -6 to 6
- offsets: int32 [64, 2], replicated, may hold values from 0 to 2047
Outputs:
- eta_next: float32 [2, 2048, 2048], P(None, 'wide', 'narrow')
- phi_next: float32 [2, 2048, 2048], P(None, 'wide', 'narrow')
The draws below stay inside these ranges and needn't reach their ends.
Inputs may be any that keep to these rules, and one draw needn't show every extreme that they name: Row t of offsets gives the HOS grid cell (x, y) of zone tile t's first cell; tiles may intersect and wrap around the periodic grid.
All inputs are finite; a program needn't handle non-finite values.
Results may differ from the reference program's by a relative error of at most 0.00005.
Values sent between devices are 32-bit elements; how exact they have to be, the bound alone decides.
No kernel may reach another device: no remote copies, remote signals or barrier semaphores. Data moves between devices by JAX's collectives and lax.ppermute only.
A program may use at most 128 MiB of HBM per device.

```python
import math
import jax
import jax.numpy as jnp
from jax import lax

NX = 2048
NY = 2048
ZC = 128
TILE_ROWS = 64
TILES = 64
ZONE_ROWS = 4096


def with_ends(drawn, stream_key, low, largest):
    longest = drawn.shape.index(max(drawn.shape))
    spots = []
    for shift in (0, 1):
        where = [jax.random.randint(jax.random.fold_in(stream_key, axis), (), 0, length) for axis, length in enumerate(drawn.shape)]
        where[longest] = (where[longest] + shift) % drawn.shape[longest]
        spots.append(tuple(where))
    return drawn.at[spots[0]].set(low).at[spots[1]].set(largest)


def block_scale(own_key, shape, cuts, smallest, high):
    factor_of, own = 1.0, jax.random.fold_in(own_key, 6)
    for dim, shards_of in cuts:
        steps = jnp.exp(jax.random.uniform(jax.random.fold_in(own, dim), (shards_of,), jnp.float32, smallest / len(cuts), high / len(cuts)))
        factor_of = factor_of * jnp.repeat(steps, shape[dim] // shards_of).reshape([-1 if axis == dim else 1 for axis in range(len(shape))])
    return factor_of


def normal_values(rng, shape, scale, bound, split=(), held_as=jnp.bfloat16):
    entries = jax.random.normal(rng, shape, jnp.float32) * scale
    if len(split) > 0:
        entries = block_scale(rng, shape, split, -0.22, 0.18) * entries
    return jnp.clip(entries, min=-bound, max=bound).astype(held_as)


def setup_inputs(seed: int = 0) -> dict:
    streams_of = jax.random.split(jax.random.key(seed), 5)
    eta_modes = normal_values(streams_of[0], (2, NY, NX), 1.0, 6.0, ((1, 64), (2, 8)), jnp.float32)
    phi_modes = normal_values(streams_of[1], (2, NY, NX), 1.0, 6.0, ((1, 64), (2, 8)), jnp.float32)
    zone_field = normal_values(streams_of[2], (ZONE_ROWS, ZC), 1.0, 6.0, ((0, 64),), jnp.float32)
    offsets = with_ends(jax.random.randint(streams_of[3], (TILES, 2), 0, min(NX, NY)), jax.random.fold_in(streams_of[3], 1), 0, (min(NX, NY)) - 1).astype(jnp.int32)
    return {"eta_modes": eta_modes, "phi_modes": phi_modes, "zone_field": zone_field, "offsets": offsets}


time_step = 0.04
gravity = 9.81
highest = lax.Precision.HIGHEST

def signed_wave(length):
    indices = jnp.arange(length, dtype=jnp.int32)
    return jnp.where(indices < length // 2, indices, indices - length).astype(jnp.int32)

def turn_table(first_ints, second_ints, period):
    phases = (first_ints * second_ints % period).astype(jnp.float32) * (2.0 * math.pi / period)
    return (jnp.cos(phases), jnp.sin(phases))

def reference(eta_modes, phi_modes, zone_field, offsets):
    spread = 1.0 / math.sqrt(NX * NY)
    zone_scale = 1.0 / math.sqrt(ZONE_ROWS * ZC)
    wave_x = signed_wave(NX)
    wave_y = signed_wave(NY)
    grid_x = (2.0 * math.pi / NX * wave_x.astype(jnp.float32))[None, :]
    grid_y = (2.0 * math.pi / NY * wave_y.astype(jnp.float32))[:, None]
    kappa_abs = jnp.sqrt(grid_x * grid_x + grid_y * grid_y)
    eta_complex = eta_modes[0] + 1j * eta_modes[1]
    phi_complex = phi_modes[0] + 1j * phi_modes[1]

    def physical(spectrum):
        return jnp.real(jnp.fft.ifft2(spectrum)) * (NX * NY * spread)

    def spectral(surface):
        return jnp.fft.fft2(surface) * spread
    slope_ex = physical(1j * grid_x * eta_complex)
    slope_ey = physical(1j * grid_y * eta_complex)
    slope_px = physical(1j * grid_x * phi_complex)
    slope_py = physical(1j * grid_y * phi_complex)
    lift_speed = physical(kappa_abs * phi_complex)
    steepness = slope_ex * slope_ex + slope_ey * slope_ey
    first_order = lift_speed * steepness - (slope_px * slope_ex + slope_py * slope_ey)
    second_term = 0.5 * (lift_speed * lift_speed - slope_px * slope_px - slope_py * slope_py)
    rows_zone = jnp.arange(ZONE_ROWS, dtype=jnp.int32)
    tile_of_row = (rows_zone // TILE_ROWS).astype(jnp.int32)
    within = (rows_zone % TILE_ROWS).astype(jnp.int32)
    off_x = offsets[tile_of_row, 0]
    off_y = offsets[tile_of_row, 1]
    zone_columns = jnp.arange(ZC, dtype=jnp.int32)
    cos_zoom, sin_zoom = turn_table(zone_columns[:, None], wave_x[None, :], 2 * NX)
    half_real = jnp.dot(zone_field, cos_zoom, precision=highest, preferred_element_type=jnp.float32)
    half_imag = -jnp.dot(zone_field, sin_zoom, precision=highest, preferred_element_type=jnp.float32)
    cos_shift, sin_shift = turn_table(off_x[:, None], wave_x[None, :], NX)
    proj_real = half_real * cos_shift + half_imag * sin_shift
    proj_imag = half_imag * cos_shift - half_real * sin_shift
    cos_rows, sin_rows = turn_table(wave_y[:, None], (2 * off_y + within)[None, :], 2 * NY)
    force_real = (jnp.dot(cos_rows, proj_real, precision=highest, preferred_element_type=jnp.float32) + jnp.dot(sin_rows, proj_imag, precision=highest, preferred_element_type=jnp.float32)) * zone_scale
    force_imag = (jnp.dot(cos_rows, proj_imag, precision=highest, preferred_element_type=jnp.float32) - jnp.dot(sin_rows, proj_real, precision=highest, preferred_element_type=jnp.float32)) * zone_scale
    first_modes = spectral(first_order)
    second_modes = spectral(second_term)
    eta_real = eta_modes[0] + time_step * (kappa_abs * phi_modes[0] + jnp.real(first_modes)) + force_real
    eta_imag = eta_modes[1] + time_step * (kappa_abs * phi_modes[1] + jnp.imag(first_modes)) + force_imag
    phi_real = phi_modes[0] + time_step * (-gravity * eta_modes[0] + jnp.real(second_modes))
    phi_imag = phi_modes[1] + time_step * (-gravity * eta_modes[1] + jnp.imag(second_modes))
    eta_next = jnp.stack([eta_real, eta_imag]).astype(jnp.float32)
    phi_next = jnp.stack([phi_real, phi_imag]).astype(jnp.float32)
    return (eta_next, phi_next)
```

```python
import functools
import math

import jax
import jax.numpy as jnp
import ml_dtypes
import numpy as np
from jax import lax
from jax.experimental import pallas as pl
from jax.experimental.pallas import tpu as pltpu
from jax.sharding import PartitionSpec as P

NX = 2048
NY = 2048
FINE = 4096
BOTH = ("wide", "narrow")
TURN_X = 2.0 * math.pi / NX
TURN_Y = 2.0 * math.pi / NY
time_step = 0.04
gravity = 9.81
spread = 1.0 / math.sqrt(NX * NY)
zone_scale = 1.0 / math.sqrt(4096 * 128)
f32 = jnp.float32
bf16 = jnp.bfloat16
VMEM_LIMIT = 56 * 1024 * 1024


def part(value, which):
    return np.where(which == 0, np.real(value), np.imag(value))


def angles(ints, period):
    return 2.0 * np.pi * (np.asarray(ints) % period) / period


def pair(matrix):
    high = matrix.astype(np.float32).astype(ml_dtypes.bfloat16)
    low = (matrix - high.astype(np.float64)).astype(np.float32).astype(ml_dtypes.bfloat16)
    return high, low


@functools.cache
def tables():
    out = {}
    row = np.arange(512)
    h, a, jj, slot = row // 256, row // 128 % 2, row // 32 % 4, row % 32
    f, i = slot // 4, slot % 4
    col = np.arange(320)
    cn, cf, ca, cj = col // 40, col // 8 % 5, col // 4 % 2, col % 4
    x0 = 4 * h + i
    turn = np.exp(1j * angles(x0[:, None] * cn[None, :], 8))
    turn = turn * np.where(cf < 4, 1j, 1.0)[None, :] * (1j ** ca)[None, :]
    same = (f[:, None] == cf[None, :]) & (jj[:, None] == cj[None, :])
    first = np.where(same, part(turn, a[:, None]), 0.0)
    second = np.where(same, part(1j * turn, a[:, None]), 0.0)
    out["rows"] = pair(np.concatenate([first, second], 0))
    k256 = np.arange(256)
    lanes_x0 = 4 * np.arange(2)[:, None] + np.arange(8)[None, :] % 4
    phase = angles(lanes_x0[:, :, None] * k256, NX)
    out["rows_turn"] = (np.cos(phase).astype(np.float32), np.sin(phase).astype(np.float32))
    phase = angles(k256[:, None] * k256[None, :], 256)
    out["x"] = pair(np.concatenate([np.cos(phase), np.sin(phase)], 1))
    k512 = np.arange(512)
    phase = angles(k512[:, None] * k512[None, :], 512)
    out["y"] = pair(np.concatenate([np.cos(phase), np.sin(phase)], 1))
    lane = np.arange(128)
    phase = angles(k512[:, None] * (lane // 32)[None, :], NY)
    out["y_turn"] = (np.cos(phase).astype(np.float32), np.sin(phase).astype(np.float32))
    phase = angles(k512[:, None] * (lane % 32 // 8)[None, :], NY)
    out["y_back"] = (np.cos(phase).astype(np.float32), np.sin(phase).astype(np.float32))
    ljj, lf, li = lane // 32, lane % 32 // 4, lane % 4
    gather = np.zeros((2, 128, 5, 128))
    for y0 in range(4):
        for k in range(128):
            if lf[k] < 5:
                value = np.round(np.exp(1j * angles(ljj[k] * y0, 4)) * 2) / 2
                gather[0, k, lf[k], y0 * 4 + li[k]] = value.real * spread
                gather[1, k, lf[k], y0 * 4 + li[k]] = -value.imag * spread
    out["gather"] = gather.reshape(256, 640).astype(ml_dtypes.bfloat16)
    deal = np.zeros((2, 128, 2, 128))
    for k in range(64):
        ka, kj, kf, ki = k // 32, k // 8 % 4, k // 4 % 2, k % 4
        for y0 in range(4):
            value = np.round(np.exp(-1j * angles(kj * y0, 4)) * 2) / 2
            deal[kf, y0 * 4 + ki, 0, k] = part(value, ka)
            deal[kf, y0 * 4 + ki, 1, k] = part(-1j * value, ka)
    out["deal"] = deal.reshape(256, 256).astype(ml_dtypes.bfloat16)
    row = np.arange(128)
    h, a, jj, f, i = row // 64, row // 32 % 2, row // 8 % 4, row // 4 % 2, row % 4
    x0 = 4 * h + i
    z0, za, zj = row // 8, row // 4 % 2, row % 4
    phase = np.concatenate([angles(x0[:, None] * k256, NX), angles(z0[:, None] * k256, FINE)], 0)
    out["back_turn"] = (np.cos(phase).astype(np.float32), np.sin(phase).astype(np.float32))
    on, of, oa, oj = row // 16, row // 8 % 2, row // 4 % 2, row % 4
    turn = np.exp(-1j * angles(on[:, None] * x0[None, :], 8)) * (1j ** a)[None, :]
    same = (of[:, None] == f[None, :]) & (oj[:, None] == jj[None, :])
    main = [np.where(same, part(turn * s, oa[:, None]), 0.0) for s in (1, -1j)]
    signed = np.where(on < 4, on, on - 8)
    turn = np.exp(-1j * angles(signed[:, None] * z0[None, :], 16)) * (1j ** za)[None, :]
    same = (of[:, None] == 0) & (oj[:, None] == zj[None, :])
    zone = [np.where(same, part(turn * s, oa[:, None]), 0.0) for s in (1, -1j)]
    out["back"] = pair(np.concatenate([main[0], zone[0], main[1], zone[1]], 1))
    return out


def split(value):
    high = value.astype(bf16)
    return high, (value - high.astype(f32)).astype(bf16)


def dot(left, right, dims=((1,), (0,))):
    return lax.dot_general(left, right, (dims, ((), ())), preferred_element_type=f32)


def dot3(left, right, dims=((1,), (0,))):
    return dot(left[0], right[0], dims) + (dot(left[0], right[1], dims) + dot(left[1], right[0], dims))


def iota(shape, dim):
    return lax.broadcasted_iota(jnp.int32, shape, dim)


def cos_of(phase):
    moved = phase + 512
    quarter = (moved >> 10) & 3
    angle = ((moved & 1023) - 512).astype(f32) * (2.0 * math.pi / FINE)
    square = angle * angle
    cosine = 1.0 + square * (-0.5 + square * (1.0 / 24 + square * (-1.0 / 720 + square * (1.0 / 40320))))
    sine = angle * (
        1.0 + square * (-1.0 / 6 + square * (1.0 / 120 + square * (-1.0 / 5040 + square * (1.0 / 362880))))
    )
    size = jnp.where((quarter & 1) == 0, cosine, sine)
    return jnp.where((quarter == 1) | (quarter == 2), -size, size)


def wave_of(index):
    return jnp.where(index < 1024, index, index - 2048).astype(f32)


def deal_kernel(eta, phi, out):
    for n in range(8):
        for source, base in ((eta, 0), (phi, 8)):
            for a in range(2):
                out[n, base + 4 * a : base + 4 * a + 4, :] = source[a, 4 * n : 4 * n + 4, :]


def source_kernel(place, offsets, zone, out):
    tile = place[0]
    own = place[1]
    ox = offsets[tile, 0]
    oy = offsets[tile, 1]
    lane = iota((128, 128), 1)
    wanted = (16 * own + (lane >> 3) - 2 * (ox & 7)) & 127
    pick = jnp.where(iota((128, 128), 0) == wanted, 1.0, 0.0).astype(bf16)
    high, low = split(zone[...] * zone_scale)
    cells = dot(high, pick) + dot(low, pick)
    lane = iota((64, 128), 1)
    phase = (lane & 3) * (2 * oy + iota((64, 128), 0)) + 1024 * ((lane >> 2) & 1)
    right = jnp.concatenate([cells * cos_of(phase), cells * cos_of(phase + 3072)], 0)
    lane = iota((512, 128), 1)
    m = iota((512, 128), 0)
    m = jnp.where(m < 256, m, m - 512)
    left = cos_of(4 * m * (2 * oy + (lane & 63)) + jnp.where(lane < 64, 0, 1024))
    out[...] = dot3(split(left), split(right))


def rows_kernel(place, modes, mix_high, mix_low, cos_turn, sin_turn, x_high, x_low, out):
    first_ky = 32 * place[0] + 4 * place[1]
    wave_y = wave_of(first_ky + (iota((8, 256), 0) & 3)) * TURN_Y
    tiles = []
    for n in range(8):
        wave_x = wave_of(256 * n + iota((8, 256), 1)) * TURN_X
        kappa = jnp.sqrt(wave_x * wave_x + wave_y * wave_y)
        eta = modes[n, 0:8, :]
        phi = modes[n, 8:16, :]
        tiles += [wave_x * eta, wave_y * eta, wave_x * phi, wave_y * phi, kappa * phi]
    rows = split(jnp.concatenate(tiles, 0))
    both = dot3((mix_high[...], mix_low[...]), rows)
    first = both[:512].reshape(2, 32, 8, 256)
    second = both[512:].reshape(2, 32, 8, 256)
    cosine = cos_turn[...][:, None]
    sine = sin_turn[...][:, None]
    turned = (first * cosine + second * sine).reshape(512, 256)
    quarter = (second * cosine - first * sine).reshape(512, 256)
    result = dot3(
        (x_high[...], x_low[...]), split(jnp.concatenate([turned, quarter], 1)), ((1,), (1,))
    )
    for g in range(4):
        out[pl.ds(g, 256, stride=4), :] = result[:, 128 * g : 128 * g + 128]


def columns_kernel(
    terms, source, y_high, y_low, cos_turn, sin_turn, gather, cos_back, sin_back, deal, out
):
    words = jnp.concatenate([terms[pl.ds(0, 512, stride=2), :], terms[pl.ds(1, 512, stride=2), :]], 1)
    high, low = split(words)
    with_cos = dot3((y_high[:, :512], y_low[:, :512]), (high, low))
    with_sin = dot3((y_high[:, 512:], y_low[:, 512:]), (high, low))
    real = with_cos[:, :128] - with_sin[:, 128:]
    imag = with_sin[:, :128] + with_cos[:, 128:]
    cosine = cos_turn[...]
    sine = sin_turn[...]
    high, low = split(
        jnp.concatenate([real * cosine - imag * sine, real * sine + imag * cosine], 1)
    )
    fields = dot(high, gather[...]) + dot(low, gather[...])
    slope_ex, slope_ey, slope_px, slope_py, lift = (
        fields[:, 128 * k : 128 * k + 128] for k in range(5)
    )
    first_order = lift * (slope_ex * slope_ex + slope_ey * slope_ey) - (
        slope_px * slope_ex + slope_py * slope_ey
    )
    second_term = 0.5 * (lift * lift - slope_px * slope_px - slope_py * slope_py)
    high, low = split(
        jnp.concatenate([first_order, second_term], 1) * (time_step * spread)
    )
    both = dot(high, deal[...]) + dot(low, deal[...])
    first = both[:, :128]
    second = both[:, 128:]
    cosine = cos_back[...]
    sine = sin_back[...]
    turned = jnp.concatenate([first * cosine + second * sine, second * cosine - first * sine], 0)
    out[pl.ds(0, 512, stride=2), :] = dot3((y_high[...], y_low[...]), split(turned))
    out[pl.ds(1, 512, stride=2), :] = source[...]


def rows_back_kernel(
    offsets, terms, x_high, x_low, cos_turn, sin_turn, mix_high, mix_low, out, cells, ends
):
    lane = iota((256, 128), 1)
    left = terms[pl.ds(0, 256, stride=4), :]
    right = terms[pl.ds(2, 256, stride=4), :]
    main = jnp.where(lane < 64, left, pltpu.roll(right, 64, 1))
    lane = iota((8, 128), 1)
    block = iota((8, 128), 0)
    spot = iota((8, 256), 1)
    depth = iota((8, 256), 0)
    places = []
    last_places = []
    base_rows = []
    for t in range(64):
        ox = offsets[t, 0]
        tile = terms[pl.ds(16 * t + 1, 8, stride=2), :]
        beyond = (block == 0) & (lane < 16 * (ox & 7))
        cells[8 * t : 8 * t + 8, :] = jnp.where(beyond, 0.0, tile)
        ends[t : t + 1, :] = jnp.where(beyond, tile, 0.0)[0:1, :]
        base = ox >> 3
        places.append(jnp.where(spot == ((base + depth) & 255), 1.0, 0.0))
        base_rows.append(base)
    for t in range(0, 64, 8):
        base = jnp.zeros((8, 256), jnp.int32)
        for k in range(8):
            base = jnp.where(depth == k, base_rows[t + k], base)
        last_places.append(jnp.where(spot == ((base + 8) & 255), 1.0, 0.0))
    where_to = jnp.concatenate(places + last_places, 0).astype(bf16)
    high, low = split(jnp.concatenate([cells[...].T, ends[...].T[:, :64]], 1))
    grid = dot(high, where_to) + dot(low, where_to)
    both = dot3(split(jnp.concatenate([main.T, grid], 0)), (x_high[...], x_low[...]))
    with_cos = both[:, :256]
    with_sin = both[:, 256:]
    cosine = cos_turn[...]
    sine = sin_turn[...]
    turned = jnp.concatenate(
        [with_cos * cosine - with_sin * sine, with_cos * sine + with_sin * cosine], 0
    )
    result = dot3((mix_high[...], mix_low[...]), split(turned))
    out[...] = result.reshape(8, 16, 256)


def finish_kernel(place, terms, eta, phi, eta_next, phi_next):
    first_ky = 32 * place[0]
    wave_x = wave_of(256 * place[1] + iota((32, 256), 1)) * TURN_X
    wave_y = wave_of(first_ky + iota((32, 256), 0)) * TURN_Y
    kappa = time_step * jnp.sqrt(wave_x * wave_x + wave_y * wave_y)
    for a in range(2):
        surface = eta[a]
        potential = phi[a]
        eta_next[a] = surface + kappa * potential
        phi_next[a] = potential - (time_step * gravity) * surface
        for n in range(8):
            rows = slice(4 * n, 4 * n + 4)
            eta_next[a, rows, :] += terms[n, 4 * a : 4 * a + 4, :]
            phi_next[a, rows, :] += terms[n, 8 + 4 * a : 12 + 4 * a, :]


def call(kernel, shapes, scalars, arrays, scratch=(), flops=0):
    single = isinstance(shapes, tuple)
    shapes = [shapes] if single else shapes
    vmem = pl.BlockSpec(memory_space=pltpu.VMEM)
    smem = pl.BlockSpec(memory_space=pltpu.SMEM)
    moved = sum(4 * math.prod(s) for s in shapes) + sum(x.size * x.dtype.itemsize for x in arrays)
    result = pl.pallas_call(
        kernel,
        out_shape=[jax.ShapeDtypeStruct(s, f32) for s in shapes],
        in_specs=[smem] * len(scalars) + [vmem] * len(arrays),
        out_specs=[vmem] * len(shapes),
        scratch_shapes=list(scratch),
        compiler_params=pltpu.CompilerParams(vmem_limit_bytes=VMEM_LIMIT),
        cost_estimate=pl.CostEstimate(flops=flops, bytes_accessed=moved, transcendentals=0),
        name=kernel.__name__,
    )(*scalars, *arrays)
    return result[0] if single else result


def stage_deal(eta, phi):
    return call(deal_kernel, (8, 16, 256), [], [eta, phi])


def stage_source(place, offsets, zone):
    return call(source_kernel, (512, 128), [place, offsets], [zone], flops=2**26)


def stage_rows(place, modes):
    t = tables()
    constants = [*t["rows"], *t["rows_turn"], *t["x"]]
    return call(rows_kernel, (1024, 128), [place], [modes, *constants], flops=2**30)


def stage_columns(terms, source):
    t = tables()
    constants = [*t["y"], *t["y_turn"], t["gather"], *t["y_back"], t["deal"]]
    return call(columns_kernel, (1024, 128), [], [terms, source, *constants], flops=2**30)


def stage_rows_back(offsets, terms):
    t = tables()
    constants = [*t["x"], *t["back_turn"], *t["back"]]
    scratch = [pltpu.VMEM((512, 128), f32), pltpu.VMEM((64, 128), f32)]
    return call(rows_back_kernel, (8, 16, 256), [offsets], [terms, *constants], scratch, flops=2**29)


def stage_finish(place, terms, eta, phi):
    return call(finish_kernel, [(2, 32, 256)] * 2, [place], [terms, eta, phi])


def local(eta_modes, phi_modes, zone_field, offsets):
    place = jnp.stack([lax.axis_index("wide"), lax.axis_index("narrow")]).astype(jnp.int32)
    swap = functools.partial(lax.all_to_all, split_axis=0, concat_axis=0, tiled=True)
    modes = swap(stage_deal(eta_modes, phi_modes), "narrow")
    source = stage_source(place, offsets, zone_field)
    columns = swap(stage_rows(place, modes), BOTH)
    rows = swap(stage_columns(columns, source), BOTH)
    terms = swap(stage_rows_back(offsets, rows), "narrow")
    return tuple(stage_finish(place, terms, eta_modes, phi_modes))


def solution(mesh):
    in_specs = (P(None, "wide", "narrow"), P(None, "wide", "narrow"), P("wide", None), P())
    out_specs = (P(None, "wide", "narrow"), P(None, "wide", "narrow"))
    return jax.shard_map(local, mesh=mesh, in_specs=in_specs, out_specs=out_specs, check_vma=False)
```

```python
import functools
import math

import jax
import jax.numpy as jnp
import ml_dtypes
import numpy as np
from jax import lax
from jax.experimental import pallas as pl
from jax.experimental.pallas import tpu as pltpu
from jax.sharding import Mesh
from jax.sharding import PartitionSpec as P

NX = 2048
NY = 2048
FINE = 4096
TURN_X = 2.0 * math.pi / NX
TURN_Y = 2.0 * math.pi / NY
time_step = 0.04
gravity = 9.81
spread = 1.0 / math.sqrt(NX * NY)
zone_scale = 1.0 / math.sqrt(4096 * 128)
f32 = jnp.float32
bf16 = jnp.bfloat16
VMEM_LIMIT = 24 * 1024 * 1024


def part(value, which):
    return np.where(which == 0, np.real(value), np.imag(value))


def angles(ints, period):
    return 2.0 * np.pi * (np.asarray(ints) % period) / period


def pair(matrix):
    high = matrix.astype(np.float32).astype(ml_dtypes.bfloat16)
    low = (matrix - high.astype(np.float64)).astype(np.float32).astype(ml_dtypes.bfloat16)
    return high, low


def circle(phase):
    return np.cos(phase).astype(np.float32), np.sin(phase).astype(np.float32)


@functools.cache
def tables():
    out = {}
    k256 = np.arange(256)
    phase = angles(k256[:, None] * k256[None, :], 256)
    out["turn"] = pair(np.concatenate([np.cos(phase), np.sin(phase)], 1))
    row = np.arange(64)
    i, a, jj = row // 16, row // 8 % 2, row % 8
    col = np.arange(128)
    n, ca, cj = col // 16, col // 8 % 2, col % 8
    base = np.exp(1j * angles(i[:, None] * n[None, :], 8)) * (1j ** ca)[None, :]
    same = jj[:, None] == cj[None, :]
    for name, factor in (("slope", 1j), ("lift", 1.0)):
        halves = [np.where(same, part(base * factor * s, a[:, None]), 0.0) for s in (1, 1j)]
        out[name] = pair(np.concatenate(halves, 0))
    x0 = 4 * np.arange(2)[:, None] + np.arange(64)[None, :] // 16
    out["rows_turn"] = circle(angles(x0[:, :, None] * k256, NX))
    lane = np.arange(128)
    out["y_turn"] = circle(angles(k256[:, None] * (lane % 8)[None, :], NY))
    y0 = np.arange(8)
    turn = np.exp(1j * angles((lane % 8)[:, None] * y0[None, :], 8)) * spread
    gather = np.zeros((2, 128, 4, 128))
    gather_lift = np.zeros((128, 128))
    for k in range(128):
        f, i = k // 32, k // 8 % 4
        gather[0, k, f, y0 * 4 + i] = turn[k].real
        gather[1, k, f, y0 * 4 + i] = -turn[k].imag
        if k < 64:
            gather_lift[k, y0 * 4 + i] = turn[k].real if k < 32 else -turn[k].imag
    out["gather"] = pair(gather.reshape(256, 512))
    out["gather_lift"] = pair(gather_lift)
    deal = np.zeros((2, 128, 2, 128))
    for k in range(128):
        f, a, i, jj = k // 64, k // 32 % 2, k // 8 % 4, k % 8
        turn = np.exp(-1j * angles(jj * y0, 8))
        deal[f, y0 * 4 + i, 0, k] = part(turn, a)
        deal[f, y0 * 4 + i, 1, k] = part(-1j * turn, a)
    out["deal"] = pair(deal.reshape(256, 256))
    x0 = 4 * np.arange(2)[:, None] + np.arange(32)[None, :] // 8
    out["main_turn"] = circle(angles(x0[:, :, None] * k256, NX))
    cell = np.arange(128) // 8
    out["zone_turn"] = circle(angles(cell[:, None] * k256, FINE))
    row = np.arange(256)
    n, of, oa, oj = row // 32, row // 16 % 2, row // 8 % 2, row % 8
    col = np.arange(128)
    f, a, i, jj = col // 64, col // 32 % 2, col // 8 % 4, col % 8
    turn = np.exp(-1j * angles(n[:, None] * i[None, :], 8)) * (1j ** a)[None, :]
    same = (of[:, None] == f[None, :]) & (oj[:, None] == jj[None, :])
    halves = [np.where(same, part(turn * s, oa[:, None]), 0.0) for s in (1, -1j)]
    out["main_mix"] = pair(np.concatenate(halves, 1))
    row = np.arange(128)
    n, oa, oj = row // 16, row // 8 % 2, row % 8
    a, p, jj = np.arange(256) // 128, np.arange(256) // 8 % 16, np.arange(256) % 8
    signed = np.where(n < 4, n, n - 8)
    turn = np.exp(-1j * angles(signed[:, None] * p[None, :], 16)) * (1j ** a)[None, :]
    same = oj[:, None] == jj[None, :]
    halves = [np.where(same, part(turn * s, oa[:, None]), 0.0) for s in (1, -1j)]
    out["zone_mix"] = pair(np.concatenate(halves, 1))
    return out


def split(value):
    high = value.astype(bf16)
    return high, (value - high.astype(f32)).astype(bf16)


def dot(left, right, dims=((1,), (0,))):
    return lax.dot_general(left, right, (dims, ((), ())), preferred_element_type=f32)


def dot3(left, right, dims=((1,), (0,))):
    return dot(left[0], right[0], dims) + (dot(left[0], right[1], dims) + dot(left[1], right[0], dims))


def iota(shape, dim):
    return lax.broadcasted_iota(jnp.int32, shape, dim)


def cos_of(phase):
    moved = phase + 512
    quarter = (moved >> 10) & 3
    angle = ((moved & 1023) - 512).astype(f32) * (2.0 * math.pi / FINE)
    square = angle * angle
    cosine = 1.0 + square * (-0.5 + square * (1.0 / 24 + square * (-1.0 / 720 + square * (1.0 / 40320))))
    sine = angle * (
        1.0 + square * (-1.0 / 6 + square * (1.0 / 120 + square * (-1.0 / 5040 + square * (1.0 / 362880))))
    )
    size = jnp.where((quarter & 1) == 0, cosine, sine)
    return jnp.where((quarter == 1) | (quarter == 2), -size, size)


def wave_of(index):
    return jnp.where(index < 1024, index, index - 2048).astype(f32)


def deal_kernel(eta, phi, out):
    for z in range(4):
        for source, base in ((eta, 0), (phi, 16)):
            for a in range(2):
                rows = source[a, 8 * z : 8 * z + 8, :]
                for c in range(2):
                    out[2 * z + c, base + 8 * a : base + 8 * a + 8, :] = rows


def source_kernel(place, offsets, zone, out):
    tile = place[0]
    own = 4 * place[2] + place[1]
    ox = offsets[tile, 0]
    oy = offsets[tile, 1]
    lane = iota((128, 128), 1)
    wanted = (16 * own + (lane >> 3) - 2 * (ox & 7)) & 127
    pick = jnp.where(iota((128, 128), 0) == wanted, 1.0, 0.0).astype(bf16)
    high, low = split(zone[...] * zone_scale)
    cells = dot(high, pick) + dot(low, pick)
    phase = (iota((64, 128), 1) & 7) * (2 * oy + iota((64, 128), 0))
    real = cells * cos_of(phase)
    imag = cells * cos_of(phase + 1024)
    right = jnp.concatenate(
        [jnp.concatenate([real, imag], 1), jnp.concatenate([-imag, real], 1)], 0
    )
    lane = iota((256, 128), 1)
    g = iota((256, 128), 0)
    g = jnp.where(g < 128, g, g - 256)
    left = cos_of(8 * g * (2 * oy + (lane & 63)) + jnp.where(lane < 64, 0, 1024))
    out[...] = dot3(split(left), split(right))


def rows_kernel(
    place, modes, slope_high, slope_low, lift_high, lift_low, cos_turn, sin_turn, high, low, out
):
    first_ky = 32 * place[0] + 8 * place[1]
    core = place[2]
    odd = 1.0 - 2.0 * core.astype(f32)
    wave_y = wave_of(first_ky + (iota((16, 256), 0) & 7)) * TURN_Y
    tiles = [[], [], [], [], []]
    for n in range(8):
        wave_x = wave_of(256 * n + iota((16, 256), 1)) * TURN_X
        kappa = jnp.sqrt(wave_x * wave_x + wave_y * wave_y)
        eta = modes[n, 0:16, :]
        phi = modes[n, 16:32, :]
        if n % 2:
            eta = eta * odd
            phi = phi * odd
        terms = (wave_x * eta, wave_y * eta, wave_x * phi, wave_y * phi, kappa * phi)
        for f in range(5):
            tiles[f].append(terms[f])
    cosine = cos_turn[core]
    sine = sin_turn[core]
    slope_mix = (slope_high[...], slope_low[...])
    lift_mix = (lift_high[...], lift_low[...])
    parts = [[], []]
    for f in range(5):
        rows = split(jnp.concatenate(tiles[f], 0))
        both = dot3(slope_mix if f < 4 else lift_mix, rows)
        first = both[:64]
        second = both[64:]
        turned = (first * cosine + second * sine).reshape(4, 2, 8, 256)
        quarter = (second * cosine - first * sine).reshape(4, 2, 8, 256)
        for a in range(2):
            parts[a].append(
                jnp.concatenate(
                    [turned[:, a].reshape(32, 256), quarter[:, a].reshape(32, 256)], 1
                )
            )
    real, imag = parts
    words = real[:4] + imag[:4] + [real[4], imag[4], -imag[4], real[4]]
    result = dot3((high[...], low[...]), split(jnp.concatenate(words, 0)), ((1,), (1,)))
    for q in range(3):
        out[pl.ds(q, 256, stride=4), :] = result[:, 128 * q : 128 * q + 128]
    out[pl.ds(3, 256, stride=4), :] = jnp.zeros((256, 128), f32)


def columns_kernel(
    terms,
    source,
    high,
    low,
    cos_turn,
    sin_turn,
    gather_high,
    gather_low,
    gather_lift_high,
    gather_lift_low,
    deal_high,
    deal_low,
    out,
):
    words = split(
        jnp.concatenate([terms[pl.ds(q, 256, stride=4), :] for q in range(3)], 1)
    )
    with_cos = dot3((high[:, :256], low[:, :256]), words)
    with_sin = dot3((high[:, 256:], low[:, 256:]), words)
    real = with_cos[:, :128] - with_sin[:, 128:256]
    imag = with_sin[:, :128] + with_cos[:, 128:256]
    lane = iota((256, 128), 1)
    rolled = pltpu.roll(with_sin[:, 256:], 64, 1)
    lift = with_cos[:, 256:] + jnp.where(lane < 64, rolled, -rolled)
    cosine = cos_turn[...]
    sine = sin_turn[...]
    slopes = split(
        jnp.concatenate([real * cosine - imag * sine, real * sine + imag * cosine], 1)
    )
    lift = split(lift * cosine + pltpu.roll(lift, 64, 1) * sine)
    fields = dot3(slopes, (gather_high[...], gather_low[...]))
    lift = dot3(lift, (gather_lift_high[...], gather_lift_low[...]))
    slope_ex, slope_ey, slope_px, slope_py = (
        fields[:, 128 * k : 128 * k + 128] for k in range(4)
    )
    first_order = lift * (slope_ex * slope_ex + slope_ey * slope_ey) - (
        slope_px * slope_ex + slope_py * slope_ey
    )
    second_term = 0.5 * (lift * lift - slope_px * slope_px - slope_py * slope_py)
    products = jnp.concatenate([first_order, second_term], 1) * (time_step * spread)
    both = dot3(split(products), (deal_high[...], deal_low[...]))
    first = both[:, :128]
    second = both[:, 128:]
    turned = jnp.concatenate([first * cosine + second * sine, second * cosine - first * sine], 0)
    out[pl.ds(0, 256, stride=4), :] = dot3((high[...], low[...]), split(turned))
    out[pl.ds(1, 256, stride=4), :] = source[:, :128]
    out[pl.ds(2, 256, stride=4), :] = source[:, 128:]
    out[pl.ds(3, 256, stride=4), :] = jnp.zeros((256, 128), f32)


def rows_back_kernel(
    place,
    offsets,
    terms,
    high,
    low,
    cos_main,
    sin_main,
    cos_zone,
    sin_zone,
    main_high,
    main_low,
    zone_high,
    zone_low,
    out,
    ends,
):
    core = place[2]
    depth = iota((8, 256), 0)
    spot = iota((8, 256), 1)
    lane = iota((8, 128), 1)
    row = iota((8, 128), 0)
    cells = [[], []]
    places = []
    last_places = []
    bases = []
    for t in range(0, 64, 2):
        ox = offsets[t, 0], offsets[t + 1, 0]
        base = ox[0] >> 3, ox[1] >> 3
        bases += base
        edge = jnp.where(row < 4, 8 * (2 * (ox[0] & 7)), 8 * (2 * (ox[1] & 7)))
        edge = jnp.where(((row & 3) == 0) & (core == 0), edge, 0)
        beyond = lane < edge
        for a in range(2):
            tile = terms[pl.ds(16 * t + 1 + a, 8, stride=4), :]
            cells[a].append(jnp.where(beyond, 0.0, tile))
            moved = jnp.where(beyond, tile, 0.0)
            ends[t : t + 1, 128 * a : 128 * a + 128] = moved[0:1, :]
            ends[t + 1 : t + 2, 128 * a : 128 * a + 128] = moved[4:5, :]
        target = jnp.where(depth < 4, base[0], base[1]) + (depth & 3) + 4 * core
        places.append(jnp.where(spot == (target & 255), 1.0, 0.0))
    for t in range(0, 64, 8):
        target = jnp.zeros((8, 256), jnp.int32)
        for k in range(8):
            target = jnp.where(depth == k, bases[t + k], target)
        last_places.append(jnp.where(spot == ((target + 8) & 255), 1.0, 0.0))
    where_to = jnp.concatenate(places, 0).astype(bf16)
    last_to = jnp.concatenate(last_places, 0).astype(bf16)
    cells = jnp.concatenate([jnp.concatenate(half, 0) for half in cells], 1)
    near = split(cells.T)
    far = split(ends[...].T)
    grid = (dot(near[0], where_to) + dot(near[1], where_to)) + (
        dot(far[0], last_to) + dot(far[1], last_to)
    )
    main = terms[pl.ds(0, 256, stride=4), :].T
    both = dot3(split(jnp.concatenate([main, grid], 0)), (high[...], low[...]))

    def turned(lines, cosine, sine):
        with_cos = lines[:, :, :256]
        with_sin = lines[:, :, 256:]
        real = with_cos * cosine - with_sin * sine
        imag = with_cos * sine + with_sin * cosine
        count = lines.shape[0] * lines.shape[1]
        return split(
            jnp.concatenate([real.reshape(count, 256), imag.reshape(count, 256)], 0)
        )

    main = turned(both[:128].reshape(4, 32, 512), cos_main[core][None], sin_main[core][None])
    zone = turned(both[128:].reshape(2, 128, 512), cos_zone[...][None], sin_zone[...][None])
    main = dot3((main_high[...], main_low[...]), main)
    zone = dot3((zone_high[...], zone_low[...]), zone)
    odd = 1.0 - 2.0 * core.astype(f32)
    for n in range(8):
        block = main[32 * n : 32 * n + 32]
        if n % 2:
            block = block * odd
        out[n, 0:16, :] = block[:16] + zone[16 * n : 16 * n + 16]
        out[n, 16:32, :] = block[16:]


def finish_kernel(place, terms, eta, phi, eta_next, phi_next):
    for z in range(4):
        rows = slice(8 * z, 8 * z + 8)
        wave_x = wave_of(256 * (2 * place[1] + place[2]) + iota((8, 256), 1)) * TURN_X
        wave_y = wave_of(32 * place[0] + 8 * z + iota((8, 256), 0)) * TURN_Y
        kappa = time_step * jnp.sqrt(wave_x * wave_x + wave_y * wave_y)
        for a in range(2):
            surface = eta[a, rows, :]
            potential = phi[a, rows, :]
            part_of = slice(8 * a, 8 * a + 8)
            added = terms[2 * z, part_of, :] + terms[2 * z + 1, part_of, :]
            eta_next[a, rows, :] = surface + kappa * potential + added
            part_of = slice(16 + 8 * a, 24 + 8 * a)
            added = terms[2 * z, part_of, :] + terms[2 * z + 1, part_of, :]
            phi_next[a, rows, :] = potential - (time_step * gravity) * surface + added


def call(kernel, shapes, scalars, arrays, scratch=(), flops=0):
    single = isinstance(shapes, tuple)
    shapes = [shapes] if single else shapes
    vmem = pl.BlockSpec(memory_space=pltpu.VMEM)
    smem = pl.BlockSpec(memory_space=pltpu.SMEM)
    moved = sum(4 * math.prod(s) for s in shapes) + sum(x.size * x.dtype.itemsize for x in arrays)
    result = pl.pallas_call(
        kernel,
        out_shape=[jax.ShapeDtypeStruct(s, f32) for s in shapes],
        in_specs=[smem] * len(scalars) + [vmem] * len(arrays),
        out_specs=[vmem] * len(shapes),
        scratch_shapes=list(scratch),
        compiler_params=pltpu.CompilerParams(vmem_limit_bytes=VMEM_LIMIT),
        cost_estimate=pl.CostEstimate(flops=flops, bytes_accessed=moved, transcendentals=0),
        name=kernel.__name__,
    )(*scalars, *arrays)
    return result[0] if single else result


def stage_deal(eta, phi):
    return call(deal_kernel, (8, 32, 256), [], [eta, phi])


def stage_source(place, offsets, zone):
    return call(source_kernel, (256, 256), [place, offsets], [zone], flops=2**26)


def stage_rows(place, modes):
    t = tables()
    constants = [*t["slope"], *t["lift"], *t["rows_turn"], *t["turn"]]
    return call(rows_kernel, (1024, 128), [place], [modes, *constants], flops=2**30)


def stage_columns(terms, source):
    t = tables()
    constants = [*t["turn"], *t["y_turn"], *t["gather"], *t["gather_lift"], *t["deal"]]
    return call(columns_kernel, (1024, 128), [], [terms, source, *constants], flops=2**30)


def stage_rows_back(place, offsets, terms):
    t = tables()
    constants = [*t["turn"], *t["main_turn"], *t["zone_turn"], *t["main_mix"], *t["zone_mix"]]
    scratch = [pltpu.VMEM((64, 256), f32)]
    arrays = [terms, *constants]
    return call(rows_back_kernel, (8, 32, 256), [place, offsets], arrays, scratch, flops=2**29)


def stage_finish(place, terms, eta, phi):
    return call(finish_kernel, [(2, 32, 256)] * 2, [place], [terms, eta, phi])


def local(eta_modes, phi_modes, zone_field, offsets):
    place = jnp.stack([lax.axis_index(axis) for axis in ("wide", "lane", "core")]).astype(jnp.int32)
    swap = functools.partial(lax.all_to_all, split_axis=0, concat_axis=0, tiled=True)
    modes = swap(stage_deal(eta_modes, phi_modes), ("lane", "core"))
    source = stage_source(place, offsets, zone_field)
    columns = swap(stage_rows(place, modes), ("wide", "lane"))
    rows = swap(stage_columns(columns, source), ("wide", "lane"))
    terms = swap(stage_rows_back(place, offsets, rows), ("lane", "core"))
    return tuple(stage_finish(place, terms, eta_modes, phi_modes))


def solution(mesh):
    wide, narrow = mesh.devices.shape
    chips = Mesh(mesh.devices.reshape(wide, narrow // 2, 2), ("wide", "lane", "core"))
    modes = P(None, "wide", ("lane", "core"))
    in_specs = (modes, modes, P("wide", None), P())
    return jax.shard_map(
        local, mesh=chips, in_specs=in_specs, out_specs=(modes, modes), check_vma=False
    )
```

```python
import functools
import math

import jax
import jax.numpy as jnp
import ml_dtypes
import numpy as np
from jax import lax
from jax.experimental import pallas as pl
from jax.experimental.pallas import tpu as pltpu
from jax.sharding import Mesh
from jax.sharding import PartitionSpec as P

NX = 2048
NY = 2048
FINE = 4096
TURN_X = 2.0 * math.pi / NX
TURN_Y = 2.0 * math.pi / NY
time_step = 0.04
gravity = 9.81
spread = 1.0 / math.sqrt(NX * NY)
zone_scale = 1.0 / math.sqrt(4096 * 128)
f32 = jnp.float32
bf16 = jnp.bfloat16
VMEM_LIMIT = 24 * 1024 * 1024


def part(value, which):
    return np.where(which == 0, np.real(value), np.imag(value))


def angles(ints, period):
    return 2.0 * np.pi * (np.asarray(ints) % period) / period


def pair(matrix):
    high = matrix.astype(np.float32).astype(ml_dtypes.bfloat16)
    low = (matrix - high.astype(np.float64)).astype(np.float32).astype(ml_dtypes.bfloat16)
    return high, low


def circle(phase):
    return np.cos(phase).astype(np.float32), np.sin(phase).astype(np.float32)


@functools.cache
def tables():
    out = {}
    k256 = np.arange(256)
    phase = angles(k256[:, None] * k256[None, :], 256)
    out["turn"] = pair(np.concatenate([np.cos(phase), np.sin(phase)], 1))
    row = np.arange(64)
    i, a, jj = row // 16, row // 8 % 2, row % 8
    col = np.arange(128)
    n, ca, cj = col // 16, col // 8 % 2, col % 8
    base = np.exp(1j * angles(i[:, None] * n[None, :], 8)) * (1j ** ca)[None, :]
    same = jj[:, None] == cj[None, :]
    for name, factor in (("slope", 1j), ("lift", 1.0)):
        halves = [np.where(same, part(base * factor * s, a[:, None]), 0.0) for s in (1, 1j)]
        out[name] = pair(np.concatenate(halves, 0))
    x0 = 4 * np.arange(2)[:, None] + np.arange(64)[None, :] // 16
    out["rows_turn"] = circle(angles(x0[:, :, None] * k256, NX))
    lane = np.arange(128)
    out["y_turn"] = circle(angles(k256[:, None] * (lane % 8)[None, :], NY))
    y0 = np.arange(8)
    turn = np.exp(1j * angles((lane % 8)[:, None] * y0[None, :], 8)) * spread
    gather = np.zeros((2, 128, 4, 128))
    gather_lift = np.zeros((128, 128))
    for k in range(128):
        f, i = k // 32, k // 8 % 4
        gather[0, k, f, y0 * 4 + i] = turn[k].real
        gather[1, k, f, y0 * 4 + i] = -turn[k].imag
        if k < 64:
            gather_lift[k, y0 * 4 + i] = turn[k].real if k < 32 else -turn[k].imag
    out["gather"] = pair(gather.reshape(256, 512))
    out["gather_lift"] = pair(gather_lift)
    deal = np.zeros((2, 128, 2, 128))
    for k in range(128):
        f, a, i, jj = k // 64, k // 32 % 2, k // 8 % 4, k % 8
        turn = np.exp(-1j * angles(jj * y0, 8))
        deal[f, y0 * 4 + i, 0, k] = part(turn, a)
        deal[f, y0 * 4 + i, 1, k] = part(-1j * turn, a)
    out["deal"] = pair(deal.reshape(256, 256))
    x0 = 4 * np.arange(2)[:, None] + np.arange(32)[None, :] // 8
    out["main_turn"] = circle(angles(x0[:, :, None] * k256, NX))
    cell = np.arange(128) // 8
    out["zone_turn"] = circle(angles(cell[:, None] * k256, FINE))
    row = np.arange(256)
    n, of, oa, oj = row // 32, row // 16 % 2, row // 8 % 2, row % 8
    col = np.arange(128)
    f, a, i, jj = col // 64, col // 32 % 2, col // 8 % 4, col % 8
    turn = np.exp(-1j * angles(n[:, None] * i[None, :], 8)) * (1j ** a)[None, :]
    same = (of[:, None] == f[None, :]) & (oj[:, None] == jj[None, :])
    halves = [np.where(same, part(turn * s, oa[:, None]), 0.0) for s in (1, -1j)]
    out["main_mix"] = pair(np.concatenate(halves, 1))
    row = np.arange(128)
    n, oa, oj = row // 16, row // 8 % 2, row % 8
    a, p, jj = np.arange(256) // 128, np.arange(256) // 8 % 16, np.arange(256) % 8
    signed = np.where(n < 4, n, n - 8)
    turn = np.exp(-1j * angles(signed[:, None] * p[None, :], 16)) * (1j ** a)[None, :]
    same = oj[:, None] == jj[None, :]
    halves = [np.where(same, part(turn * s, oa[:, None]), 0.0) for s in (1, -1j)]
    out["zone_mix"] = pair(np.concatenate(halves, 1))
    return out


def split(value):
    high = value.astype(bf16)
    return high, (value - high.astype(f32)).astype(bf16)


def dot(left, right, dims=((1,), (0,))):
    return lax.dot_general(left, right, (dims, ((), ())), preferred_element_type=f32)


def dot3(left, right, dims=((1,), (0,))):
    return dot(left[0], right[0], dims) + (dot(left[0], right[1], dims) + dot(left[1], right[0], dims))


def iota(shape, dim):
    return lax.broadcasted_iota(jnp.int32, shape, dim)


def cos_of(phase):
    moved = phase + 512
    quarter = (moved >> 10) & 3
    angle = ((moved & 1023) - 512).astype(f32) * (2.0 * math.pi / FINE)
    square = angle * angle
    cosine = 1.0 + square * (-0.5 + square * (1.0 / 24 + square * (-1.0 / 720 + square * (1.0 / 40320))))
    sine = angle * (
        1.0 + square * (-1.0 / 6 + square * (1.0 / 120 + square * (-1.0 / 5040 + square * (1.0 / 362880))))
    )
    size = jnp.where((quarter & 1) == 0, cosine, sine)
    return jnp.where((quarter == 1) | (quarter == 2), -size, size)


def wave_of(index):
    return jnp.where(index < 1024, index, index - 2048).astype(f32)


def deal_kernel(eta, phi, out, done):
    copies = []
    for z in range(4):
        for k, source in enumerate((eta, phi)):
            for c in range(2):
                copies.append(
                    pltpu.make_async_copy(
                        source.at[:, 8 * z : 8 * z + 8, :], out.at[2 * z + c, k], done.at[len(copies)]
                    )
                )
    for copy in copies:
        copy.start()
    for copy in copies:
        copy.wait()


def source_kernel(place, offsets, zone, out):
    tile = place[0]
    own = 4 * place[2] + place[1]
    ox = offsets[tile, 0]
    oy = offsets[tile, 1]
    lane = iota((128, 128), 1)
    wanted = (16 * own + (lane >> 3) - 2 * (ox & 7)) & 127
    pick = jnp.where(iota((128, 128), 0) == wanted, 1.0, 0.0).astype(bf16)
    high, low = split(zone[...] * zone_scale)
    cells = dot(high, pick) + dot(low, pick)
    phase = (iota((64, 128), 1) & 7) * (2 * oy + iota((64, 128), 0))
    real = cells * cos_of(phase)
    imag = cells * cos_of(phase + 1024)
    right = jnp.concatenate(
        [jnp.concatenate([real, imag], 1), jnp.concatenate([-imag, real], 1)], 0
    )
    lane = iota((256, 128), 1)
    g = iota((256, 128), 0)
    g = jnp.where(g < 128, g, g - 256)
    left = cos_of(8 * g * (2 * oy + (lane & 63)) + jnp.where(lane < 64, 0, 1024))
    out[...] = dot3(split(left), split(right))


def rows_kernel(
    place, modes, slope_high, slope_low, lift_high, lift_low, cos_turn, sin_turn, high, low, out
):
    first_ky = 32 * place[0] + 8 * place[1]
    core = place[2]
    odd = 1.0 - 2.0 * core.astype(f32)
    wave_y = wave_of(first_ky + (iota((16, 256), 0) & 7)) * TURN_Y
    tiles = [[], [], [], [], []]
    for n in range(8):
        wave_x = wave_of(256 * n + iota((16, 256), 1)) * TURN_X
        kappa = jnp.sqrt(wave_x * wave_x + wave_y * wave_y)
        eta = modes[n, 0:16, :]
        phi = modes[n, 16:32, :]
        if n % 2:
            eta = eta * odd
            phi = phi * odd
        terms = (wave_x * eta, wave_y * eta, wave_x * phi, wave_y * phi, kappa * phi)
        for f in range(5):
            tiles[f].append(terms[f])
    cosine = cos_turn[core]
    sine = sin_turn[core]
    slope_mix = (slope_high[...], slope_low[...])
    lift_mix = (lift_high[...], lift_low[...])
    parts = [[], []]
    for f in range(5):
        rows = split(jnp.concatenate(tiles[f], 0))
        both = dot3(slope_mix if f < 4 else lift_mix, rows)
        first = both[:64]
        second = both[64:]
        turned = (first * cosine + second * sine).reshape(4, 2, 8, 256)
        quarter = (second * cosine - first * sine).reshape(4, 2, 8, 256)
        for a in range(2):
            parts[a].append(
                jnp.concatenate(
                    [turned[:, a].reshape(32, 256), quarter[:, a].reshape(32, 256)], 1
                )
            )
    real, imag = parts
    words = real[:4] + imag[:4] + [real[4], imag[4], -imag[4], real[4]]
    result = dot3((high[...], low[...]), split(jnp.concatenate(words, 0)), ((1,), (1,)))
    for q in range(3):
        out[pl.ds(q, 256, stride=3), :] = result[:, 128 * q : 128 * q + 128]


def columns_kernel(
    terms,
    source,
    high,
    low,
    cos_turn,
    sin_turn,
    gather_high,
    gather_low,
    gather_lift_high,
    gather_lift_low,
    deal_high,
    deal_low,
    out,
):
    words = split(
        jnp.concatenate([terms[pl.ds(q, 256, stride=3), :] for q in range(3)], 1)
    )
    with_cos = dot3((high[:, :256], low[:, :256]), words)
    with_sin = dot3((high[:, 256:], low[:, 256:]), words)
    real = with_cos[:, :128] - with_sin[:, 128:256]
    imag = with_sin[:, :128] + with_cos[:, 128:256]
    lane = iota((256, 128), 1)
    rolled = pltpu.roll(with_sin[:, 256:], 64, 1)
    lift = with_cos[:, 256:] + jnp.where(lane < 64, rolled, -rolled)
    cosine = cos_turn[...]
    sine = sin_turn[...]
    slopes = split(
        jnp.concatenate([real * cosine - imag * sine, real * sine + imag * cosine], 1)
    )
    lift = split(lift * cosine + pltpu.roll(lift, 64, 1) * sine)
    fields = dot3(slopes, (gather_high[...], gather_low[...]))
    lift = dot3(lift, (gather_lift_high[...], gather_lift_low[...]))
    slope_ex, slope_ey, slope_px, slope_py = (
        fields[:, 128 * k : 128 * k + 128] for k in range(4)
    )
    first_order = lift * (slope_ex * slope_ex + slope_ey * slope_ey) - (
        slope_px * slope_ex + slope_py * slope_ey
    )
    second_term = 0.5 * (lift * lift - slope_px * slope_px - slope_py * slope_py)
    products = jnp.concatenate([first_order, second_term], 1) * (time_step * spread)
    both = dot3(split(products), (deal_high[...], deal_low[...]))
    first = both[:, :128]
    second = both[:, 128:]
    turned = jnp.concatenate([first * cosine + second * sine, second * cosine - first * sine], 0)
    out[pl.ds(0, 256, stride=3), :] = dot3((high[...], low[...]), split(turned))
    out[pl.ds(1, 256, stride=3), :] = source[:, :128]
    out[pl.ds(2, 256, stride=3), :] = source[:, 128:]


def rows_back_kernel(
    place,
    offsets,
    terms,
    high,
    low,
    cos_main,
    sin_main,
    cos_zone,
    sin_zone,
    main_high,
    main_low,
    zone_high,
    zone_low,
    out,
    ends,
):
    core = place[2]
    depth = iota((8, 256), 0)
    spot = iota((8, 256), 1)
    lane = iota((8, 128), 1)
    row = iota((8, 128), 0)
    cells = [[], []]
    places = []
    last_places = []
    bases = []
    for t in range(0, 64, 2):
        ox = offsets[t, 0], offsets[t + 1, 0]
        base = ox[0] >> 3, ox[1] >> 3
        bases += base
        edge = jnp.where(row < 4, 8 * (2 * (ox[0] & 7)), 8 * (2 * (ox[1] & 7)))
        edge = jnp.where(((row & 3) == 0) & (core == 0), edge, 0)
        beyond = lane < edge
        for a in range(2):
            tile = terms[pl.ds(12 * t + 1 + a, 8, stride=3), :]
            cells[a].append(jnp.where(beyond, 0.0, tile))
            moved = jnp.where(beyond, tile, 0.0)
            ends[t : t + 1, 128 * a : 128 * a + 128] = moved[0:1, :]
            ends[t + 1 : t + 2, 128 * a : 128 * a + 128] = moved[4:5, :]
        target = jnp.where(depth < 4, base[0], base[1]) + (depth & 3) + 4 * core
        places.append(jnp.where(spot == (target & 255), 1.0, 0.0))
    for t in range(0, 64, 8):
        target = jnp.zeros((8, 256), jnp.int32)
        for k in range(8):
            target = jnp.where(depth == k, bases[t + k], target)
        last_places.append(jnp.where(spot == ((target + 8) & 255), 1.0, 0.0))
    where_to = jnp.concatenate(places, 0).astype(bf16)
    last_to = jnp.concatenate(last_places, 0).astype(bf16)
    cells = jnp.concatenate([jnp.concatenate(half, 0) for half in cells], 1)
    near = split(cells.T)
    far = split(ends[...].T)
    grid = (dot(near[0], where_to) + dot(near[1], where_to)) + (
        dot(far[0], last_to) + dot(far[1], last_to)
    )
    main = terms[pl.ds(0, 256, stride=3), :].T
    both = dot3(split(jnp.concatenate([main, grid], 0)), (high[...], low[...]))

    def turned(lines, cosine, sine):
        with_cos = lines[:, :, :256]
        with_sin = lines[:, :, 256:]
        real = with_cos * cosine - with_sin * sine
        imag = with_cos * sine + with_sin * cosine
        count = lines.shape[0] * lines.shape[1]
        return split(
            jnp.concatenate([real.reshape(count, 256), imag.reshape(count, 256)], 0)
        )

    main = turned(both[:128].reshape(4, 32, 512), cos_main[core][None], sin_main[core][None])
    zone = turned(both[128:].reshape(2, 128, 512), cos_zone[...][None], sin_zone[...][None])
    main = dot3((main_high[...], main_low[...]), main)
    zone = dot3((zone_high[...], zone_low[...]), zone)
    odd = 1.0 - 2.0 * core.astype(f32)
    for n in range(8):
        block = main[32 * n : 32 * n + 32]
        if n % 2:
            block = block * odd
        out[n, 0:16, :] = block[:16] + zone[16 * n : 16 * n + 16]
        out[n, 16:32, :] = block[16:]


def finish_kernel(place, terms, eta, phi, eta_next, phi_next):
    for z in range(4):
        rows = slice(8 * z, 8 * z + 8)
        wave_x = wave_of(256 * (2 * place[1] + place[2]) + iota((8, 256), 1)) * TURN_X
        wave_y = wave_of(32 * place[0] + 8 * z + iota((8, 256), 0)) * TURN_Y
        kappa = time_step * jnp.sqrt(wave_x * wave_x + wave_y * wave_y)
        for a in range(2):
            surface = eta[a, rows, :]
            potential = phi[a, rows, :]
            part_of = slice(8 * a, 8 * a + 8)
            added = terms[2 * z, part_of, :] + terms[2 * z + 1, part_of, :]
            eta_next[a, rows, :] = surface + kappa * potential + added
            part_of = slice(16 + 8 * a, 24 + 8 * a)
            added = terms[2 * z, part_of, :] + terms[2 * z + 1, part_of, :]
            phi_next[a, rows, :] = potential - (time_step * gravity) * surface + added


def call(kernel, shapes, scalars, arrays, scratch=(), flops=0):
    single = isinstance(shapes, tuple)
    shapes = [shapes] if single else shapes
    vmem = pl.BlockSpec(memory_space=pltpu.VMEM)
    smem = pl.BlockSpec(memory_space=pltpu.SMEM)
    moved = sum(4 * math.prod(s) for s in shapes) + sum(x.size * x.dtype.itemsize for x in arrays)
    result = pl.pallas_call(
        kernel,
        out_shape=[jax.ShapeDtypeStruct(s, f32) for s in shapes],
        in_specs=[smem] * len(scalars) + [vmem] * len(arrays),
        out_specs=[vmem] * len(shapes),
        scratch_shapes=list(scratch),
        compiler_params=pltpu.CompilerParams(vmem_limit_bytes=VMEM_LIMIT),
        cost_estimate=pl.CostEstimate(flops=flops, bytes_accessed=moved, transcendentals=0),
        name=kernel.__name__,
    )(*scalars, *arrays)
    return result[0] if single else result


def stage_deal(eta, phi):
    anywhere = pl.BlockSpec(memory_space=pl.ANY)
    dealt = pl.pallas_call(
        deal_kernel,
        out_shape=jax.ShapeDtypeStruct((8, 2, 2, 8, 256), f32),
        in_specs=[anywhere, anywhere],
        out_specs=anywhere,
        scratch_shapes=[pltpu.SemaphoreType.DMA((16,))],
        compiler_params=pltpu.CompilerParams(vmem_limit_bytes=56 * 1024 * 1024),
        cost_estimate=pl.CostEstimate(flops=0, bytes_accessed=3 * 2**17, transcendentals=0),
        name="deal_kernel",
    )(eta, phi)
    return dealt.reshape(8, 32, 256)


def stage_source(place, offsets, zone):
    return call(source_kernel, (256, 256), [place, offsets], [zone], flops=2**26)


def stage_rows(place, modes):
    t = tables()
    constants = [*t["slope"], *t["lift"], *t["rows_turn"], *t["turn"]]
    return call(rows_kernel, (768, 128), [place], [modes, *constants], flops=2**30)


def stage_columns(terms, source):
    t = tables()
    constants = [*t["turn"], *t["y_turn"], *t["gather"], *t["gather_lift"], *t["deal"]]
    return call(columns_kernel, (768, 128), [], [terms, source, *constants], flops=2**30)


def stage_rows_back(place, offsets, terms):
    t = tables()
    constants = [*t["turn"], *t["main_turn"], *t["zone_turn"], *t["main_mix"], *t["zone_mix"]]
    scratch = [pltpu.VMEM((64, 256), f32)]
    arrays = [terms, *constants]
    return call(rows_back_kernel, (8, 32, 256), [place, offsets], arrays, scratch, flops=2**29)


def stage_finish(place, terms, eta, phi):
    return call(finish_kernel, [(2, 32, 256)] * 2, [place], [terms, eta, phi])


def local(eta_modes, phi_modes, zone_field, offsets):
    place = jnp.stack([lax.axis_index(axis) for axis in ("wide", "lane", "core")]).astype(jnp.int32)
    swap = functools.partial(lax.all_to_all, split_axis=0, concat_axis=0, tiled=True)

    def turn(words):
        return swap(words.reshape(256, 1, 384), ("wide", "lane")).reshape(768, 128)

    modes = swap(stage_deal(eta_modes, phi_modes), ("lane", "core"))
    source = stage_source(place, offsets, zone_field)
    columns = turn(stage_rows(place, modes))
    rows = turn(stage_columns(columns, source))
    terms = swap(stage_rows_back(place, offsets, rows), ("lane", "core"))
    return tuple(stage_finish(place, terms, eta_modes, phi_modes))


def solution(mesh):
    wide, narrow = mesh.devices.shape
    chips = Mesh(mesh.devices.reshape(wide, narrow // 2, 2), ("wide", "lane", "core"))
    modes = P(None, "wide", ("lane", "core"))
    in_specs = (modes, modes, P("wide", None), P())
    return jax.shard_map(
        local, mesh=chips, in_specs=in_specs, out_specs=(modes, modes), check_vma=False
    )
```

```python
import functools
import math

import jax
import jax.numpy as jnp
import ml_dtypes
import numpy as np
from jax import lax
from jax.experimental import pallas as pl
from jax.experimental.pallas import tpu as pltpu
from jax.sharding import Mesh
from jax.sharding import PartitionSpec as P

NX = 2048
NY = 2048
FINE = 4096
TURN_X = 2.0 * math.pi / NX
TURN_Y = 2.0 * math.pi / NY
time_step = 0.04
gravity = 9.81
spread = 1.0 / math.sqrt(NX * NY)
zone_scale = 1.0 / math.sqrt(4096 * 128)
f32 = jnp.float32
bf16 = jnp.bfloat16


def part(value, which):
    return np.where(which == 0, np.real(value), np.imag(value))


def angles(ints, period):
    return 2.0 * np.pi * (np.asarray(ints) % period) / period


def pair(matrix):
    high = matrix.astype(np.float32).astype(ml_dtypes.bfloat16)
    low = (matrix - high.astype(np.float64)).astype(np.float32).astype(ml_dtypes.bfloat16)
    return high, low


def circle(phase):
    return np.cos(phase).astype(np.float32), np.sin(phase).astype(np.float32)


@functools.cache
def tables():
    out = {}
    k256 = np.arange(256)
    phase = angles(k256[:, None] * k256[None, :], 256)
    out["turn"] = pair(np.concatenate([np.cos(phase), np.sin(phase)], 1))
    row = np.arange(64)
    i, a, jj = row // 16, row // 8 % 2, row % 8
    col = np.arange(128)
    n, ca, cj = col // 16, col // 8 % 2, col % 8
    base = np.exp(1j * angles(i[:, None] * n[None, :], 8)) * (1j ** ca)[None, :]
    same = jj[:, None] == cj[None, :]
    for name, factor in (("slope", 1j), ("lift", 1.0)):
        halves = [np.where(same, part(base * factor * s, a[:, None]), 0.0) for s in (1, 1j)]
        out[name] = pair(np.concatenate(halves, 0))
    x0 = 4 * np.arange(2)[:, None] + np.arange(64)[None, :] // 16
    out["rows_turn"] = circle(angles(x0[:, :, None] * k256, NX))
    lane = np.arange(128)
    out["y_turn"] = circle(angles(k256[:, None] * (lane % 8)[None, :], NY))
    y0 = np.arange(8)
    turn = np.exp(1j * angles((lane % 8)[:, None] * y0[None, :], 8)) * spread
    gather = np.zeros((2, 128, 4, 128))
    gather_lift = np.zeros((128, 128))
    for k in range(128):
        f, i = k // 32, k // 8 % 4
        gather[0, k, f, y0 * 4 + i] = turn[k].real
        gather[1, k, f, y0 * 4 + i] = -turn[k].imag
        if k < 64:
            gather_lift[k, y0 * 4 + i] = turn[k].real if k < 32 else -turn[k].imag
    out["gather"] = pair(gather.reshape(256, 512))
    out["gather_lift"] = pair(gather_lift)
    deal = np.zeros((2, 128, 2, 128))
    for k in range(128):
        f, a, i, jj = k // 64, k // 32 % 2, k // 8 % 4, k % 8
        turn = np.exp(-1j * angles(jj * y0, 8))
        deal[f, y0 * 4 + i, 0, k] = part(turn, a)
        deal[f, y0 * 4 + i, 1, k] = part(-1j * turn, a)
    out["deal"] = pair(deal.reshape(256, 256))
    x0 = 4 * np.arange(2)[:, None] + np.arange(32)[None, :] // 8
    out["main_turn"] = circle(angles(x0[:, :, None] * k256, NX))
    cell = np.arange(128) // 8
    out["zone_turn"] = circle(angles(cell[:, None] * k256, FINE))
    row = np.arange(256)
    n, of, oa, oj = row // 32, row // 16 % 2, row // 8 % 2, row % 8
    col = np.arange(128)
    f, a, i, jj = col // 64, col // 32 % 2, col // 8 % 4, col % 8
    turn = np.exp(-1j * angles(n[:, None] * i[None, :], 8)) * (1j ** a)[None, :]
    same = (of[:, None] == f[None, :]) & (oj[:, None] == jj[None, :])
    halves = [np.where(same, part(turn * s, oa[:, None]), 0.0) for s in (1, -1j)]
    out["main_mix"] = pair(np.concatenate(halves, 1))
    row = np.arange(128)
    n, oa, oj = row // 16, row // 8 % 2, row % 8
    a, p, jj = np.arange(256) // 128, np.arange(256) // 8 % 16, np.arange(256) % 8
    signed = np.where(n < 4, n, n - 8)
    turn = np.exp(-1j * angles(signed[:, None] * p[None, :], 16)) * (1j ** a)[None, :]
    same = oj[:, None] == jj[None, :]
    halves = [np.where(same, part(turn * s, oa[:, None]), 0.0) for s in (1, -1j)]
    out["zone_mix"] = pair(np.concatenate(halves, 1))
    return out


def split(value):
    high = value.astype(bf16)
    return high, (value - high.astype(f32)).astype(bf16)


def dot(left, right, dims=((1,), (0,))):
    return lax.dot_general(left, right, (dims, ((), ())), preferred_element_type=f32)


def dot3(left, right, dims=((1,), (0,))):
    return dot(left[0], right[0], dims) + (dot(left[0], right[1], dims) + dot(left[1], right[0], dims))


def iota(shape, dim):
    return lax.broadcasted_iota(jnp.int32, shape, dim)


def cos_of(phase):
    moved = phase + 512
    quarter = (moved >> 10) & 3
    angle = ((moved & 1023) - 512).astype(f32) * (2.0 * math.pi / FINE)
    square = angle * angle
    cosine = 1.0 + square * (-0.5 + square * (1.0 / 24 + square * (-1.0 / 720 + square * (1.0 / 40320))))
    sine = angle * (
        1.0 + square * (-1.0 / 6 + square * (1.0 / 120 + square * (-1.0 / 5040 + square * (1.0 / 362880))))
    )
    size = jnp.where((quarter & 1) == 0, cosine, sine)
    return jnp.where((quarter == 1) | (quarter == 2), -size, size)


def wave_of(index):
    return jnp.where(index < 1024, index, index - 2048).astype(f32)


def deal_kernel(eta, phi, out):
    for z in range(4):
        for source, base in ((eta, 0), (phi, 16)):
            for a in range(2):
                rows = source[a, 8 * z : 8 * z + 8, :]
                out[z, base + 8 * a : base + 8 * a + 8, :] = rows


def source_kernel(place, offsets, zone, out):
    tile = place[0]
    own = 4 * place[2] + place[1]
    ox = offsets[tile, 0]
    oy = offsets[tile, 1]
    lane = iota((128, 128), 1)
    wanted = (16 * own + (lane >> 3) - 2 * (ox & 7)) & 127
    pick = jnp.where(iota((128, 128), 0) == wanted, 1.0, 0.0).astype(bf16)
    high, low = split(zone[...] * zone_scale)
    cells = dot(high, pick) + dot(low, pick)
    phase = (iota((64, 128), 1) & 7) * (2 * oy + iota((64, 128), 0))
    real = cells * cos_of(phase)
    imag = cells * cos_of(phase + 1024)
    right = jnp.concatenate(
        [jnp.concatenate([real, imag], 1), jnp.concatenate([-imag, real], 1)], 0
    )
    lane = iota((256, 128), 1)
    g = iota((256, 128), 0)
    g = jnp.where(g < 128, g, g - 256)
    left = cos_of(8 * g * (2 * oy + (lane & 63)) + jnp.where(lane < 64, 0, 1024))
    out[...] = dot3(split(left), split(right))


def rows_kernel(
    place, own, other, slope_high, slope_low, lift_high, lift_low, cos_turn, sin_turn, high, low, out
):
    first_ky = 32 * place[0] + 8 * place[1]
    core = place[2]
    odd = 1.0 - 2.0 * core.astype(f32)
    wave_y = wave_of(first_ky + (iota((16, 256), 0) & 7)) * TURN_Y
    tiles = [[], [], [], [], []]
    for n in range(8):
        wave_x = wave_of(256 * n + iota((16, 256), 1)) * TURN_X
        kappa = jnp.sqrt(wave_x * wave_x + wave_y * wave_y)
        mine, theirs = (own, other) if n % 2 == 0 else (other, own)
        z = n // 2
        eta = jnp.where(core == 0, mine[z, 0:16, :], theirs[z, 0:16, :])
        phi = jnp.where(core == 0, mine[z, 16:32, :], theirs[z, 16:32, :])
        if n % 2:
            eta = eta * odd
            phi = phi * odd
        terms = (wave_x * eta, wave_y * eta, wave_x * phi, wave_y * phi, kappa * phi)
        for f in range(5):
            tiles[f].append(terms[f])
    cosine = cos_turn[core]
    sine = sin_turn[core]
    slope_mix = (slope_high[...], slope_low[...])
    lift_mix = (lift_high[...], lift_low[...])
    parts = [[], []]
    for f in range(5):
        rows = split(jnp.concatenate(tiles[f], 0))
        both = dot3(slope_mix if f < 4 else lift_mix, rows)
        first = both[:64]
        second = both[64:]
        turned = (first * cosine + second * sine).reshape(4, 2, 8, 256)
        quarter = (second * cosine - first * sine).reshape(4, 2, 8, 256)
        for a in range(2):
            parts[a].append(
                jnp.concatenate(
                    [turned[:, a].reshape(32, 256), quarter[:, a].reshape(32, 256)], 1
                )
            )
    real, imag = parts
    words = real[:4] + imag[:4] + [real[4], imag[4], -imag[4], real[4]]
    result = dot3((high[...], low[...]), split(jnp.concatenate(words, 0)), ((1,), (1,)))
    for q in range(3):
        out[pl.ds(q, 256, stride=3), :] = result[:, 128 * q : 128 * q + 128]


def columns_kernel(
    terms,
    source,
    high,
    low,
    cos_turn,
    sin_turn,
    gather_high,
    gather_low,
    gather_lift_high,
    gather_lift_low,
    deal_high,
    deal_low,
    out,
):
    words = split(
        jnp.concatenate([terms[pl.ds(q, 256, stride=3), :] for q in range(3)], 1)
    )
    with_cos = dot3((high[:, :256], low[:, :256]), words)
    with_sin = dot3((high[:, 256:], low[:, 256:]), words)
    real = with_cos[:, :128] - with_sin[:, 128:256]
    imag = with_sin[:, :128] + with_cos[:, 128:256]
    lane = iota((256, 128), 1)
    rolled = pltpu.roll(with_sin[:, 256:], 64, 1)
    lift = with_cos[:, 256:] + jnp.where(lane < 64, rolled, -rolled)
    cosine = cos_turn[...]
    sine = sin_turn[...]
    slopes = split(
        jnp.concatenate([real * cosine - imag * sine, real * sine + imag * cosine], 1)
    )
    lift = split(lift * cosine + pltpu.roll(lift, 64, 1) * sine)
    fields = dot3(slopes, (gather_high[...], gather_low[...]))
    lift = dot3(lift, (gather_lift_high[...], gather_lift_low[...]))
    slope_ex, slope_ey, slope_px, slope_py = (
        fields[:, 128 * k : 128 * k + 128] for k in range(4)
    )
    first_order = lift * (slope_ex * slope_ex + slope_ey * slope_ey) - (
        slope_px * slope_ex + slope_py * slope_ey
    )
    second_term = 0.5 * (lift * lift - slope_px * slope_px - slope_py * slope_py)
    products = jnp.concatenate([first_order, second_term], 1) * (time_step * spread)
    both = dot3(split(products), (deal_high[...], deal_low[...]))
    first = both[:, :128]
    second = both[:, 128:]
    turned = jnp.concatenate([first * cosine + second * sine, second * cosine - first * sine], 0)
    out[pl.ds(0, 256, stride=3), :] = dot3((high[...], low[...]), split(turned))
    out[pl.ds(1, 256, stride=3), :] = source[:, :128]
    out[pl.ds(2, 256, stride=3), :] = source[:, 128:]


def rows_back_kernel(
    place,
    offsets,
    terms,
    high,
    low,
    cos_main,
    sin_main,
    cos_zone,
    sin_zone,
    main_high,
    main_low,
    zone_high,
    zone_low,
    out,
    away,
    ends,
):
    core = place[2]
    depth = iota((8, 256), 0)
    spot = iota((8, 256), 1)
    lane = iota((8, 128), 1)
    row = iota((8, 128), 0)
    cells = [[], []]
    places = []
    last_places = []
    bases = []
    for t in range(0, 64, 2):
        ox = offsets[t, 0], offsets[t + 1, 0]
        base = ox[0] >> 3, ox[1] >> 3
        bases += base
        edge = jnp.where(row < 4, 8 * (2 * (ox[0] & 7)), 8 * (2 * (ox[1] & 7)))
        edge = jnp.where(((row & 3) == 0) & (core == 0), edge, 0)
        beyond = lane < edge
        for a in range(2):
            tile = terms[pl.ds(12 * t + 1 + a, 8, stride=3), :]
            cells[a].append(jnp.where(beyond, 0.0, tile))
            moved = jnp.where(beyond, tile, 0.0)
            ends[t : t + 1, 128 * a : 128 * a + 128] = moved[0:1, :]
            ends[t + 1 : t + 2, 128 * a : 128 * a + 128] = moved[4:5, :]
        target = jnp.where(depth < 4, base[0], base[1]) + (depth & 3) + 4 * core
        places.append(jnp.where(spot == (target & 255), 1.0, 0.0))
    for t in range(0, 64, 8):
        target = jnp.zeros((8, 256), jnp.int32)
        for k in range(8):
            target = jnp.where(depth == k, bases[t + k], target)
        last_places.append(jnp.where(spot == ((target + 8) & 255), 1.0, 0.0))
    where_to = jnp.concatenate(places, 0).astype(bf16)
    last_to = jnp.concatenate(last_places, 0).astype(bf16)
    cells = jnp.concatenate([jnp.concatenate(half, 0) for half in cells], 1)
    near = split(cells.T)
    far = split(ends[...].T)
    grid = (dot(near[0], where_to) + dot(near[1], where_to)) + (
        dot(far[0], last_to) + dot(far[1], last_to)
    )
    main = terms[pl.ds(0, 256, stride=3), :].T
    both = dot3(split(jnp.concatenate([main, grid], 0)), (high[...], low[...]))

    def turned(lines, cosine, sine):
        with_cos = lines[:, :, :256]
        with_sin = lines[:, :, 256:]
        real = with_cos * cosine - with_sin * sine
        imag = with_cos * sine + with_sin * cosine
        count = lines.shape[0] * lines.shape[1]
        return split(
            jnp.concatenate([real.reshape(count, 256), imag.reshape(count, 256)], 0)
        )

    main = turned(both[:128].reshape(4, 32, 512), cos_main[core][None], sin_main[core][None])
    zone = turned(both[128:].reshape(2, 128, 512), cos_zone[...][None], sin_zone[...][None])
    main = dot3((main_high[...], main_low[...]), main)
    zone = dot3((zone_high[...], zone_low[...]), zone)
    odd = 1.0 - 2.0 * core.astype(f32)
    blocks = []
    for n in range(8):
        block = main[32 * n : 32 * n + 32]
        if n % 2:
            block = block * odd
        blocks.append(
            jnp.concatenate([block[:16] + zone[16 * n : 16 * n + 16], block[16:]], 0)
        )
    for z in range(4):
        out[z] = jnp.where(core == 0, blocks[2 * z], blocks[2 * z + 1])
        away[z] = jnp.where(core == 0, blocks[2 * z + 1], blocks[2 * z])


def finish_kernel(place, terms, eta, phi, eta_next, phi_next):
    for z in range(4):
        rows = slice(8 * z, 8 * z + 8)
        wave_x = wave_of(256 * (2 * place[1] + place[2]) + iota((8, 256), 1)) * TURN_X
        wave_y = wave_of(32 * place[0] + 8 * z + iota((8, 256), 0)) * TURN_Y
        kappa = time_step * jnp.sqrt(wave_x * wave_x + wave_y * wave_y)
        for a in range(2):
            surface = eta[a, rows, :]
            potential = phi[a, rows, :]
            part_of = slice(8 * a, 8 * a + 8)
            eta_next[a, rows, :] = surface + kappa * potential + terms[z, part_of, :]
            part_of = slice(16 + 8 * a, 24 + 8 * a)
            linear = potential - (time_step * gravity) * surface
            phi_next[a, rows, :] = linear + terms[z, part_of, :]


def call(kernel, shapes, scalars, arrays, scratch=(), flops=0, limit=24):
    single = isinstance(shapes, tuple)
    shapes = [shapes] if single else shapes
    vmem = pl.BlockSpec(memory_space=pltpu.VMEM)
    smem = pl.BlockSpec(memory_space=pltpu.SMEM)
    moved = sum(4 * math.prod(s) for s in shapes) + sum(x.size * x.dtype.itemsize for x in arrays)
    result = pl.pallas_call(
        kernel,
        out_shape=[jax.ShapeDtypeStruct(s, f32) for s in shapes],
        in_specs=[smem] * len(scalars) + [vmem] * len(arrays),
        out_specs=[vmem] * len(shapes),
        scratch_shapes=list(scratch),
        compiler_params=pltpu.CompilerParams(vmem_limit_bytes=limit * 1024 * 1024),
        cost_estimate=pl.CostEstimate(flops=flops, bytes_accessed=moved, transcendentals=0),
        name=kernel.__name__,
    )(*scalars, *arrays)
    return result[0] if single else result


def stage_deal(eta, phi):
    return call(deal_kernel, (4, 32, 256), [], [eta, phi], limit=56)


def stage_source(place, offsets, zone):
    return call(source_kernel, (256, 256), [place, offsets], [zone], flops=2**26)


def stage_rows(place, own, other):
    t = tables()
    constants = [*t["slope"], *t["lift"], *t["rows_turn"], *t["turn"]]
    return call(rows_kernel, (768, 128), [place], [own, other, *constants], flops=2**30)


def stage_columns(terms, source):
    t = tables()
    constants = [*t["turn"], *t["y_turn"], *t["gather"], *t["gather_lift"], *t["deal"]]
    return call(columns_kernel, (768, 128), [], [terms, source, *constants], flops=2**30)


def stage_rows_back(place, offsets, terms):
    t = tables()
    constants = [*t["turn"], *t["main_turn"], *t["zone_turn"], *t["main_mix"], *t["zone_mix"]]
    scratch = [pltpu.VMEM((64, 256), f32)]
    arrays = [terms, *constants]
    return call(rows_back_kernel, [(4, 32, 256)] * 2, [place, offsets], arrays, scratch, flops=2**29)


def stage_finish(place, terms, eta, phi):
    return call(finish_kernel, [(2, 32, 256)] * 2, [place], [terms, eta, phi])


def local(eta_modes, phi_modes, zone_field, offsets):
    place = jnp.stack([lax.axis_index(axis) for axis in ("wide", "lane", "core")]).astype(jnp.int32)
    swap = functools.partial(lax.all_to_all, split_axis=0, concat_axis=0, tiled=True)

    def turn(words):
        return swap(words.reshape(256, 1, 384), ("wide", "lane")).reshape(768, 128)

    def across(rows):
        return lax.ppermute(rows, "core", [(0, 1), (1, 0)])

    own = swap(stage_deal(eta_modes, phi_modes), "lane")
    source = stage_source(place, offsets, zone_field)
    own, source = lax.optimization_barrier((own, source))
    columns = turn(stage_rows(place, own, across(own)))
    rows = turn(stage_columns(columns, source))
    share, away = stage_rows_back(place, offsets, rows)
    terms = swap(share + across(away), "lane")
    return tuple(stage_finish(place, terms, eta_modes, phi_modes))


def solution(mesh):
    wide, narrow = mesh.devices.shape
    chips = Mesh(mesh.devices.reshape(wide, narrow // 2, 2), ("wide", "lane", "core"))
    modes = P(None, "wide", ("lane", "core"))
    in_specs = (modes, modes, P("wide", None), P())
    return jax.shard_map(
        local, mesh=chips, in_specs=in_specs, out_specs=(modes, modes), check_vma=False
    )
```

```python
import functools
import math

import jax
import jax.numpy as jnp
import ml_dtypes
import numpy as np
from jax import lax
from jax.experimental import pallas as pl
from jax.experimental.pallas import tpu as pltpu
from jax.sharding import Mesh
from jax.sharding import PartitionSpec as P

NX = 2048
NY = 2048
FINE = 4096
TURN_X = 2.0 * math.pi / NX
TURN_Y = 2.0 * math.pi / NY
time_step = 0.04
gravity = 9.81
spread = 1.0 / math.sqrt(NX * NY)
zone_scale = 1.0 / math.sqrt(4096 * 128)
f32 = jnp.float32
bf16 = jnp.bfloat16


def part(value, which):
    return np.where(which == 0, np.real(value), np.imag(value))


def angles(ints, period):
    return 2.0 * np.pi * (np.asarray(ints) % period) / period


def pair(matrix):
    high = matrix.astype(np.float32).astype(ml_dtypes.bfloat16)
    low = (matrix - high.astype(np.float64)).astype(np.float32).astype(ml_dtypes.bfloat16)
    return np.stack([high, low])


def circle(phase):
    return np.stack([np.cos(phase), np.sin(phase)]).astype(np.float32)


@functools.cache
def tables():
    out = {}
    k256 = np.arange(256)
    phase = angles(k256[:, None] * k256[None, :], 256)
    out["turn"] = pair(np.concatenate([np.cos(phase), np.sin(phase)], 1))
    row = np.arange(64)
    i, a, jj = row // 16, row // 8 % 2, row % 8
    col = np.arange(128)
    n, ca, cj = col // 16, col // 8 % 2, col % 8
    base = np.exp(1j * angles(i[:, None] * n[None, :], 8)) * (1j ** ca)[None, :]
    same = jj[:, None] == cj[None, :]
    halves = [np.where(same, part(base * s, a[:, None]), 0.0) for s in (1j, -1, 1, 1j)]
    out["rows_mix"] = pair(np.concatenate(halves, 0))
    x0 = 4 * np.arange(2)[:, None] + np.arange(64)[None, :] // 16
    out["rows_turn"] = circle(angles(x0[:, :, None] * k256, NX))
    lane = np.arange(128)
    out["y_turn"] = circle(angles(k256[:, None] * (lane % 8)[None, :], NY))
    y0 = np.arange(8)
    turn = np.exp(1j * angles((lane % 8)[:, None] * y0[None, :], 8)) * spread
    gather = np.zeros((2, 128, 4, 128))
    gather_lift = np.zeros((128, 128))
    for k in range(128):
        f, i = k // 32, k // 8 % 4
        gather[0, k, f, y0 * 4 + i] = turn[k].real
        gather[1, k, f, y0 * 4 + i] = -turn[k].imag
        if k < 64:
            gather_lift[k, y0 * 4 + i] = turn[k].real if k < 32 else -turn[k].imag
    gather = np.concatenate([gather.reshape(256, 512), np.zeros((256, 128))], 1)
    gather[:128, 512:] = gather_lift
    out["gather"] = pair(gather)
    deal = np.zeros((2, 128, 2, 128))
    for k in range(128):
        f, a, i, jj = k // 64, k // 32 % 2, k // 8 % 4, k % 8
        turn = np.exp(-1j * angles(jj * y0, 8))
        deal[f, y0 * 4 + i, 0, k] = part(turn, a)
        deal[f, y0 * 4 + i, 1, k] = part(-1j * turn, a)
    out["deal"] = pair(deal.reshape(256, 256))
    x0 = 4 * np.arange(2)[:, None] + np.arange(32)[None, :] // 8
    out["main_turn"] = circle(angles(x0[:, :, None] * k256, NX))
    cell = np.arange(128) // 8
    out["zone_turn"] = circle(angles(cell[:, None] * k256, FINE))
    row = np.arange(256)
    n, of, oa, oj = row // 32, row // 16 % 2, row // 8 % 2, row % 8
    col = np.arange(128)
    f, a, i, jj = col // 64, col // 32 % 2, col // 8 % 4, col % 8
    turn = np.exp(-1j * angles(n[:, None] * i[None, :], 8)) * (1j ** a)[None, :]
    same = (of[:, None] == f[None, :]) & (oj[:, None] == jj[None, :])
    halves = [np.where(same, part(turn * s, oa[:, None]), 0.0) for s in (1, -1j)]
    out["main_mix"] = pair(np.concatenate(halves, 1))
    row = np.arange(128)
    n, oa, oj = row // 16, row // 8 % 2, row % 8
    a, p, jj = np.arange(256) // 128, np.arange(256) // 8 % 16, np.arange(256) % 8
    signed = np.where(n < 4, n, n - 8)
    turn = np.exp(-1j * angles(signed[:, None] * p[None, :], 16)) * (1j ** a)[None, :]
    same = oj[:, None] == jj[None, :]
    halves = [np.where(same, part(turn * s, oa[:, None]), 0.0) for s in (1, -1j)]
    out["zone_mix"] = pair(np.concatenate(halves, 1))
    return out


def split(value):
    high = value.astype(bf16)
    return high, (value - high.astype(f32)).astype(bf16)


def dot(left, right, dims=((1,), (0,))):
    return lax.dot_general(left, right, (dims, ((), ())), preferred_element_type=f32)


def dot3(left, right, dims=((1,), (0,))):
    return dot(left[0], right[0], dims) + (dot(left[0], right[1], dims) + dot(left[1], right[0], dims))


def iota(shape, dim):
    return lax.broadcasted_iota(jnp.int32, shape, dim)


def cos_of(phase):
    moved = phase + 512
    quarter = (moved >> 10) & 3
    angle = ((moved & 1023) - 512).astype(f32) * (2.0 * math.pi / FINE)
    square = angle * angle
    cosine = 1.0 + square * (-0.5 + square * (1.0 / 24 + square * (-1.0 / 720 + square * (1.0 / 40320))))
    sine = angle * (
        1.0 + square * (-1.0 / 6 + square * (1.0 / 120 + square * (-1.0 / 5040 + square * (1.0 / 362880))))
    )
    size = jnp.where((quarter & 1) == 0, cosine, sine)
    return jnp.where((quarter == 1) | (quarter == 2), -size, size)


def wave_of(index):
    return jnp.where(index < 1024, index, index - 2048).astype(f32)


def deal_kernel(eta, phi, out):
    for z in range(4):
        for source, base in ((eta, 0), (phi, 16)):
            for a in range(2):
                rows = source[a, 8 * z : 8 * z + 8, :]
                out[z, base + 8 * a : base + 8 * a + 8, :] = rows


def source_kernel(place, offsets, zone, out, places, beyond):
    tile = place[0]
    core = place[2]
    own = 4 * core + place[1]
    ox = offsets[tile, 0]
    oy = offsets[tile, 1]
    lane = iota((128, 128), 1)
    wanted = (16 * own + (lane >> 3) - 2 * (ox & 7)) & 127
    pick = jnp.where(iota((128, 128), 0) == wanted, 1.0, 0.0).astype(bf16)
    high, low = split(zone[...] * zone_scale)
    cells = dot(high, pick) + dot(low, pick)
    phase = (iota((64, 128), 1) & 7) * (2 * oy + iota((64, 128), 0))
    real = cells * cos_of(phase)
    imag = cells * cos_of(phase + 1024)
    right = jnp.concatenate(
        [jnp.concatenate([real, imag], 1), jnp.concatenate([-imag, real], 1)], 0
    )
    lane = iota((256, 128), 1)
    g = iota((256, 128), 0)
    g = jnp.where(g < 128, g, g - 256)
    left = cos_of(8 * g * (2 * oy + (lane & 63)) + jnp.where(lane < 64, 0, 1024))
    out[...] = dot3(split(left), split(right))
    row = iota((16, 256), 0)
    spot = iota((16, 256), 1)
    edge = jnp.zeros((8, 256), jnp.int32)
    tile_of = iota((8, 256), 1) >> 2
    for t in range(0, 64, 4):
        target = jnp.zeros((16, 256), jnp.int32)
        for k in range(4):
            x = offsets[t + k, 0]
            target = jnp.where((row >> 2) == k, x >> 3, target)
            edge = jnp.where(tile_of == t + k, 2 * (x & 7), edge)
        near = (target + (row & 3) + 4 * core) & 255
        far = (target + 8) & 255
        places[4 * t : 4 * t + 16, :] = jnp.where(spot == near, 1.0, 0.0).astype(bf16)
        places[256 + 4 * t : 272 + 4 * t, :] = jnp.where(spot == far, 1.0, 0.0).astype(bf16)
    edge = jnp.where(((iota((8, 256), 1) & 3) == 0) & (core == 0), edge, 0)
    for p in range(16):
        beyond[8 * p : 8 * p + 8, :] = jnp.where(edge > p, 1.0, 0.0)


def rows_kernel(
    place, own, other, mix, turn, circles, out
):
    first_ky = 32 * place[0] + 8 * place[1]
    core = place[2]
    odd = 1.0 - 2.0 * core.astype(f32)
    wave_y = wave_of(first_ky + (iota((16, 256), 0) & 7)) * TURN_Y
    tiles = [[], [], [], [], []]
    for n in range(8):
        wave_x = wave_of(256 * n + iota((16, 256), 1)) * TURN_X
        kappa = jnp.sqrt(wave_x * wave_x + wave_y * wave_y)
        mine, theirs = (own, other) if n % 2 == 0 else (other, own)
        z = n // 2
        eta = jnp.where(core == 0, mine[z, 0:16, :], theirs[z, 0:16, :])
        phi = jnp.where(core == 0, mine[z, 16:32, :], theirs[z, 16:32, :])
        if n % 2:
            eta = eta * odd
            phi = phi * odd
        terms = (wave_x * eta, wave_y * eta, wave_x * phi, wave_y * phi, kappa * phi)
        for f in range(5):
            tiles[f].append(terms[f])
    cosine = turn[0, core]
    sine = turn[1, core]
    parts = [[], []]
    for f in range(5):
        rows = split(jnp.concatenate(tiles[f], 0))
        kind = slice(0, 128) if f < 4 else slice(128, 256)
        both = dot3((mix[0, kind], mix[1, kind]), rows)
        first = both[:64]
        second = both[64:]
        turned = (first * cosine + second * sine).reshape(4, 2, 8, 256)
        quarter = (second * cosine - first * sine).reshape(4, 2, 8, 256)
        for a in range(2):
            parts[a].append(
                jnp.concatenate(
                    [turned[:, a].reshape(32, 256), quarter[:, a].reshape(32, 256)], 1
                )
            )
    real, imag = parts
    words = real[:4] + imag[:4] + [real[4], imag[4], -imag[4], real[4]]
    result = dot3(circles, split(jnp.concatenate(words, 0)), ((1,), (1,)))
    for q in range(3):
        out[pl.ds(q, 256, stride=3), :] = result[:, 128 * q : 128 * q + 128]


def columns_kernel(terms, source, circles, turn, gather, deal, out):
    words = split(
        jnp.concatenate([terms[pl.ds(q, 256, stride=3), :] for q in range(3)], 1)
    )
    with_cos = dot3((circles[0, :, :256], circles[1, :, :256]), words)
    with_sin = dot3((circles[0, :, 256:], circles[1, :, 256:]), words)
    real = with_cos[:, :128] - with_sin[:, 128:256]
    imag = with_sin[:, :128] + with_cos[:, 128:256]
    lane = iota((256, 128), 1)
    rolled = pltpu.roll(with_sin[:, 256:], 64, 1)
    lift = with_cos[:, 256:] + jnp.where(lane < 64, rolled, -rolled)
    cosine = turn[0]
    sine = turn[1]
    slopes = split(
        jnp.concatenate([real * cosine - imag * sine, real * sine + imag * cosine], 1)
    )
    lift = split(lift * cosine + pltpu.roll(lift, 64, 1) * sine)
    fields = dot3(slopes, (gather[0, :, :512], gather[1, :, :512]))
    lift = dot3(lift, (gather[0, :128, 512:], gather[1, :128, 512:]))
    slope_ex, slope_ey, slope_px, slope_py = (
        fields[:, 128 * k : 128 * k + 128] for k in range(4)
    )
    first_order = lift * (slope_ex * slope_ex + slope_ey * slope_ey) - (
        slope_px * slope_ex + slope_py * slope_ey
    )
    second_term = 0.5 * (lift * lift - slope_px * slope_px - slope_py * slope_py)
    products = jnp.concatenate([first_order, second_term], 1) * (time_step * spread)
    both = dot3(split(products), deal)
    first = both[:, :128]
    second = both[:, 128:]
    turned = jnp.concatenate([first * cosine + second * sine, second * cosine - first * sine], 0)
    out[pl.ds(0, 256, stride=3), :] = dot3(circles, split(turned))
    out[pl.ds(1, 256, stride=3), :] = source[:, :128]
    out[pl.ds(2, 256, stride=3), :] = source[:, 128:]


def rows_back_kernel(
    place, terms, places, beyond, circles, main_turn, zone_turn, main_mix, zone_mix, out
):
    core = place[2]
    cells = jnp.concatenate(
        [terms[pl.ds(1, 256, stride=3), :], terms[pl.ds(2, 256, stride=3), :]], 1
    ).T
    far = cells * jnp.concatenate([beyond[...], beyond[...]], 0)
    high, low = split(jnp.concatenate([cells - far, far], 1))
    grid = dot(high, places[...]) + dot(low, places[...])
    main = terms[pl.ds(0, 256, stride=3), :].T
    both = dot3(split(jnp.concatenate([main, grid], 0)), circles)

    def turned(lines, cosine, sine):
        with_cos = lines[:, :, :256]
        with_sin = lines[:, :, 256:]
        real = with_cos * cosine - with_sin * sine
        imag = with_cos * sine + with_sin * cosine
        count = lines.shape[0] * lines.shape[1]
        return split(
            jnp.concatenate([real.reshape(count, 256), imag.reshape(count, 256)], 0)
        )

    main = turned(both[:128].reshape(4, 32, 512), main_turn[0, core][None], main_turn[1, core][None])
    zone = turned(both[128:].reshape(2, 128, 512), zone_turn[0][None], zone_turn[1][None])
    main = dot3(main_mix, main)
    zone = dot3(zone_mix, zone)
    odd = 1.0 - 2.0 * core.astype(f32)
    for n in range(8):
        block = main[32 * n : 32 * n + 32]
        if n % 2:
            block = block * odd
        out[n, 0:16, :] = block[:16] + zone[16 * n : 16 * n + 16]
        out[n, 16:32, :] = block[16:]


def finish_kernel(place, terms, eta, phi, eta_next, phi_next):
    for z in range(4):
        rows = slice(8 * z, 8 * z + 8)
        wave_x = wave_of(256 * (2 * place[1] + place[2]) + iota((8, 256), 1)) * TURN_X
        wave_y = wave_of(32 * place[0] + 8 * z + iota((8, 256), 0)) * TURN_Y
        kappa = time_step * jnp.sqrt(wave_x * wave_x + wave_y * wave_y)
        for a in range(2):
            surface = eta[a, rows, :]
            potential = phi[a, rows, :]
            part_of = slice(8 * a, 8 * a + 8)
            added = terms[2 * z, part_of, :] + terms[2 * z + 1, part_of, :]
            eta_next[a, rows, :] = surface + kappa * potential + added
            part_of = slice(16 + 8 * a, 24 + 8 * a)
            added = terms[2 * z, part_of, :] + terms[2 * z + 1, part_of, :]
            phi_next[a, rows, :] = potential - (time_step * gravity) * surface + added


def call(kernel, shapes, scalars, arrays, flops=0, limit=24, types=None):
    single = isinstance(shapes, tuple)
    shapes = [shapes] if single else shapes
    types = [f32] * len(shapes) if types is None else types
    vmem = pl.BlockSpec(memory_space=pltpu.VMEM)
    smem = pl.BlockSpec(memory_space=pltpu.SMEM)
    moved = sum(4 * math.prod(s) for s in shapes) + sum(x.size * x.dtype.itemsize for x in arrays)
    result = pl.pallas_call(
        kernel,
        out_shape=[jax.ShapeDtypeStruct(s, t) for s, t in zip(shapes, types)],
        in_specs=[smem] * len(scalars) + [vmem] * len(arrays),
        out_specs=[vmem] * len(shapes),
        compiler_params=pltpu.CompilerParams(vmem_limit_bytes=limit * 1024 * 1024),
        cost_estimate=pl.CostEstimate(flops=flops, bytes_accessed=moved, transcendentals=0),
        name=kernel.__name__,
    )(*scalars, *arrays)
    return result[0] if single else result


def stage_deal(eta, phi):
    return call(deal_kernel, (4, 32, 256), [], [eta, phi], limit=56, flops=2**33)


def stage_source(place, offsets, zone):
    shapes = [(256, 256), (512, 256), (128, 256)]
    types = [f32, bf16, f32]
    return call(source_kernel, shapes, [place, offsets], [zone], flops=2**26, types=types)


def stage_rows(place, own, other):
    t = tables()
    arrays = [own, other, t["rows_mix"], t["rows_turn"], t["turn"]]
    return call(rows_kernel, (768, 128), [place], arrays, flops=2**30)


def stage_columns(terms, source):
    t = tables()
    arrays = [terms, source, t["turn"], t["y_turn"], t["gather"], t["deal"]]
    return call(columns_kernel, (768, 128), [], arrays, flops=2**30)


def stage_rows_back(place, terms, places, beyond):
    t = tables()
    arrays = [terms, places, beyond, t["turn"], t["main_turn"], t["zone_turn"]]
    arrays += [t["main_mix"], t["zone_mix"]]
    return call(rows_back_kernel, (8, 32, 256), [place], arrays, flops=2**29)


def stage_finish(place, terms, eta, phi):
    return call(finish_kernel, [(2, 32, 256)] * 2, [place], [terms, eta, phi])


def local(eta_modes, phi_modes, zone_field, offsets):
    place = jnp.stack([lax.axis_index(axis) for axis in ("wide", "lane", "core")]).astype(jnp.int32)
    swap = functools.partial(lax.all_to_all, split_axis=0, concat_axis=0, tiled=True)

    def turn(words):
        return swap(words.reshape(256, 1, 384), ("wide", "lane")).reshape(768, 128)

    def across(rows):
        return lax.ppermute(rows, "core", [(0, 1), (1, 0)])

    own, place = lax.optimization_barrier((swap(stage_deal(eta_modes, phi_modes), "lane"), place))
    source, places, beyond = stage_source(place, offsets, zone_field)
    columns = turn(stage_rows(place, own, across(own)))
    rows = turn(stage_columns(columns, source))
    terms = swap(stage_rows_back(place, rows, places, beyond), ("lane", "core"))
    return tuple(stage_finish(place, terms, eta_modes, phi_modes))


def solution(mesh):
    wide, narrow = mesh.devices.shape
    chips = Mesh(mesh.devices.reshape(wide, narrow // 2, 2), ("wide", "lane", "core"))
    modes = P(None, "wide", ("lane", "core"))
    in_specs = (modes, modes, P("wide", None), P())
    return jax.shard_map(
        local, mesh=chips, in_specs=in_specs, out_specs=(modes, modes), check_vma=False
    )
```

```python
import functools
import math

import jax
import jax.numpy as jnp
import ml_dtypes
import numpy as np
from jax import lax
from jax.experimental import pallas as pl
from jax.experimental.pallas import tpu as pltpu
from jax.sharding import Mesh
from jax.sharding import PartitionSpec as P

NX = 2048
NY = 2048
FINE = 4096
TURN_X = 2.0 * math.pi / NX
TURN_Y = 2.0 * math.pi / NY
time_step = 0.04
gravity = 9.81
spread = 1.0 / math.sqrt(NX * NY)
zone_scale = 1.0 / math.sqrt(4096 * 128)
f32 = jnp.float32
bf16 = jnp.bfloat16


def part(value, which):
    return np.where(which == 0, np.real(value), np.imag(value))


def angles(ints, period):
    return 2.0 * np.pi * (np.asarray(ints) % period) / period


def pair(matrix):
    high = matrix.astype(np.float32).astype(ml_dtypes.bfloat16)
    low = (matrix - high.astype(np.float64)).astype(np.float32).astype(ml_dtypes.bfloat16)
    return np.stack([high, low])


def circle(phase):
    return np.stack([np.cos(phase), np.sin(phase)]).astype(np.float32)


@functools.cache
def tables():
    out = {}
    k256 = np.arange(256)
    phase = angles(k256[:, None] * k256[None, :], 256)
    out["turn"] = pair(np.concatenate([np.cos(phase), np.sin(phase)], 1))
    row = np.arange(64)
    i, a, jj = row // 16, row // 8 % 2, row % 8
    col = np.arange(128)
    n, ca, cj = col // 16, col // 8 % 2, col % 8
    base = np.exp(1j * angles(i[:, None] * n[None, :], 8)) * (1j ** ca)[None, :]
    same = jj[:, None] == cj[None, :]
    halves = [np.where(same, part(base * s, a[:, None]), 0.0) for s in (1j, -1, 1, 1j)]
    out["rows_mix"] = pair(np.concatenate(halves, 0))
    x0 = 4 * np.arange(2)[:, None] + np.arange(64)[None, :] // 16
    out["rows_turn"] = circle(angles(x0[:, :, None] * k256, NX))
    lane = np.arange(128)
    out["y_turn"] = circle(angles(k256[:, None] * (lane % 8)[None, :], NY))
    y0 = np.arange(8)
    turn = np.exp(1j * angles((lane % 8)[:, None] * y0[None, :], 8)) * spread
    gather = np.zeros((2, 128, 4, 128))
    gather_lift = np.zeros((128, 128))
    for k in range(128):
        f, i = k // 32, k // 8 % 4
        gather[0, k, f, y0 * 4 + i] = turn[k].real
        gather[1, k, f, y0 * 4 + i] = -turn[k].imag
        if k < 64:
            gather_lift[k, y0 * 4 + i] = turn[k].real if k < 32 else -turn[k].imag
    gather = np.concatenate([gather.reshape(256, 512), np.zeros((256, 128))], 1)
    gather[:128, 512:] = gather_lift
    out["gather"] = pair(gather)
    deal = np.zeros((2, 128, 2, 128))
    for k in range(128):
        f, a, i, jj = k // 64, k // 32 % 2, k // 8 % 4, k % 8
        turn = np.exp(-1j * angles(jj * y0, 8))
        deal[f, y0 * 4 + i, 0, k] = part(turn, a)
        deal[f, y0 * 4 + i, 1, k] = part(-1j * turn, a)
    out["deal"] = pair(deal.reshape(256, 256))
    x0 = 4 * np.arange(2)[:, None] + np.arange(32)[None, :] // 8
    out["main_turn"] = circle(angles(x0[:, :, None] * k256, NX))
    cell = np.arange(128) // 8
    out["zone_turn"] = circle(angles(cell[:, None] * k256, FINE))
    row = np.arange(256)
    n, of, oa, oj = row // 32, row // 16 % 2, row // 8 % 2, row % 8
    col = np.arange(128)
    f, a, i, jj = col // 64, col // 32 % 2, col // 8 % 4, col % 8
    turn = np.exp(-1j * angles(n[:, None] * i[None, :], 8)) * (1j ** a)[None, :]
    same = (of[:, None] == f[None, :]) & (oj[:, None] == jj[None, :])
    halves = [np.where(same, part(turn * s, oa[:, None]), 0.0) for s in (1, -1j)]
    out["main_mix"] = pair(np.concatenate(halves, 1))
    row = np.arange(128)
    n, oa, oj = row // 16, row // 8 % 2, row % 8
    a, p, jj = np.arange(256) // 128, np.arange(256) // 8 % 16, np.arange(256) % 8
    signed = np.where(n < 4, n, n - 8)
    turn = np.exp(-1j * angles(signed[:, None] * p[None, :], 16)) * (1j ** a)[None, :]
    same = oj[:, None] == jj[None, :]
    halves = [np.where(same, part(turn * s, oa[:, None]), 0.0) for s in (1, -1j)]
    out["zone_mix"] = pair(np.concatenate(halves, 1))
    return out


def split(value):
    high = value.astype(bf16)
    return high, (value - high.astype(f32)).astype(bf16)


def dot(left, right, dims=((1,), (0,))):
    return lax.dot_general(left, right, (dims, ((), ())), preferred_element_type=f32)


def dot3(left, right, dims=((1,), (0,))):
    return dot(left[0], right[0], dims) + (dot(left[0], right[1], dims) + dot(left[1], right[0], dims))


def iota(shape, dim):
    return lax.broadcasted_iota(jnp.int32, shape, dim)


def cos_of(phase):
    moved = phase + 512
    quarter = (moved >> 10) & 3
    angle = ((moved & 1023) - 512).astype(f32) * (2.0 * math.pi / FINE)
    square = angle * angle
    cosine = 1.0 + square * (-0.5 + square * (1.0 / 24 + square * (-1.0 / 720 + square * (1.0 / 40320))))
    sine = angle * (
        1.0 + square * (-1.0 / 6 + square * (1.0 / 120 + square * (-1.0 / 5040 + square * (1.0 / 362880))))
    )
    size = jnp.where((quarter & 1) == 0, cosine, sine)
    return jnp.where((quarter == 1) | (quarter == 2), -size, size)


def wave_of(index):
    return jnp.where(index < 1024, index, index - 2048).astype(f32)


def deal_kernel(eta, phi, out):
    for z in range(4):
        for source, base in ((eta, 0), (phi, 16)):
            for a in range(2):
                rows = source[a, 8 * z : 8 * z + 8, :]
                for c in range(2):
                    out[2 * z + c, base + 8 * a : base + 8 * a + 8, :] = rows


def source_kernel(place, offsets, zone, out, places, beyond):
    tile = place[0]
    core = place[2]
    own = 4 * core + place[1]
    ox = offsets[tile, 0]
    oy = offsets[tile, 1]
    lane = iota((128, 128), 1)
    wanted = (16 * own + (lane >> 3) - 2 * (ox & 7)) & 127
    pick = jnp.where(iota((128, 128), 0) == wanted, 1.0, 0.0).astype(bf16)
    high, low = split(zone[...] * zone_scale)
    cells = dot(high, pick) + dot(low, pick)
    phase = (iota((64, 128), 1) & 7) * (2 * oy + iota((64, 128), 0))
    real = cells * cos_of(phase)
    imag = cells * cos_of(phase + 1024)
    right = jnp.concatenate(
        [jnp.concatenate([real, imag], 1), jnp.concatenate([-imag, real], 1)], 0
    )
    lane = iota((256, 128), 1)
    g = iota((256, 128), 0)
    g = jnp.where(g < 128, g, g - 256)
    left = cos_of(8 * g * (2 * oy + (lane & 63)) + jnp.where(lane < 64, 0, 1024))
    out[...] = dot3(split(left), split(right))
    row = iota((16, 256), 0)
    spot = iota((16, 256), 1)
    edge = jnp.zeros((8, 256), jnp.int32)
    tile_of = iota((8, 256), 1) >> 2
    for t in range(0, 64, 4):
        target = jnp.zeros((16, 256), jnp.int32)
        for k in range(4):
            x = offsets[t + k, 0]
            target = jnp.where((row >> 2) == k, x >> 3, target)
            edge = jnp.where(tile_of == t + k, 2 * (x & 7), edge)
        near = (target + (row & 3) + 4 * core) & 255
        far = (target + 8) & 255
        places[4 * t : 4 * t + 16, :] = jnp.where(spot == near, 1.0, 0.0).astype(bf16)
        places[256 + 4 * t : 272 + 4 * t, :] = jnp.where(spot == far, 1.0, 0.0).astype(bf16)
    edge = jnp.where(((iota((8, 256), 1) & 3) == 0) & (core == 0), edge, 0)
    for p in range(16):
        beyond[8 * p : 8 * p + 8, :] = jnp.where(edge > p, 1.0, 0.0)


def rows_kernel(place, modes, mix, turn, circles, out):
    first_ky = 32 * place[0] + 8 * place[1]
    core = place[2]
    odd = 1.0 - 2.0 * core.astype(f32)
    wave_y = wave_of(first_ky + (iota((16, 256), 0) & 7)) * TURN_Y
    tiles = [[], [], [], [], []]
    for n in range(8):
        wave_x = wave_of(256 * n + iota((16, 256), 1)) * TURN_X
        kappa = jnp.sqrt(wave_x * wave_x + wave_y * wave_y)
        eta = modes[n, 0:16, :]
        phi = modes[n, 16:32, :]
        if n % 2:
            eta = eta * odd
            phi = phi * odd
        terms = (wave_x * eta, wave_y * eta, wave_x * phi, wave_y * phi, kappa * phi)
        for f in range(5):
            tiles[f].append(terms[f])
    cosine = turn[0, core]
    sine = turn[1, core]
    parts = [[], []]
    for f in range(5):
        rows = split(jnp.concatenate(tiles[f], 0))
        kind = slice(0, 128) if f < 4 else slice(128, 256)
        both = dot3((mix[0, kind], mix[1, kind]), rows)
        first = both[:64]
        second = both[64:]
        turned = (first * cosine + second * sine).reshape(4, 2, 8, 256)
        quarter = (second * cosine - first * sine).reshape(4, 2, 8, 256)
        for a in range(2):
            parts[a].append(
                jnp.concatenate(
                    [turned[:, a].reshape(32, 256), quarter[:, a].reshape(32, 256)], 1
                )
            )
    real, imag = parts
    words = real[:4] + imag[:4] + [real[4], imag[4], -imag[4], real[4]]
    result = dot3(circles, split(jnp.concatenate(words, 0)), ((1,), (1,)))
    for q in range(3):
        out[pl.ds(q, 256, stride=3), :] = result[:, 128 * q : 128 * q + 128]


def columns_kernel(terms, source, circles, turn, gather, deal, out):
    words = split(
        jnp.concatenate([terms[pl.ds(q, 256, stride=3), :] for q in range(3)], 1)
    )
    with_cos = dot3((circles[0, :, :256], circles[1, :, :256]), words)
    with_sin = dot3((circles[0, :, 256:], circles[1, :, 256:]), words)
    real = with_cos[:, :128] - with_sin[:, 128:256]
    imag = with_sin[:, :128] + with_cos[:, 128:256]
    lane = iota((256, 128), 1)
    rolled = pltpu.roll(with_sin[:, 256:], 64, 1)
    lift = with_cos[:, 256:] + jnp.where(lane < 64, rolled, -rolled)
    cosine = turn[0]
    sine = turn[1]
    slopes = split(
        jnp.concatenate([real * cosine - imag * sine, real * sine + imag * cosine], 1)
    )
    lift = split(lift * cosine + pltpu.roll(lift, 64, 1) * sine)
    fields = dot3(slopes, (gather[0, :, :512], gather[1, :, :512]))
    lift = dot3(lift, (gather[0, :128, 512:], gather[1, :128, 512:]))
    slope_ex, slope_ey, slope_px, slope_py = (
        fields[:, 128 * k : 128 * k + 128] for k in range(4)
    )
    first_order = lift * (slope_ex * slope_ex + slope_ey * slope_ey) - (
        slope_px * slope_ex + slope_py * slope_ey
    )
    second_term = 0.5 * (lift * lift - slope_px * slope_px - slope_py * slope_py)
    products = jnp.concatenate([first_order, second_term], 1) * (time_step * spread)
    both = dot3(split(products), deal)
    first = both[:, :128]
    second = both[:, 128:]
    turned = jnp.concatenate([first * cosine + second * sine, second * cosine - first * sine], 0)
    out[pl.ds(0, 256, stride=3), :] = dot3(circles, split(turned))
    out[pl.ds(1, 256, stride=3), :] = source[:, :128]
    out[pl.ds(2, 256, stride=3), :] = source[:, 128:]


def rows_back_kernel(
    place, terms, places, beyond, circles, main_turn, zone_turn, main_mix, zone_mix, out
):
    core = place[2]
    cells = jnp.concatenate(
        [terms[pl.ds(1, 256, stride=3), :], terms[pl.ds(2, 256, stride=3), :]], 1
    ).T
    far = cells * jnp.concatenate([beyond[...], beyond[...]], 0)
    high, low = split(jnp.concatenate([cells - far, far], 1))
    grid = dot(high, places[...]) + dot(low, places[...])
    main = terms[pl.ds(0, 256, stride=3), :].T
    both = dot3(split(jnp.concatenate([main, grid], 0)), circles)

    def turned(lines, cosine, sine):
        with_cos = lines[:, :, :256]
        with_sin = lines[:, :, 256:]
        real = with_cos * cosine - with_sin * sine
        imag = with_cos * sine + with_sin * cosine
        count = lines.shape[0] * lines.shape[1]
        return split(
            jnp.concatenate([real.reshape(count, 256), imag.reshape(count, 256)], 0)
        )

    main = turned(both[:128].reshape(4, 32, 512), main_turn[0, core][None], main_turn[1, core][None])
    zone = turned(both[128:].reshape(2, 128, 512), zone_turn[0][None], zone_turn[1][None])
    main = dot3(main_mix, main)
    zone = dot3(zone_mix, zone)
    odd = 1.0 - 2.0 * core.astype(f32)
    for n in range(8):
        block = main[32 * n : 32 * n + 32]
        if n % 2:
            block = block * odd
        out[n, 0:16, :] = block[:16] + zone[16 * n : 16 * n + 16]
        out[n, 16:32, :] = block[16:]


def finish_kernel(place, terms, eta, phi, eta_next, phi_next):
    for z in range(4):
        rows = slice(8 * z, 8 * z + 8)
        wave_x = wave_of(256 * (2 * place[1] + place[2]) + iota((8, 256), 1)) * TURN_X
        wave_y = wave_of(32 * place[0] + 8 * z + iota((8, 256), 0)) * TURN_Y
        kappa = time_step * jnp.sqrt(wave_x * wave_x + wave_y * wave_y)
        for a in range(2):
            surface = eta[a, rows, :]
            potential = phi[a, rows, :]
            part_of = slice(8 * a, 8 * a + 8)
            added = terms[2 * z, part_of, :] + terms[2 * z + 1, part_of, :]
            eta_next[a, rows, :] = surface + kappa * potential + added
            part_of = slice(16 + 8 * a, 24 + 8 * a)
            added = terms[2 * z, part_of, :] + terms[2 * z + 1, part_of, :]
            phi_next[a, rows, :] = potential - (time_step * gravity) * surface + added


def call(kernel, shapes, scalars, arrays, flops=0, limit=24, types=None):
    single = isinstance(shapes, tuple)
    shapes = [shapes] if single else shapes
    types = [f32] * len(shapes) if types is None else types
    vmem = pl.BlockSpec(memory_space=pltpu.VMEM)
    smem = pl.BlockSpec(memory_space=pltpu.SMEM)
    moved = sum(4 * math.prod(s) for s in shapes) + sum(x.size * x.dtype.itemsize for x in arrays)
    result = pl.pallas_call(
        kernel,
        out_shape=[jax.ShapeDtypeStruct(s, t) for s, t in zip(shapes, types)],
        in_specs=[smem] * len(scalars) + [vmem] * len(arrays),
        out_specs=[vmem] * len(shapes),
        compiler_params=pltpu.CompilerParams(vmem_limit_bytes=limit * 1024 * 1024),
        cost_estimate=pl.CostEstimate(flops=flops, bytes_accessed=moved, transcendentals=0),
        name=kernel.__name__,
    )(*scalars, *arrays)
    return result[0] if single else result


def stage_deal(eta, phi):
    return call(deal_kernel, (8, 32, 256), [], [eta, phi], limit=56, flops=2**33)


def stage_source(place, offsets, zone):
    shapes = [(256, 256), (512, 256), (128, 256)]
    types = [f32, bf16, f32]
    return call(source_kernel, shapes, [place, offsets], [zone], flops=2**26, types=types)


def stage_rows(place, modes):
    t = tables()
    arrays = [modes, t["rows_mix"], t["rows_turn"], t["turn"]]
    return call(rows_kernel, (768, 128), [place], arrays, flops=2**30)


def stage_columns(terms, source):
    t = tables()
    arrays = [terms, source, t["turn"], t["y_turn"], t["gather"], t["deal"]]
    return call(columns_kernel, (768, 128), [], arrays, flops=2**30)


def stage_rows_back(place, terms, places, beyond):
    t = tables()
    arrays = [terms, places, beyond, t["turn"], t["main_turn"], t["zone_turn"]]
    arrays += [t["main_mix"], t["zone_mix"]]
    return call(rows_back_kernel, (8, 32, 256), [place], arrays, flops=2**29)


def stage_finish(place, terms, eta, phi):
    return call(finish_kernel, [(2, 32, 256)] * 2, [place], [terms, eta, phi])


def local(eta_modes, phi_modes, zone_field, offsets):
    place = jnp.stack([lax.axis_index(axis) for axis in ("wide", "lane", "core")]).astype(jnp.int32)
    swap = functools.partial(lax.all_to_all, split_axis=0, concat_axis=0, tiled=True)

    def turn(words):
        return swap(words.reshape(256, 1, 384), ("wide", "lane")).reshape(768, 128)

    modes = swap(stage_deal(eta_modes, phi_modes), ("lane", "core"))
    ready = stage_source(place, offsets, zone_field)
    modes, (source, places, beyond) = lax.optimization_barrier((modes, ready))
    columns = turn(stage_rows(place, modes))
    rows = turn(stage_columns(columns, source))
    terms = swap(stage_rows_back(place, rows, places, beyond), ("lane", "core"))
    return tuple(stage_finish(place, terms, eta_modes, phi_modes))


def solution(mesh):
    wide, narrow = mesh.devices.shape
    chips = Mesh(mesh.devices.reshape(wide, narrow // 2, 2), ("wide", "lane", "core"))
    modes = P(None, "wide", ("lane", "core"))
    in_specs = (modes, modes, P("wide", None), P())
    return jax.shard_map(
        local, mesh=chips, in_specs=in_specs, out_specs=(modes, modes), check_vma=False
    )
```

```python
import functools
import math

import jax
import jax.numpy as jnp
import ml_dtypes
import numpy as np
from jax import lax
from jax.experimental import pallas as pl
from jax.experimental.pallas import tpu as pltpu
from jax.sharding import Mesh
from jax.sharding import PartitionSpec as P

NX = 2048
NY = 2048
FINE = 4096
TURN_X = 2.0 * math.pi / NX
TURN_Y = 2.0 * math.pi / NY
time_step = 0.04
gravity = 9.81
spread = 1.0 / math.sqrt(NX * NY)
zone_scale = 1.0 / math.sqrt(4096 * 128)
f32 = jnp.float32
bf16 = jnp.bfloat16


def part(value, which):
    return np.where(which == 0, np.real(value), np.imag(value))


def angles(ints, period):
    return 2.0 * np.pi * (np.asarray(ints) % period) / period


def pair(matrix):
    high = matrix.astype(np.float32).astype(ml_dtypes.bfloat16)
    low = (matrix - high.astype(np.float64)).astype(np.float32).astype(ml_dtypes.bfloat16)
    return np.stack([high, low])


def circle(phase):
    return np.stack([np.cos(phase), np.sin(phase)]).astype(np.float32)


@functools.cache
def tables():
    out = {}
    k256 = np.arange(256)
    phase = angles(k256[:, None] * k256[None, :], 256)
    out["turn"] = pair(np.concatenate([np.cos(phase), np.sin(phase)], 1))
    held = np.arange(256) % 64 * 4 + np.arange(256) // 64
    phase = angles(k256[:, None] * held[None, :], 256)
    out["into_y"] = pair(np.concatenate([np.cos(phase), np.sin(phase)], 1))
    out["from_y"] = pair(np.concatenate([np.cos(phase).T, np.sin(phase).T], 1))
    row = np.arange(64)
    i, a, jj = row // 16, row // 8 % 2, row % 8
    col = np.arange(128)
    n, ca, cj = col // 16, col // 8 % 2, col % 8
    base = np.exp(1j * angles(i[:, None] * n[None, :], 8)) * (1j ** ca)[None, :]
    same = jj[:, None] == cj[None, :]
    halves = [np.where(same, part(base * s, a[:, None]), 0.0) for s in (1j, -1, 1, 1j)]
    out["rows_mix"] = pair(np.concatenate(halves, 0))
    x0 = 4 * np.arange(2)[:, None] + np.arange(64)[None, :] // 16
    out["rows_turn"] = circle(angles(x0[:, :, None] * k256, NX))
    lane = np.arange(128)
    out["y_turn"] = circle(angles(k256[:, None] * (lane % 8)[None, :], NY))
    y0 = np.arange(8)
    turn = np.exp(1j * angles((lane % 8)[:, None] * y0[None, :], 8)) * spread
    gather = np.zeros((2, 128, 4, 128))
    gather_lift = np.zeros((128, 128))
    for k in range(128):
        f, i = k // 32, k // 8 % 4
        gather[0, k, f, y0 * 4 + i] = turn[k].real
        gather[1, k, f, y0 * 4 + i] = -turn[k].imag
        if k < 64:
            gather_lift[k, y0 * 4 + i] = turn[k].real if k < 32 else -turn[k].imag
    gather = np.concatenate([gather.reshape(256, 512), np.zeros((256, 128))], 1)
    gather[:128, 512:] = gather_lift
    out["gather"] = pair(gather)
    deal = np.zeros((2, 128, 2, 128))
    for k in range(128):
        f, a, i, jj = k // 64, k // 32 % 2, k // 8 % 4, k % 8
        turn = np.exp(-1j * angles(jj * y0, 8))
        deal[f, y0 * 4 + i, 0, k] = part(turn, a)
        deal[f, y0 * 4 + i, 1, k] = part(-1j * turn, a)
    out["deal"] = pair(deal.reshape(256, 256))
    x0 = 4 * np.arange(2)[:, None] + np.arange(32)[None, :] // 8
    out["main_turn"] = circle(angles(x0[:, :, None] * k256, NX))
    cell = np.arange(128) // 8
    out["zone_turn"] = circle(angles(cell[:, None] * k256, FINE))
    row = np.arange(256)
    n, of, oa, oj = row // 32, row // 16 % 2, row // 8 % 2, row % 8
    col = np.arange(128)
    f, a, i, jj = col // 64, col // 32 % 2, col // 8 % 4, col % 8
    turn = np.exp(-1j * angles(n[:, None] * i[None, :], 8)) * (1j ** a)[None, :]
    same = (of[:, None] == f[None, :]) & (oj[:, None] == jj[None, :])
    halves = [np.where(same, part(turn * s, oa[:, None]), 0.0) for s in (1, -1j)]
    out["main_mix"] = pair(np.concatenate(halves, 1))
    row = np.arange(128)
    n, oa, oj = row // 16, row // 8 % 2, row % 8
    a, p, jj = np.arange(256) // 128, np.arange(256) // 8 % 16, np.arange(256) % 8
    signed = np.where(n < 4, n, n - 8)
    turn = np.exp(-1j * angles(signed[:, None] * p[None, :], 16)) * (1j ** a)[None, :]
    same = oj[:, None] == jj[None, :]
    halves = [np.where(same, part(turn * s, oa[:, None]), 0.0) for s in (1, -1j)]
    out["zone_mix"] = pair(np.concatenate(halves, 1))
    return out


def split(value):
    high = value.astype(bf16)
    return high, (value - high.astype(f32)).astype(bf16)


def dot(left, right, dims=((1,), (0,))):
    return lax.dot_general(left, right, (dims, ((), ())), preferred_element_type=f32)


def dot3(left, right, dims=((1,), (0,))):
    along = dims[0][0], dims[1][0]
    left = jnp.concatenate([left[0], left[0], left[1]], along[0])
    right = jnp.concatenate([right[0], right[1], right[0]], along[1])
    return dot(left, right, dims)


def iota(shape, dim):
    return lax.broadcasted_iota(jnp.int32, shape, dim)


def cos_of(phase):
    moved = phase + 512
    quarter = (moved >> 10) & 3
    angle = ((moved & 1023) - 512).astype(f32) * (2.0 * math.pi / FINE)
    square = angle * angle
    cosine = 1.0 + square * (-0.5 + square * (1.0 / 24 + square * (-1.0 / 720 + square * (1.0 / 40320))))
    sine = angle * (
        1.0 + square * (-1.0 / 6 + square * (1.0 / 120 + square * (-1.0 / 5040 + square * (1.0 / 362880))))
    )
    size = jnp.where((quarter & 1) == 0, cosine, sine)
    return jnp.where((quarter == 1) | (quarter == 2), -size, size)


def wave_of(index):
    return jnp.where(index < 1024, index, index - 2048).astype(f32)


def deal_kernel(eta, phi, out, held, arrived, left):
    copies = [
        pltpu.make_async_copy(source, held.at[k], arrived.at[k])
        for k, source in enumerate((eta, phi))
    ]
    for copy in copies:
        copy.start()
    dealt = []
    for k in range(2):
        copies[k].wait()
        for n in range(8):
            rows = held.at[k, :, 8 * (n % 4) : 8 * (n % 4) + 8, :]
            dealt.append(pltpu.make_async_copy(rows, out.at[n, k], left.at[8 * k + n]))
            dealt[-1].start()
    for copy in dealt:
        copy.wait()


def source_kernel(place, offsets, zone, out, places, beyond):
    tile = place[0]
    core = place[2]
    own = 4 * core + place[1]
    ox = offsets[tile, 0]
    oy = offsets[tile, 1]
    lane = iota((128, 128), 1)
    wanted = (16 * own + (lane >> 3) - 2 * (ox & 7)) & 127
    pick = jnp.where(iota((128, 128), 0) == wanted, 1.0, 0.0).astype(bf16)
    high, low = split(zone[...] * zone_scale)
    cells = dot(high, pick) + dot(low, pick)
    phase = (iota((64, 128), 1) & 7) * (2 * oy + iota((64, 128), 0))
    real = cells * cos_of(phase)
    imag = cells * cos_of(phase + 1024)
    right = jnp.concatenate(
        [jnp.concatenate([real, imag], 1), jnp.concatenate([-imag, real], 1)], 0
    )
    lane = iota((256, 128), 1)
    g = iota((256, 128), 0)
    g = 4 * (g & 63) + (g >> 6)
    g = jnp.where(g < 128, g, g - 256)
    left = cos_of(8 * g * (2 * oy + (lane & 63)) + jnp.where(lane < 64, 0, 1024))
    out[...] = dot3(split(left), split(right))
    row = iota((16, 256), 0)
    spot = iota((16, 256), 1)
    edge = jnp.zeros((8, 256), jnp.int32)
    tile_of = iota((8, 256), 1) & 63
    for t in range(0, 64, 16):
        target = jnp.zeros((16, 256), jnp.int32)
        for k in range(16):
            x = offsets[t + k, 0]
            target = jnp.where(row == k, x >> 3, target)
            edge = jnp.where(tile_of == t + k, 2 * (x & 7), edge)
        far = (target + 8) & 255
        for z in range(4):
            near = (target + z + 4 * core) & 255
            first = 64 * z + t
            places[first : first + 16, :] = jnp.where(spot == near, 1.0, 0.0).astype(bf16)
            first += 256
            places[first : first + 16, :] = jnp.where(spot == far, 1.0, 0.0).astype(bf16)
    edge = jnp.where((iota((8, 256), 1) < 64) & (core == 0), edge, 0)
    for p in range(16):
        beyond[8 * p : 8 * p + 8, :] = jnp.where(edge > p, 1.0, 0.0)


def rows_kernel(place, modes, mix, turn, circles, out):
    first_ky = 32 * place[0] + 8 * place[1]
    core = place[2]
    odd = 1.0 - 2.0 * core.astype(f32)
    wave_y = wave_of(first_ky + (iota((16, 256), 0) & 7)) * TURN_Y
    tiles = [[], [], [], [], []]
    for n in range(8):
        wave_x = wave_of(256 * n + iota((16, 256), 1)) * TURN_X
        kappa = jnp.sqrt(wave_x * wave_x + wave_y * wave_y)
        block = 4 * (n % 2) + n // 2
        eta = modes[block, 0:16, :]
        phi = modes[block, 16:32, :]
        if n % 2:
            eta = eta * odd
            phi = phi * odd
        terms = (wave_x * eta, wave_y * eta, wave_x * phi, wave_y * phi, kappa * phi)
        for f in range(5):
            tiles[f].append(terms[f])
    cosine = turn[0, core]
    sine = turn[1, core]
    parts = [[], []]
    for f in range(5):
        rows = split(jnp.concatenate(tiles[f], 0))
        kind = slice(0, 128) if f < 4 else slice(128, 256)
        both = dot3((mix[0, kind], mix[1, kind]), rows)
        first = both[:64]
        second = both[64:]
        turned = (first * cosine + second * sine).reshape(4, 2, 8, 256)
        quarter = (second * cosine - first * sine).reshape(4, 2, 8, 256)
        for a in range(2):
            parts[a].append(
                jnp.concatenate(
                    [turned[:, a].reshape(32, 256), quarter[:, a].reshape(32, 256)], 1
                )
            )
    real, imag = parts
    words = real[:4] + imag[:4] + [real[4], imag[4], -imag[4], real[4]]
    result = dot3(circles, split(jnp.concatenate(words, 0)), ((1,), (1,)))
    for q in range(3):
        out[pl.ds(q, 256, stride=3), :] = result[:, 128 * q : 128 * q + 128]


def columns_kernel(terms, source, into_y, from_y, turn, gather, deal, out):
    words = split(
        jnp.concatenate([terms[pl.ds(q, 256, stride=3), :] for q in range(3)], 1)
    )
    with_cos = dot3((into_y[0, :, :256], into_y[1, :, :256]), words)
    with_sin = dot3((into_y[0, :, 256:], into_y[1, :, 256:]), words)
    real = with_cos[:, :128] - with_sin[:, 128:256]
    imag = with_sin[:, :128] + with_cos[:, 128:256]
    lane = iota((256, 128), 1)
    rolled = pltpu.roll(with_sin[:, 256:], 64, 1)
    lift = with_cos[:, 256:] + jnp.where(lane < 64, rolled, -rolled)
    cosine = turn[0]
    sine = turn[1]
    slopes = split(
        jnp.concatenate([real * cosine - imag * sine, real * sine + imag * cosine], 1)
    )
    lift = split(lift * cosine + pltpu.roll(lift, 64, 1) * sine)
    fields = dot3(slopes, (gather[0, :, :512], gather[1, :, :512]))
    lift = dot3(lift, (gather[0, :128, 512:], gather[1, :128, 512:]))
    slope_ex, slope_ey, slope_px, slope_py = (
        fields[:, 128 * k : 128 * k + 128] for k in range(4)
    )
    first_order = lift * (slope_ex * slope_ex + slope_ey * slope_ey) - (
        slope_px * slope_ex + slope_py * slope_ey
    )
    second_term = 0.5 * (lift * lift - slope_px * slope_px - slope_py * slope_py)
    products = jnp.concatenate([first_order, second_term], 1) * (time_step * spread)
    both = dot3(split(products), deal)
    first = both[:, :128]
    second = both[:, 128:]
    turned = jnp.concatenate([first * cosine + second * sine, second * cosine - first * sine], 0)
    out[pl.ds(0, 256, stride=3), :] = dot3(from_y, split(turned))
    out[pl.ds(1, 256, stride=3), :] = source[:, :128]
    out[pl.ds(2, 256, stride=3), :] = source[:, 128:]


def rows_back_kernel(
    place, terms, places, beyond, circles, main_turn, zone_turn, main_mix, zone_mix, out
):
    core = place[2]
    cells = jnp.concatenate(
        [terms[pl.ds(1, 256, stride=3), :], terms[pl.ds(2, 256, stride=3), :]], 1
    ).T
    far = cells * jnp.concatenate([beyond[...], beyond[...]], 0)
    high, low = split(jnp.concatenate([cells - far, far], 1))
    grid = dot(high, places[...]) + dot(low, places[...])
    main = terms[pl.ds(0, 256, stride=3), :].T
    both = dot3(split(jnp.concatenate([main, grid], 0)), circles)

    def turned(lines, cosine, sine):
        with_cos = lines[:, :, :256]
        with_sin = lines[:, :, 256:]
        real = with_cos * cosine - with_sin * sine
        imag = with_cos * sine + with_sin * cosine
        count = lines.shape[0] * lines.shape[1]
        return split(
            jnp.concatenate([real.reshape(count, 256), imag.reshape(count, 256)], 0)
        )

    main = turned(both[:128].reshape(4, 32, 512), main_turn[0, core][None], main_turn[1, core][None])
    zone = turned(both[128:].reshape(2, 128, 512), zone_turn[0][None], zone_turn[1][None])
    main = dot3(main_mix, main)
    zone = dot3(zone_mix, zone)
    odd = 1.0 - 2.0 * core.astype(f32)
    for n in range(8):
        block = main[32 * n : 32 * n + 32]
        if n % 2:
            block = block * odd
        where = 4 * (n % 2) + n // 2
        out[where, 0:16, :] = block[:16] + zone[16 * n : 16 * n + 16]
        out[where, 16:32, :] = block[16:]


def finish_kernel(place, terms, eta, phi, eta_next, phi_next):
    for z in range(4):
        rows = slice(8 * z, 8 * z + 8)
        wave_x = wave_of(256 * (2 * place[1] + place[2]) + iota((8, 256), 1)) * TURN_X
        wave_y = wave_of(32 * place[0] + 8 * z + iota((8, 256), 0)) * TURN_Y
        kappa = time_step * jnp.sqrt(wave_x * wave_x + wave_y * wave_y)
        for a in range(2):
            surface = eta[a, rows, :]
            potential = phi[a, rows, :]
            part_of = slice(8 * a, 8 * a + 8)
            added = terms[z, part_of, :] + terms[4 + z, part_of, :]
            eta_next[a, rows, :] = surface + kappa * potential + added
            part_of = slice(16 + 8 * a, 24 + 8 * a)
            added = terms[z, part_of, :] + terms[4 + z, part_of, :]
            phi_next[a, rows, :] = potential - (time_step * gravity) * surface + added


def call(kernel, shapes, scalars, arrays, flops=0, limit=24, types=None):
    single = isinstance(shapes, tuple)
    shapes = [shapes] if single else shapes
    types = [f32] * len(shapes) if types is None else types
    vmem = pl.BlockSpec(memory_space=pltpu.VMEM)
    smem = pl.BlockSpec(memory_space=pltpu.SMEM)
    moved = sum(4 * math.prod(s) for s in shapes) + sum(x.size * x.dtype.itemsize for x in arrays)
    result = pl.pallas_call(
        kernel,
        out_shape=[jax.ShapeDtypeStruct(s, t) for s, t in zip(shapes, types)],
        in_specs=[smem] * len(scalars) + [vmem] * len(arrays),
        out_specs=[vmem] * len(shapes),
        compiler_params=pltpu.CompilerParams(vmem_limit_bytes=limit * 1024 * 1024),
        cost_estimate=pl.CostEstimate(flops=flops, bytes_accessed=moved, transcendentals=0),
        name=kernel.__name__,
    )(*scalars, *arrays)
    return result[0] if single else result


def stage_deal(eta, phi):
    far = pl.BlockSpec(memory_space=pltpu.HBM)
    dealt = pl.pallas_call(
        deal_kernel,
        out_shape=jax.ShapeDtypeStruct((8, 2, 2, 8, 256), f32),
        in_specs=[far, far],
        out_specs=pl.BlockSpec(memory_space=pl.ANY),
        scratch_shapes=[
            pltpu.VMEM((2, 2, 32, 256), f32),
            pltpu.SemaphoreType.DMA((2,)),
            pltpu.SemaphoreType.DMA((16,)),
        ],
        compiler_params=pltpu.CompilerParams(vmem_limit_bytes=56 * 1024 * 1024),
        cost_estimate=pl.CostEstimate(flops=2**33, bytes_accessed=2**19, transcendentals=0),
        name="deal_kernel",
    )(eta, phi)
    return dealt.reshape(8, 32, 256)


def stage_source(place, offsets, zone):
    shapes = [(256, 256), (512, 256), (128, 256)]
    types = [f32, bf16, f32]
    return call(source_kernel, shapes, [place, offsets], [zone], flops=2**26, types=types)


def stage_rows(place, modes):
    t = tables()
    arrays = [modes, t["rows_mix"], t["rows_turn"], t["turn"]]
    return call(rows_kernel, (768, 128), [place], arrays, flops=2**30)


def stage_columns(terms, source):
    t = tables()
    arrays = [terms, source, t["into_y"], t["from_y"], t["y_turn"], t["gather"], t["deal"]]
    return call(columns_kernel, (768, 128), [], arrays, flops=2**30)


def stage_rows_back(place, terms, places, beyond):
    t = tables()
    arrays = [terms, places, beyond, t["turn"], t["main_turn"], t["zone_turn"]]
    arrays += [t["main_mix"], t["zone_mix"]]
    return call(rows_back_kernel, (8, 32, 256), [place], arrays, flops=2**29)


def stage_finish(place, terms, eta, phi):
    return call(finish_kernel, [(2, 32, 256)] * 2, [place], [terms, eta, phi])


def local(eta_modes, phi_modes, zone_field, offsets):
    place = jnp.stack([lax.axis_index(axis) for axis in ("wide", "lane", "core")]).astype(jnp.int32)
    swap = functools.partial(lax.all_to_all, split_axis=0, concat_axis=0, tiled=True)

    def turn(words):
        return swap(words.reshape(256, 1, 384), ("lane", "wide")).reshape(768, 128)

    modes = swap(stage_deal(eta_modes, phi_modes), ("core", "lane"))
    ready = stage_source(place, offsets, zone_field)
    modes, (source, places, beyond) = lax.optimization_barrier((modes, ready))
    columns = turn(stage_rows(place, modes))
    rows = turn(stage_columns(columns, source))
    terms = swap(stage_rows_back(place, rows, places, beyond), ("core", "lane"))
    return tuple(stage_finish(place, terms, eta_modes, phi_modes))


def solution(mesh):
    wide, narrow = mesh.devices.shape
    chips = Mesh(mesh.devices.reshape(wide, narrow // 2, 2), ("wide", "lane", "core"))
    modes = P(None, "wide", ("lane", "core"))
    in_specs = (modes, modes, P("wide", None), P())
    return jax.shard_map(
        local, mesh=chips, in_specs=in_specs, out_specs=(modes, modes), check_vma=False
    )
```

```python
import functools
import math

import jax
import jax.numpy as jnp
import ml_dtypes
import numpy as np
from jax import lax
from jax.experimental import pallas as pl
from jax.experimental.pallas import tpu as pltpu
from jax.sharding import Mesh
from jax.sharding import PartitionSpec as P

NX = 2048
NY = 2048
FINE = 4096
TURN_X = 2.0 * math.pi / NX
TURN_Y = 2.0 * math.pi / NY
time_step = 0.04
gravity = 9.81
spread = 1.0 / math.sqrt(NX * NY)
zone_scale = 1.0 / math.sqrt(4096 * 128)
f32 = jnp.float32
bf16 = jnp.bfloat16


def part(value, which):
    return np.where(which == 0, np.real(value), np.imag(value))


def angles(ints, period):
    return 2.0 * np.pi * (np.asarray(ints) % period) / period


def pair(matrix):
    high = matrix.astype(np.float32).astype(ml_dtypes.bfloat16)
    low = (matrix - high.astype(np.float64)).astype(np.float32).astype(ml_dtypes.bfloat16)
    return np.stack([high, low])


def circle(phase):
    return np.stack([np.cos(phase), np.sin(phase)]).astype(np.float32)


@functools.cache
def tables():
    out = {}
    k256 = np.arange(256)
    phase = angles(k256[:, None] * k256[None, :], 256)
    out["turn"] = pair(np.concatenate([np.cos(phase), np.sin(phase)], 1))
    row = np.arange(64)
    i, a, jj = row // 16, row // 8 % 2, row % 8
    col = np.arange(128)
    n, ca, cj = col // 16, col // 8 % 2, col % 8
    base = np.exp(1j * angles(i[:, None] * n[None, :], 8)) * (1j ** ca)[None, :]
    same = jj[:, None] == cj[None, :]
    halves = [np.where(same, part(base * s, a[:, None]), 0.0) for s in (1j, -1, 1, 1j)]
    out["rows_mix"] = pair(np.concatenate(halves, 0))
    x0 = 4 * np.arange(2)[:, None] + np.arange(64)[None, :] // 16
    out["rows_turn"] = circle(angles(x0[:, :, None] * k256, NX))
    lane = np.arange(128)
    out["y_turn"] = circle(angles(k256[:, None] * (lane % 8)[None, :], NY))
    y0 = np.arange(8)
    turn = np.exp(1j * angles((lane % 8)[:, None] * y0[None, :], 8)) * spread
    gather = np.zeros((2, 128, 4, 128))
    gather_lift = np.zeros((128, 128))
    for k in range(128):
        f, i = k // 32, k // 8 % 4
        gather[0, k, f, y0 * 4 + i] = turn[k].real
        gather[1, k, f, y0 * 4 + i] = -turn[k].imag
        if k < 64:
            gather_lift[k, y0 * 4 + i] = turn[k].real if k < 32 else -turn[k].imag
    gather = np.concatenate([gather.reshape(256, 512), np.zeros((256, 128))], 1)
    gather[:128, 512:] = gather_lift
    out["gather"] = pair(gather)
    deal = np.zeros((2, 128, 2, 128))
    for k in range(128):
        f, a, i, jj = k // 64, k // 32 % 2, k // 8 % 4, k % 8
        turn = np.exp(-1j * angles(jj * y0, 8))
        deal[f, y0 * 4 + i, 0, k] = part(turn, a)
        deal[f, y0 * 4 + i, 1, k] = part(-1j * turn, a)
    out["deal"] = pair(deal.reshape(256, 256))
    x0 = 4 * np.arange(2)[:, None] + np.arange(32)[None, :] // 8
    out["main_turn"] = circle(angles(x0[:, :, None] * k256, NX))
    cell = np.arange(128) // 8
    out["zone_turn"] = circle(angles(cell[:, None] * k256, FINE))
    row = np.arange(256)
    n, of, oa, oj = row // 32, row // 16 % 2, row // 8 % 2, row % 8
    col = np.arange(128)
    f, a, i, jj = col // 64, col // 32 % 2, col // 8 % 4, col % 8
    turn = np.exp(-1j * angles(n[:, None] * i[None, :], 8)) * (1j ** a)[None, :]
    same = (of[:, None] == f[None, :]) & (oj[:, None] == jj[None, :])
    halves = [np.where(same, part(turn * s, oa[:, None]), 0.0) for s in (1, -1j)]
    out["main_mix"] = pair(np.concatenate(halves, 1))
    row = np.arange(128)
    n, oa, oj = row // 16, row // 8 % 2, row % 8
    a, p, jj = np.arange(256) // 128, np.arange(256) // 8 % 16, np.arange(256) % 8
    signed = np.where(n < 4, n, n - 8)
    turn = np.exp(-1j * angles(signed[:, None] * p[None, :], 16)) * (1j ** a)[None, :]
    same = oj[:, None] == jj[None, :]
    halves = [np.where(same, part(turn * s, oa[:, None]), 0.0) for s in (1, -1j)]
    out["zone_mix"] = pair(np.concatenate(halves, 1))
    return out


def split(value):
    high = value.astype(bf16)
    return high, (value - high.astype(f32)).astype(bf16)


def dot(left, right, dims=((1,), (0,))):
    return lax.dot_general(left, right, (dims, ((), ())), preferred_element_type=f32)


def dot3(left, right, dims=((1,), (0,))):
    along = dims[0][0], dims[1][0]
    left = jnp.concatenate([left[0], left[0], left[1]], along[0])
    right = jnp.concatenate([right[0], right[1], right[0]], along[1])
    return dot(left, right, dims)


def iota(shape, dim):
    return lax.broadcasted_iota(jnp.int32, shape, dim)


def cos_of(phase):
    moved = phase + 512
    quarter = (moved >> 10) & 3
    angle = ((moved & 1023) - 512).astype(f32) * (2.0 * math.pi / FINE)
    square = angle * angle
    cosine = 1.0 + square * (-0.5 + square * (1.0 / 24 + square * (-1.0 / 720 + square * (1.0 / 40320))))
    sine = angle * (
        1.0 + square * (-1.0 / 6 + square * (1.0 / 120 + square * (-1.0 / 5040 + square * (1.0 / 362880))))
    )
    size = jnp.where((quarter & 1) == 0, cosine, sine)
    return jnp.where((quarter == 1) | (quarter == 2), -size, size)


def wave_of(index):
    return jnp.where(index < 1024, index, index - 2048).astype(f32)


def deal_kernel(eta, phi, out):
    for z in range(4):
        for source, base in ((eta, 0), (phi, 16)):
            for a in range(2):
                rows = source[a, 8 * z : 8 * z + 8, :]
                for c in range(2):
                    out[4 * c + z, base + 8 * a : base + 8 * a + 8, :] = rows


def source_kernel(place, offsets, zone, out, places, beyond):
    tile = place[0]
    core = place[2]
    own = 4 * core + place[1]
    ox = offsets[tile, 0]
    oy = offsets[tile, 1]
    lane = iota((128, 128), 1)
    wanted = (16 * own + (lane >> 3) - 2 * (ox & 7)) & 127
    pick = jnp.where(iota((128, 128), 0) == wanted, 1.0, 0.0).astype(bf16)
    high, low = split(zone[...] * zone_scale)
    cells = dot(high, pick) + dot(low, pick)
    phase = (iota((64, 128), 1) & 7) * (2 * oy + iota((64, 128), 0))
    real = cells * cos_of(phase)
    imag = cells * cos_of(phase + 1024)
    right = jnp.concatenate(
        [jnp.concatenate([real, imag], 1), jnp.concatenate([-imag, real], 1)], 0
    )
    lane = iota((256, 128), 1)
    g = iota((256, 128), 0)
    g = jnp.where(g < 128, g, g - 256)
    left = cos_of(8 * g * (2 * oy + (lane & 63)) + jnp.where(lane < 64, 0, 1024))
    out[...] = dot3(split(left), split(right))
    row = iota((16, 256), 0)
    spot = iota((16, 256), 1)
    edge = jnp.zeros((8, 256), jnp.int32)
    tile_of = iota((8, 256), 1) >> 2
    for t in range(0, 64, 4):
        target = jnp.zeros((16, 256), jnp.int32)
        for k in range(4):
            x = offsets[t + k, 0]
            target = jnp.where((row >> 2) == k, x >> 3, target)
            edge = jnp.where(tile_of == t + k, 2 * (x & 7), edge)
        near = (target + (row & 3) + 4 * core) & 255
        far = (target + 8) & 255
        places[4 * t : 4 * t + 16, :] = jnp.where(spot == near, 1.0, 0.0).astype(bf16)
        places[256 + 4 * t : 272 + 4 * t, :] = jnp.where(spot == far, 1.0, 0.0).astype(bf16)
    edge = jnp.where(((iota((8, 256), 1) & 3) == 0) & (core == 0), edge, 0)
    for p in range(16):
        beyond[8 * p : 8 * p + 8, :] = jnp.where(edge > p, 1.0, 0.0)


def rows_kernel(place, modes, mix, turn, circles, out):
    first_ky = 32 * place[0] + 8 * place[1]
    core = place[2]
    odd = 1.0 - 2.0 * core.astype(f32)
    wave_y = wave_of(first_ky + (iota((16, 256), 0) & 7)) * TURN_Y
    tiles = [[], [], [], [], []]
    for n in range(8):
        wave_x = wave_of(256 * n + iota((16, 256), 1)) * TURN_X
        kappa = jnp.sqrt(wave_x * wave_x + wave_y * wave_y)
        block = 4 * (n % 2) + n // 2
        eta = modes[block, 0:16, :]
        phi = modes[block, 16:32, :]
        if n % 2:
            eta = eta * odd
            phi = phi * odd
        terms = (wave_x * eta, wave_y * eta, wave_x * phi, wave_y * phi, kappa * phi)
        for f in range(5):
            tiles[f].append(terms[f])
    cosine = turn[0, core]
    sine = turn[1, core]
    parts = [[], []]
    for f in range(5):
        rows = split(jnp.concatenate(tiles[f], 0))
        kind = slice(0, 128) if f < 4 else slice(128, 256)
        both = dot3((mix[0, kind], mix[1, kind]), rows)
        first = both[:64]
        second = both[64:]
        turned = (first * cosine + second * sine).reshape(4, 2, 8, 256)
        quarter = (second * cosine - first * sine).reshape(4, 2, 8, 256)
        for a in range(2):
            parts[a].append(
                jnp.concatenate(
                    [turned[:, a].reshape(32, 256), quarter[:, a].reshape(32, 256)], 1
                )
            )
    real, imag = parts
    words = real[:4] + imag[:4] + [real[4], imag[4], -imag[4], real[4]]
    result = dot3(circles, split(jnp.concatenate(words, 0)), ((1,), (1,)))
    for q in range(3):
        out[pl.ds(q, 256, stride=3), :] = result[:, 128 * q : 128 * q + 128]


def columns_kernel(terms, source, circles, turn, gather, deal, out):
    words = split(
        jnp.concatenate([terms[pl.ds(q, 256, stride=3), :] for q in range(3)], 1)
    )
    with_cos = dot3((circles[0, :, :256], circles[1, :, :256]), words)
    with_sin = dot3((circles[0, :, 256:], circles[1, :, 256:]), words)
    real = with_cos[:, :128] - with_sin[:, 128:256]
    imag = with_sin[:, :128] + with_cos[:, 128:256]
    lane = iota((256, 128), 1)
    rolled = pltpu.roll(with_sin[:, 256:], 64, 1)
    lift = with_cos[:, 256:] + jnp.where(lane < 64, rolled, -rolled)
    cosine = turn[0]
    sine = turn[1]
    slopes = split(
        jnp.concatenate([real * cosine - imag * sine, real * sine + imag * cosine], 1)
    )
    lift = split(lift * cosine + pltpu.roll(lift, 64, 1) * sine)
    fields = dot3(slopes, (gather[0, :, :512], gather[1, :, :512]))
    lift = dot3(lift, (gather[0, :128, 512:], gather[1, :128, 512:]))
    slope_ex, slope_ey, slope_px, slope_py = (
        fields[:, 128 * k : 128 * k + 128] for k in range(4)
    )
    first_order = lift * (slope_ex * slope_ex + slope_ey * slope_ey) - (
        slope_px * slope_ex + slope_py * slope_ey
    )
    second_term = 0.5 * (lift * lift - slope_px * slope_px - slope_py * slope_py)
    products = jnp.concatenate([first_order, second_term], 1) * (time_step * spread)
    both = dot3(split(products), deal)
    first = both[:, :128]
    second = both[:, 128:]
    turned = jnp.concatenate([first * cosine + second * sine, second * cosine - first * sine], 0)
    out[pl.ds(0, 256, stride=3), :] = dot3(circles, split(turned))
    out[pl.ds(1, 256, stride=3), :] = source[:, :128]
    out[pl.ds(2, 256, stride=3), :] = source[:, 128:]


def rows_back_kernel(
    place, terms, places, beyond, circles, main_turn, zone_turn, main_mix, zone_mix, out
):
    core = place[2]
    cells = jnp.concatenate(
        [terms[pl.ds(1, 256, stride=3), :], terms[pl.ds(2, 256, stride=3), :]], 1
    ).T
    far = cells * jnp.concatenate([beyond[...], beyond[...]], 0)
    cells = jnp.concatenate(split(jnp.concatenate([cells - far, far], 1)), 1)
    grid = dot(cells, jnp.concatenate([places[...], places[...]], 0))
    main = terms[pl.ds(0, 256, stride=3), :].T
    both = dot3(split(jnp.concatenate([main, grid], 0)), circles)

    def turned(lines, cosine, sine):
        with_cos = lines[:, :, :256]
        with_sin = lines[:, :, 256:]
        real = with_cos * cosine - with_sin * sine
        imag = with_cos * sine + with_sin * cosine
        count = lines.shape[0] * lines.shape[1]
        return split(
            jnp.concatenate([real.reshape(count, 256), imag.reshape(count, 256)], 0)
        )

    main = turned(both[:128].reshape(4, 32, 512), main_turn[0, core][None], main_turn[1, core][None])
    zone = turned(both[128:].reshape(2, 128, 512), zone_turn[0][None], zone_turn[1][None])
    main = dot3(main_mix, main)
    zone = dot3(zone_mix, zone)
    odd = 1.0 - 2.0 * core.astype(f32)
    for n in range(8):
        block = main[32 * n : 32 * n + 32]
        if n % 2:
            block = block * odd
        where = 4 * (n % 2) + n // 2
        out[where, 0:16, :] = block[:16] + zone[16 * n : 16 * n + 16]
        out[where, 16:32, :] = block[16:]


def finish_kernel(place, terms, eta, phi, eta_next, phi_next):
    for z in range(4):
        rows = slice(8 * z, 8 * z + 8)
        wave_x = wave_of(256 * (2 * place[1] + place[2]) + iota((8, 256), 1)) * TURN_X
        wave_y = wave_of(32 * place[0] + 8 * z + iota((8, 256), 0)) * TURN_Y
        kappa = time_step * jnp.sqrt(wave_x * wave_x + wave_y * wave_y)
        for a in range(2):
            surface = eta[a, rows, :]
            potential = phi[a, rows, :]
            part_of = slice(8 * a, 8 * a + 8)
            added = terms[z, part_of, :] + terms[4 + z, part_of, :]
            eta_next[a, rows, :] = surface + kappa * potential + added
            part_of = slice(16 + 8 * a, 24 + 8 * a)
            added = terms[z, part_of, :] + terms[4 + z, part_of, :]
            phi_next[a, rows, :] = potential - (time_step * gravity) * surface + added


def call(kernel, shapes, scalars, arrays, flops=0, limit=24, types=None):
    single = isinstance(shapes, tuple)
    shapes = [shapes] if single else shapes
    types = [f32] * len(shapes) if types is None else types
    vmem = pl.BlockSpec(memory_space=pltpu.VMEM)
    smem = pl.BlockSpec(memory_space=pltpu.SMEM)
    moved = sum(4 * math.prod(s) for s in shapes) + sum(x.size * x.dtype.itemsize for x in arrays)
    result = pl.pallas_call(
        kernel,
        out_shape=[jax.ShapeDtypeStruct(s, t) for s, t in zip(shapes, types)],
        in_specs=[smem] * len(scalars) + [vmem] * len(arrays),
        out_specs=[vmem] * len(shapes),
        compiler_params=pltpu.CompilerParams(vmem_limit_bytes=limit * 1024 * 1024),
        cost_estimate=pl.CostEstimate(flops=flops, bytes_accessed=moved, transcendentals=0),
        name=kernel.__name__,
    )(*scalars, *arrays)
    return result[0] if single else result


def stage_deal(eta, phi):
    return call(deal_kernel, (8, 32, 256), [], [eta, phi], limit=56, flops=2**33)


def stage_source(place, offsets, zone):
    shapes = [(256, 256), (512, 256), (128, 256)]
    types = [f32, bf16, f32]
    return call(source_kernel, shapes, [place, offsets], [zone], flops=2**26, types=types)


def stage_rows(place, modes):
    t = tables()
    arrays = [modes, t["rows_mix"], t["rows_turn"], t["turn"]]
    return call(rows_kernel, (768, 128), [place], arrays, flops=2**30)


def stage_columns(terms, source):
    t = tables()
    arrays = [terms, source, t["turn"], t["y_turn"], t["gather"], t["deal"]]
    return call(columns_kernel, (768, 128), [], arrays, flops=2**30)


def stage_rows_back(place, terms, places, beyond):
    t = tables()
    arrays = [terms, places, beyond, t["turn"], t["main_turn"], t["zone_turn"]]
    arrays += [t["main_mix"], t["zone_mix"]]
    return call(rows_back_kernel, (8, 32, 256), [place], arrays, flops=2**29)


def stage_finish(place, terms, eta, phi):
    return call(finish_kernel, [(2, 32, 256)] * 2, [place], [terms, eta, phi])


def local(eta_modes, phi_modes, zone_field, offsets):
    place = jnp.stack([lax.axis_index(axis) for axis in ("wide", "lane", "core")]).astype(jnp.int32)
    swap = functools.partial(lax.all_to_all, split_axis=0, concat_axis=0, tiled=True)

    def turn(words):
        return swap(words.reshape(256, 1, 384), ("wide", "lane")).reshape(768, 128)

    modes = swap(stage_deal(eta_modes, phi_modes), ("core", "lane"))
    ready = stage_source(place, offsets, zone_field)
    modes, (source, places, beyond) = lax.optimization_barrier((modes, ready))
    columns = turn(stage_rows(place, modes))
    rows = turn(stage_columns(columns, source))
    terms = swap(stage_rows_back(place, rows, places, beyond), ("core", "lane"))
    return tuple(stage_finish(place, terms, eta_modes, phi_modes))


def solution(mesh):
    wide, narrow = mesh.devices.shape
    chips = Mesh(mesh.devices.reshape(wide, narrow // 2, 2), ("wide", "lane", "core"))
    modes = P(None, "wide", ("lane", "core"))
    in_specs = (modes, modes, P("wide", None), P())
    return jax.shard_map(
        local, mesh=chips, in_specs=in_specs, out_specs=(modes, modes), check_vma=False
    )
```

```python
import functools
import math

import jax
import jax.numpy as jnp
import ml_dtypes
import numpy as np
from jax import lax
from jax.experimental import pallas as pl
from jax.experimental.pallas import tpu as pltpu
from jax.sharding import Mesh
from jax.sharding import PartitionSpec as P

NX = 2048
NY = 2048
FINE = 4096
TURN_X = 2.0 * math.pi / NX
TURN_Y = 2.0 * math.pi / NY
time_step = 0.04
gravity = 9.81
spread = 1.0 / math.sqrt(NX * NY)
zone_scale = 1.0 / math.sqrt(4096 * 128)
f32 = jnp.float32
bf16 = jnp.bfloat16


def part(value, which):
    return np.where(which == 0, np.real(value), np.imag(value))


def angles(ints, period):
    return 2.0 * np.pi * (np.asarray(ints) % period) / period


def pair(matrix):
    high = matrix.astype(np.float32).astype(ml_dtypes.bfloat16)
    low = (matrix - high.astype(np.float64)).astype(np.float32).astype(ml_dtypes.bfloat16)
    return np.stack([high, low])


def circle(phase):
    return np.stack([np.cos(phase), np.sin(phase)]).astype(np.float32)


@functools.cache
def tables():
    out = {}
    k256 = np.arange(256)
    phase = angles(k256[:, None] * k256[None, :], 256)
    out["turn"] = pair(np.concatenate([np.cos(phase), np.sin(phase)], 1))
    row = np.arange(64)
    i, a, jj = row // 16, row // 8 % 2, row % 8
    col = np.arange(128)
    n, ca, cj = col // 16, col // 8 % 2, col % 8
    base = np.exp(1j * angles(i[:, None] * n[None, :], 8)) * (1j ** ca)[None, :]
    same = jj[:, None] == cj[None, :]
    halves = [np.where(same, part(base * s, a[:, None]), 0.0) for s in (1j, -1, 1, 1j)]
    out["rows_mix"] = pair(np.concatenate(halves, 0))
    x0 = 4 * np.arange(2)[:, None] + np.arange(64)[None, :] // 16
    out["rows_turn"] = circle(angles(x0[:, :, None] * k256, NX))
    lane = np.arange(128)
    out["y_turn"] = circle(angles(k256[:, None] * (lane % 8)[None, :], NY))
    y0 = np.arange(8)
    turn = np.exp(1j * angles((lane % 8)[:, None] * y0[None, :], 8)) * spread
    gather = np.zeros((2, 128, 4, 128))
    gather_lift = np.zeros((128, 128))
    for k in range(128):
        f, i = k // 32, k // 8 % 4
        gather[0, k, f, y0 * 4 + i] = turn[k].real
        gather[1, k, f, y0 * 4 + i] = -turn[k].imag
        if k < 64:
            gather_lift[k, y0 * 4 + i] = turn[k].real if k < 32 else -turn[k].imag
    gather = np.concatenate([gather.reshape(256, 512), np.zeros((256, 128))], 1)
    gather[:128, 512:] = gather_lift
    out["gather"] = pair(gather)
    deal = np.zeros((2, 128, 2, 128))
    for k in range(128):
        f, a, i, jj = k // 64, k // 32 % 2, k // 8 % 4, k % 8
        turn = np.exp(-1j * angles(jj * y0, 8))
        deal[f, y0 * 4 + i, 0, k] = part(turn, a)
        deal[f, y0 * 4 + i, 1, k] = part(-1j * turn, a)
    out["deal"] = pair(deal.reshape(256, 256))
    x0 = 4 * np.arange(2)[:, None] + np.arange(32)[None, :] // 8
    out["main_turn"] = circle(angles(x0[:, :, None] * k256, NX))
    cell = np.arange(128) // 8
    out["zone_turn"] = circle(angles(cell[:, None] * k256, FINE))
    row = np.arange(256)
    n, of, oa, oj = row // 32, row // 16 % 2, row // 8 % 2, row % 8
    col = np.arange(128)
    f, a, i, jj = col // 64, col // 32 % 2, col // 8 % 4, col % 8
    turn = np.exp(-1j * angles(n[:, None] * i[None, :], 8)) * (1j ** a)[None, :]
    same = (of[:, None] == f[None, :]) & (oj[:, None] == jj[None, :])
    halves = [np.where(same, part(turn * s, oa[:, None]), 0.0) for s in (1, -1j)]
    out["main_mix"] = pair(np.concatenate(halves, 1))
    row = np.arange(128)
    n, oa, oj = row // 16, row // 8 % 2, row % 8
    a, p, jj = np.arange(256) // 128, np.arange(256) // 8 % 16, np.arange(256) % 8
    signed = np.where(n < 4, n, n - 8)
    turn = np.exp(-1j * angles(signed[:, None] * p[None, :], 16)) * (1j ** a)[None, :]
    same = oj[:, None] == jj[None, :]
    halves = [np.where(same, part(turn * s, oa[:, None]), 0.0) for s in (1, -1j)]
    out["zone_mix"] = pair(np.concatenate(halves, 1))
    return out


def split(value):
    high = value.astype(bf16)
    return high, (value - high.astype(f32)).astype(bf16)


def dot(left, right, dims=((1,), (0,))):
    return lax.dot_general(left, right, (dims, ((), ())), preferred_element_type=f32)


def dot3(left, right, dims=((1,), (0,))):
    along = dims[0][0], dims[1][0]
    left = jnp.concatenate([left[0], left[0], left[1]], along[0])
    right = jnp.concatenate([right[0], right[1], right[0]], along[1])
    return dot(left, right, dims)


def iota(shape, dim):
    return lax.broadcasted_iota(jnp.int32, shape, dim)


def cos_of(phase):
    moved = phase + 512
    quarter = (moved >> 10) & 3
    angle = ((moved & 1023) - 512).astype(f32) * (2.0 * math.pi / FINE)
    square = angle * angle
    cosine = 1.0 + square * (-0.5 + square * (1.0 / 24 + square * (-1.0 / 720 + square * (1.0 / 40320))))
    sine = angle * (
        1.0 + square * (-1.0 / 6 + square * (1.0 / 120 + square * (-1.0 / 5040 + square * (1.0 / 362880))))
    )
    size = jnp.where((quarter & 1) == 0, cosine, sine)
    return jnp.where((quarter == 1) | (quarter == 2), -size, size)


def wave_of(index):
    return jnp.where(index < 1024, index, index - 2048).astype(f32)


def deal_kernel(eta, phi, out):
    for z in range(4):
        for source, base in ((eta, 0), (phi, 16)):
            for a in range(2):
                rows = source[a, 8 * z : 8 * z + 8, :]
                for c in range(2):
                    out[4 * c + z, base + 8 * a : base + 8 * a + 8, :] = rows


def source_kernel(place, offsets, zone, out, places, beyond):
    tile = place[0]
    core = place[2]
    own = 4 * core + place[1]
    ox = offsets[tile, 0]
    oy = offsets[tile, 1]
    lane = iota((128, 128), 1)
    wanted = (16 * own + (lane >> 3) - 2 * (ox & 7)) & 127
    pick = jnp.where(iota((128, 128), 0) == wanted, 1.0, 0.0).astype(bf16)
    high, low = split(zone[...] * zone_scale)
    cells = dot(high, pick) + dot(low, pick)
    phase = (iota((64, 128), 1) & 7) * (2 * oy + iota((64, 128), 0))
    real = cells * cos_of(phase)
    imag = cells * cos_of(phase + 1024)
    right = jnp.concatenate(
        [jnp.concatenate([real, imag], 1), jnp.concatenate([-imag, real], 1)], 0
    )
    lane = iota((256, 128), 1)
    g = iota((256, 128), 0)
    g = jnp.where(g < 128, g, g - 256)
    left = cos_of(8 * g * (2 * oy + (lane & 63)) + jnp.where(lane < 64, 0, 1024))
    out[...] = dot3(split(left), split(right))
    row = iota((16, 256), 0)
    spot = iota((16, 256), 1)
    edge = jnp.zeros((8, 256), jnp.int32)
    tile_of = iota((8, 256), 1) >> 2
    for t in range(0, 64, 4):
        target = jnp.zeros((16, 256), jnp.int32)
        for k in range(4):
            x = offsets[t + k, 0]
            target = jnp.where((row >> 2) == k, x >> 3, target)
            edge = jnp.where(tile_of == t + k, 2 * (x & 7), edge)
        near = (target + (row & 3) + 4 * core) & 255
        far = (target + 8) & 255
        places[4 * t : 4 * t + 16, :] = jnp.where(spot == near, 1.0, 0.0).astype(bf16)
        places[256 + 4 * t : 272 + 4 * t, :] = jnp.where(spot == far, 1.0, 0.0).astype(bf16)
    edge = jnp.where(((iota((8, 256), 1) & 3) == 0) & (core == 0), edge, 0)
    for p in range(16):
        beyond[8 * p : 8 * p + 8, :] = jnp.where(edge > p, 1.0, 0.0)


def rows_kernel(place, modes, mix, turn, circles, out):
    first_ky = 32 * place[0] + 8 * place[1]
    core = place[2]
    odd = 1.0 - 2.0 * core.astype(f32)
    wave_y = wave_of(first_ky + (iota((16, 256), 0) & 7)) * TURN_Y
    tiles = [[], [], [], [], []]
    for n in range(8):
        wave_x = wave_of(256 * n + iota((16, 256), 1)) * TURN_X
        kappa = jnp.sqrt(wave_x * wave_x + wave_y * wave_y)
        block = 4 * (n % 2) + n // 2
        eta = modes[block, 0:16, :]
        phi = modes[block, 16:32, :]
        if n % 2:
            eta = eta * odd
            phi = phi * odd
        terms = (wave_x * eta, wave_y * eta, wave_x * phi, wave_y * phi, kappa * phi)
        for f in range(5):
            tiles[f].append(terms[f])
    cosine = turn[0, core]
    sine = turn[1, core]
    parts = [[], []]
    for f in range(5):
        rows = split(jnp.concatenate(tiles[f], 0))
        kind = slice(0, 128) if f < 4 else slice(128, 256)
        both = dot3((mix[0, kind], mix[1, kind]), rows)
        first = both[:64]
        second = both[64:]
        turned = (first * cosine + second * sine).reshape(4, 2, 8, 256)
        quarter = (second * cosine - first * sine).reshape(4, 2, 8, 256)
        for a in range(2):
            parts[a].append(
                jnp.concatenate(
                    [turned[:, a].reshape(32, 256), quarter[:, a].reshape(32, 256)], 1
                )
            )
    real, imag = parts
    words = real[:4] + imag[:4] + [real[4], imag[4], -imag[4], real[4]]
    result = dot3(circles, split(jnp.concatenate(words, 0)), ((1,), (1,)))
    for q in range(3):
        out[pl.ds(q, 256, stride=3), :] = result[:, 128 * q : 128 * q + 128]


def columns_kernel(terms, source, circles, turn, gather, deal, out):
    words = split(
        jnp.concatenate([terms[pl.ds(q, 256, stride=3), :] for q in range(3)], 1)
    )
    with_cos = dot3((circles[0, :, :256], circles[1, :, :256]), words)
    with_sin = dot3((circles[0, :, 256:], circles[1, :, 256:]), words)
    real = with_cos[:, :128] - with_sin[:, 128:256]
    imag = with_sin[:, :128] + with_cos[:, 128:256]
    lane = iota((256, 128), 1)
    rolled = pltpu.roll(with_sin[:, 256:], 64, 1)
    lift = with_cos[:, 256:] + jnp.where(lane < 64, rolled, -rolled)
    cosine = turn[0]
    sine = turn[1]
    slopes = split(
        jnp.concatenate([real * cosine - imag * sine, real * sine + imag * cosine], 1)
    )
    lift = split(lift * cosine + pltpu.roll(lift, 64, 1) * sine)
    fields = dot3(slopes, (gather[0, :, :512], gather[1, :, :512]))
    lift = dot3(lift, (gather[0, :128, 512:], gather[1, :128, 512:]))
    slope_ex, slope_ey, slope_px, slope_py = (
        fields[:, 128 * k : 128 * k + 128] for k in range(4)
    )
    first_order = lift * (slope_ex * slope_ex + slope_ey * slope_ey) - (
        slope_px * slope_ex + slope_py * slope_ey
    )
    second_term = 0.5 * (lift * lift - slope_px * slope_px - slope_py * slope_py)
    products = jnp.concatenate([first_order, second_term], 1) * (time_step * spread)
    both = dot3(split(products), deal)
    first = both[:, :128]
    second = both[:, 128:]
    turned = jnp.concatenate([first * cosine + second * sine, second * cosine - first * sine], 0)
    out[pl.ds(0, 256, stride=3), :] = dot3(circles, split(turned))
    out[pl.ds(1, 256, stride=3), :] = source[:, :128]
    out[pl.ds(2, 256, stride=3), :] = source[:, 128:]


def rows_back_kernel(
    place, terms, places, beyond, circles, main_turn, zone_turn, main_mix, zone_mix, out
):
    core = place[2]
    cells = jnp.concatenate(
        [terms[pl.ds(1, 256, stride=3), :], terms[pl.ds(2, 256, stride=3), :]], 1
    ).T
    far = cells * jnp.concatenate([beyond[...], beyond[...]], 0)
    cells = jnp.concatenate(split(jnp.concatenate([cells - far, far], 1)), 1)
    grid = dot(cells, jnp.concatenate([places[...], places[...]], 0))
    main = terms[pl.ds(0, 256, stride=3), :].T
    both = dot3(split(jnp.concatenate([main, grid], 0)), circles)

    def turned(lines, cosine, sine):
        with_cos = lines[:, :, :256]
        with_sin = lines[:, :, 256:]
        real = with_cos * cosine - with_sin * sine
        imag = with_cos * sine + with_sin * cosine
        count = lines.shape[0] * lines.shape[1]
        return split(
            jnp.concatenate([real.reshape(count, 256), imag.reshape(count, 256)], 0)
        )

    main = turned(both[:128].reshape(4, 32, 512), main_turn[0, core][None], main_turn[1, core][None])
    zone = turned(both[128:].reshape(2, 128, 512), zone_turn[0][None], zone_turn[1][None])
    main = dot3(main_mix, main)
    zone = dot3(zone_mix, zone)
    odd = 1.0 - 2.0 * core.astype(f32)
    for n in range(8):
        block = main[32 * n : 32 * n + 32]
        if n % 2:
            block = block * odd
        where = 4 * (n % 2) + n // 2
        out[where, 0:16, :] = block[:16] + zone[16 * n : 16 * n + 16]
        out[where, 16:32, :] = block[16:]


def finish_kernel(place, terms, eta, phi, eta_next, phi_next):
    for z in range(4):
        rows = slice(8 * z, 8 * z + 8)
        wave_x = wave_of(256 * (2 * place[1] + place[2]) + iota((8, 256), 1)) * TURN_X
        wave_y = wave_of(32 * place[0] + 8 * z + iota((8, 256), 0)) * TURN_Y
        kappa = time_step * jnp.sqrt(wave_x * wave_x + wave_y * wave_y)
        for a in range(2):
            surface = eta[a, rows, :]
            potential = phi[a, rows, :]
            part_of = slice(8 * a, 8 * a + 8)
            added = terms[z, part_of, :] + terms[4 + z, part_of, :]
            eta_next[a, rows, :] = surface + kappa * potential + added
            part_of = slice(16 + 8 * a, 24 + 8 * a)
            added = terms[z, part_of, :] + terms[4 + z, part_of, :]
            phi_next[a, rows, :] = potential - (time_step * gravity) * surface + added


def call(kernel, shapes, scalars, arrays, flops=0, limit=24, types=None):
    single = isinstance(shapes, tuple)
    shapes = [shapes] if single else shapes
    types = [f32] * len(shapes) if types is None else types
    vmem = pl.BlockSpec(memory_space=pltpu.VMEM)
    smem = pl.BlockSpec(memory_space=pltpu.SMEM)
    moved = sum(4 * math.prod(s) for s in shapes) + sum(x.size * x.dtype.itemsize for x in arrays)
    result = pl.pallas_call(
        kernel,
        out_shape=[jax.ShapeDtypeStruct(s, t) for s, t in zip(shapes, types)],
        in_specs=[smem] * len(scalars) + [vmem] * len(arrays),
        out_specs=[vmem] * len(shapes),
        compiler_params=pltpu.CompilerParams(vmem_limit_bytes=limit * 1024 * 1024),
        cost_estimate=pl.CostEstimate(flops=flops, bytes_accessed=moved, transcendentals=0),
        name=kernel.__name__,
    )(*scalars, *arrays)
    return result[0] if single else result


def stage_deal(eta, phi):
    return call(deal_kernel, (8, 32, 256), [], [eta, phi], limit=56, flops=2**33)


def stage_source(place, offsets, zone):
    shapes = [(256, 256), (512, 256), (128, 256)]
    types = [f32, bf16, f32]
    return call(source_kernel, shapes, [place, offsets], [zone], flops=2**26, types=types)


def stage_rows(place, modes):
    t = tables()
    arrays = [modes, t["rows_mix"], t["rows_turn"], t["turn"]]
    return call(rows_kernel, (768, 128), [place], arrays, flops=2**30)


def stage_columns(terms, source):
    t = tables()
    arrays = [terms, source, t["turn"], t["y_turn"], t["gather"], t["deal"]]
    return call(columns_kernel, (768, 128), [], arrays, flops=2**30)


def stage_rows_back(place, terms, places, beyond):
    t = tables()
    arrays = [terms, places, beyond, t["turn"], t["main_turn"], t["zone_turn"]]
    arrays += [t["main_mix"], t["zone_mix"]]
    return call(rows_back_kernel, (8, 32, 256), [place], arrays, flops=2**29)


def stage_finish(place, terms, eta, phi):
    return call(finish_kernel, [(2, 32, 256)] * 2, [place], [terms, eta, phi])


def local(eta_modes, phi_modes, zone_field, offsets):
    place = jnp.stack([lax.axis_index(axis) for axis in ("wide", "lane", "core")]).astype(jnp.int32)
    swap = functools.partial(lax.all_to_all, split_axis=0, concat_axis=0, tiled=True)

    def turn(words):
        return swap(words.reshape(256, 3, 1, 128), ("wide", "lane")).reshape(768, 128)

    modes = swap(stage_deal(eta_modes, phi_modes), ("core", "lane"))
    ready = stage_source(place, offsets, zone_field)
    modes, (source, places, beyond) = lax.optimization_barrier((modes, ready))
    columns = turn(stage_rows(place, modes))
    rows = turn(stage_columns(columns, source))
    terms = swap(stage_rows_back(place, rows, places, beyond), ("core", "lane"))
    return tuple(stage_finish(place, terms, eta_modes, phi_modes))


def solution(mesh):
    wide, narrow = mesh.devices.shape
    chips = Mesh(mesh.devices.reshape(wide, narrow // 2, 2), ("wide", "lane", "core"))
    modes = P(None, "wide", ("lane", "core"))
    in_specs = (modes, modes, P("wide", None), P())
    return jax.shard_map(
        local, mesh=chips, in_specs=in_specs, out_specs=(modes, modes), check_vma=False
    )
```

```python
import functools
import math

import jax
import jax.numpy as jnp
import ml_dtypes
import numpy as np
from jax import lax
from jax.experimental import pallas as pl
from jax.experimental.pallas import tpu as pltpu
from jax.sharding import Mesh
from jax.sharding import PartitionSpec as P

NX = 2048
NY = 2048
FINE = 4096
TURN_X = 2.0 * math.pi / NX
TURN_Y = 2.0 * math.pi / NY
time_step = 0.04
gravity = 9.81
spread = 1.0 / math.sqrt(NX * NY)
zone_scale = 1.0 / math.sqrt(4096 * 128)
f32 = jnp.float32
bf16 = jnp.bfloat16


def part(value, which):
    return np.where(which == 0, np.real(value), np.imag(value))


def angles(ints, period):
    return 2.0 * np.pi * (np.asarray(ints) % period) / period


def pair(matrix):
    high = matrix.astype(np.float32).astype(ml_dtypes.bfloat16)
    low = (matrix - high.astype(np.float64)).astype(np.float32).astype(ml_dtypes.bfloat16)
    return np.stack([high, low])


def circle(phase):
    return np.stack([np.cos(phase), np.sin(phase)]).astype(np.float32)


@functools.cache
def tables():
    out = {}
    k256 = np.arange(256)
    phase = angles(k256[:, None] * k256[None, :], 256)
    out["turn"] = pair(np.concatenate([np.cos(phase), np.sin(phase)], 1))
    row = np.arange(64)
    i, a, jj = row // 16, row // 8 % 2, row % 8
    col = np.arange(128)
    n, ca, cj = col // 16, col // 8 % 2, col % 8
    base = np.exp(1j * angles(i[:, None] * n[None, :], 8)) * (1j ** ca)[None, :]
    same = jj[:, None] == cj[None, :]
    halves = [np.where(same, part(base * s, a[:, None]), 0.0) for s in (1j, -1, 1, 1j)]
    out["rows_mix"] = pair(np.concatenate(halves, 0))
    x0 = 4 * np.arange(2)[:, None] + np.arange(64)[None, :] // 16
    out["rows_turn"] = circle(angles(x0[:, :, None] * k256, NX))
    lane = np.arange(128)
    out["y_turn"] = circle(angles(k256[:, None] * (lane % 8)[None, :], NY))
    y0 = np.arange(8)
    turn = np.exp(1j * angles((lane % 8)[:, None] * y0[None, :], 8)) * spread
    gather = np.zeros((2, 128, 4, 128))
    gather_lift = np.zeros((128, 128))
    for k in range(128):
        f, i = k // 32, k // 8 % 4
        gather[0, k, f, y0 * 4 + i] = turn[k].real
        gather[1, k, f, y0 * 4 + i] = -turn[k].imag
        if k < 64:
            gather_lift[k, y0 * 4 + i] = turn[k].real if k < 32 else -turn[k].imag
    gather = np.concatenate([gather.reshape(256, 512), np.zeros((256, 128))], 1)
    gather[:128, 512:] = gather_lift
    out["gather"] = pair(gather)
    deal = np.zeros((2, 128, 2, 128))
    for k in range(128):
        f, a, i, jj = k // 64, k // 32 % 2, k // 8 % 4, k % 8
        turn = np.exp(-1j * angles(jj * y0, 8))
        deal[f, y0 * 4 + i, 0, k] = part(turn, a)
        deal[f, y0 * 4 + i, 1, k] = part(-1j * turn, a)
    out["deal"] = pair(deal.reshape(256, 256))
    x0 = 4 * np.arange(2)[:, None] + np.arange(32)[None, :] // 8
    out["main_turn"] = circle(angles(x0[:, :, None] * k256, NX))
    cell = np.arange(128) // 8
    out["zone_turn"] = circle(angles(cell[:, None] * k256, FINE))
    row = np.arange(256)
    n, of, oa, oj = row // 32, row // 16 % 2, row // 8 % 2, row % 8
    col = np.arange(128)
    f, a, i, jj = col // 64, col // 32 % 2, col // 8 % 4, col % 8
    turn = np.exp(-1j * angles(n[:, None] * i[None, :], 8)) * (1j ** a)[None, :]
    same = (of[:, None] == f[None, :]) & (oj[:, None] == jj[None, :])
    halves = [np.where(same, part(turn * s, oa[:, None]), 0.0) for s in (1, -1j)]
    out["main_mix"] = pair(np.concatenate(halves, 1))
    row = np.arange(128)
    n, oa, oj = row // 16, row // 8 % 2, row % 8
    a, p, jj = np.arange(256) // 128, np.arange(256) // 8 % 16, np.arange(256) % 8
    signed = np.where(n < 4, n, n - 8)
    turn = np.exp(-1j * angles(signed[:, None] * p[None, :], 16)) * (1j ** a)[None, :]
    same = oj[:, None] == jj[None, :]
    halves = [np.where(same, part(turn * s, oa[:, None]), 0.0) for s in (1, -1j)]
    out["zone_mix"] = pair(np.concatenate(halves, 1))
    return out


def split(value):
    high = value.astype(bf16)
    return high, (value - high.astype(f32)).astype(bf16)


def dot(left, right, dims=((1,), (0,))):
    return lax.dot_general(left, right, (dims, ((), ())), preferred_element_type=f32)


def dot3(left, right, dims=((1,), (0,))):
    along = dims[0][0], dims[1][0]
    left = jnp.concatenate([left[0], left[0], left[1]], along[0])
    right = jnp.concatenate([right[0], right[1], right[0]], along[1])
    return dot(left, right, dims)


def iota(shape, dim):
    return lax.broadcasted_iota(jnp.int32, shape, dim)


def cos_of(phase):
    moved = phase + 512
    quarter = (moved >> 10) & 3
    angle = ((moved & 1023) - 512).astype(f32) * (2.0 * math.pi / FINE)
    square = angle * angle
    cosine = 1.0 + square * (-0.5 + square * (1.0 / 24 + square * (-1.0 / 720 + square * (1.0 / 40320))))
    sine = angle * (
        1.0 + square * (-1.0 / 6 + square * (1.0 / 120 + square * (-1.0 / 5040 + square * (1.0 / 362880))))
    )
    size = jnp.where((quarter & 1) == 0, cosine, sine)
    return jnp.where((quarter == 1) | (quarter == 2), -size, size)


def wave_of(index):
    return jnp.where(index < 1024, index, index - 2048).astype(f32)


def order_of(n):
    return 4 * (n >> 1 & 1) + 2 * (n >> 2) + (n & 1)


def deal_kernel(eta, phi, out):
    for z in range(4):
        for source, base in ((eta, 0), (phi, 16)):
            for a in range(2):
                rows = source[a, 8 * z : 8 * z + 8, :]
                for c in range(2):
                    out[4 * c + z, base + 8 * a : base + 8 * a + 8, :] = rows


def source_kernel(place, offsets, zone, out, places, beyond):
    tile = place[0]
    half = place[2]
    own = 4 * half + place[1]
    ox = offsets[tile, 0]
    oy = offsets[tile, 1]
    lane = iota((128, 128), 1)
    wanted = (16 * own + (lane >> 3) - 2 * (ox & 7)) & 127
    pick = jnp.where(iota((128, 128), 0) == wanted, 1.0, 0.0).astype(bf16)
    high, low = split(zone[...] * zone_scale)
    cells = dot(high, pick) + dot(low, pick)
    phase = (iota((64, 128), 1) & 7) * (2 * oy + iota((64, 128), 0))
    real = cells * cos_of(phase)
    imag = cells * cos_of(phase + 1024)
    right = jnp.concatenate(
        [jnp.concatenate([real, imag], 1), jnp.concatenate([-imag, real], 1)], 0
    )
    lane = iota((256, 128), 1)
    g = iota((256, 128), 0)
    g = jnp.where(g < 128, g, g - 256)
    left = cos_of(8 * g * (2 * oy + (lane & 63)) + jnp.where(lane < 64, 0, 1024))
    out[...] = dot3(split(left), split(right))
    row = iota((16, 256), 0)
    spot = iota((16, 256), 1)
    edge = jnp.zeros((8, 256), jnp.int32)
    tile_of = iota((8, 256), 1) >> 2
    for t in range(0, 64, 4):
        target = jnp.zeros((16, 256), jnp.int32)
        for k in range(4):
            x = offsets[t + k, 0]
            target = jnp.where((row >> 2) == k, x >> 3, target)
            edge = jnp.where(tile_of == t + k, 2 * (x & 7), edge)
        near = (target + (row & 3) + 4 * half) & 255
        far = (target + 8) & 255
        places[4 * t : 4 * t + 16, :] = jnp.where(spot == near, 1.0, 0.0).astype(bf16)
        places[256 + 4 * t : 272 + 4 * t, :] = jnp.where(spot == far, 1.0, 0.0).astype(bf16)
    edge = jnp.where(((iota((8, 256), 1) & 3) == 0) & (half == 0), edge, 0)
    for p in range(16):
        beyond[8 * p : 8 * p + 8, :] = jnp.where(edge > p, 1.0, 0.0)


def rows_kernel(place, modes, mix, turn, circles, out):
    first_ky = 32 * place[0] + 8 * place[1]
    half = place[2]
    odd = 1.0 - 2.0 * half.astype(f32)
    wave_y = wave_of(first_ky + (iota((16, 256), 0) & 7)) * TURN_Y
    tiles = [[], [], [], [], []]
    for n in range(8):
        wave_x = wave_of(256 * n + iota((16, 256), 1)) * TURN_X
        kappa = jnp.sqrt(wave_x * wave_x + wave_y * wave_y)
        block = order_of(n)
        eta = modes[block, 0:16, :]
        phi = modes[block, 16:32, :]
        if n % 2:
            eta = eta * odd
            phi = phi * odd
        terms = (wave_x * eta, wave_y * eta, wave_x * phi, wave_y * phi, kappa * phi)
        for f in range(5):
            tiles[f].append(terms[f])
    cosine = turn[0, half]
    sine = turn[1, half]
    parts = [[], []]
    for f in range(5):
        rows = split(jnp.concatenate(tiles[f], 0))
        kind = slice(0, 128) if f < 4 else slice(128, 256)
        both = dot3((mix[0, kind], mix[1, kind]), rows)
        first = both[:64]
        second = both[64:]
        turned = (first * cosine + second * sine).reshape(4, 2, 8, 256)
        quarter = (second * cosine - first * sine).reshape(4, 2, 8, 256)
        for a in range(2):
            parts[a].append(
                jnp.concatenate(
                    [turned[:, a].reshape(32, 256), quarter[:, a].reshape(32, 256)], 1
                )
            )
    real, imag = parts
    words = real[:4] + imag[:4] + [real[4], imag[4], -imag[4], real[4]]
    result = dot3(circles, split(jnp.concatenate(words, 0)), ((1,), (1,)))
    for q in range(3):
        out[pl.ds(q, 256, stride=3), :] = result[:, 128 * q : 128 * q + 128]


def columns_kernel(terms, source, circles, turn, gather, deal, out):
    words = split(
        jnp.concatenate([terms[pl.ds(q, 256, stride=3), :] for q in range(3)], 1)
    )
    with_cos = dot3((circles[0, :, :256], circles[1, :, :256]), words)
    with_sin = dot3((circles[0, :, 256:], circles[1, :, 256:]), words)
    real = with_cos[:, :128] - with_sin[:, 128:256]
    imag = with_sin[:, :128] + with_cos[:, 128:256]
    lane = iota((256, 128), 1)
    rolled = pltpu.roll(with_sin[:, 256:], 64, 1)
    lift = with_cos[:, 256:] + jnp.where(lane < 64, rolled, -rolled)
    cosine = turn[0]
    sine = turn[1]
    slopes = split(
        jnp.concatenate([real * cosine - imag * sine, real * sine + imag * cosine], 1)
    )
    lift = split(lift * cosine + pltpu.roll(lift, 64, 1) * sine)
    fields = dot3(slopes, (gather[0, :, :512], gather[1, :, :512]))
    lift = dot3(lift, (gather[0, :128, 512:], gather[1, :128, 512:]))
    slope_ex, slope_ey, slope_px, slope_py = (
        fields[:, 128 * k : 128 * k + 128] for k in range(4)
    )
    first_order = lift * (slope_ex * slope_ex + slope_ey * slope_ey) - (
        slope_px * slope_ex + slope_py * slope_ey
    )
    second_term = 0.5 * (lift * lift - slope_px * slope_px - slope_py * slope_py)
    products = jnp.concatenate([first_order, second_term], 1) * (time_step * spread)
    both = dot3(split(products), deal)
    first = both[:, :128]
    second = both[:, 128:]
    turned = jnp.concatenate([first * cosine + second * sine, second * cosine - first * sine], 0)
    out[pl.ds(0, 256, stride=3), :] = dot3(circles, split(turned))
    out[pl.ds(1, 256, stride=3), :] = source[:, :128]
    out[pl.ds(2, 256, stride=3), :] = source[:, 128:]


def rows_back_kernel(
    place, terms, places, beyond, circles, main_turn, zone_turn, main_mix, zone_mix, out
):
    half = place[2]
    cells = jnp.concatenate(
        [terms[pl.ds(1, 256, stride=3), :], terms[pl.ds(2, 256, stride=3), :]], 1
    ).T
    far = cells * jnp.concatenate([beyond[...], beyond[...]], 0)
    cells = jnp.concatenate(split(jnp.concatenate([cells - far, far], 1)), 1)
    grid = dot(cells, jnp.concatenate([places[...], places[...]], 0))
    main = terms[pl.ds(0, 256, stride=3), :].T
    both = dot3(split(jnp.concatenate([main, grid], 0)), circles)

    def turned(lines, cosine, sine):
        with_cos = lines[:, :, :256]
        with_sin = lines[:, :, 256:]
        real = with_cos * cosine - with_sin * sine
        imag = with_cos * sine + with_sin * cosine
        count = lines.shape[0] * lines.shape[1]
        return split(
            jnp.concatenate([real.reshape(count, 256), imag.reshape(count, 256)], 0)
        )

    main = turned(both[:128].reshape(4, 32, 512), main_turn[0, half][None], main_turn[1, half][None])
    zone = turned(both[128:].reshape(2, 128, 512), zone_turn[0][None], zone_turn[1][None])
    main = dot3(main_mix, main)
    zone = dot3(zone_mix, zone)
    odd = 1.0 - 2.0 * half.astype(f32)
    for n in range(8):
        block = main[32 * n : 32 * n + 32]
        if n % 2:
            block = block * odd
        where = order_of(n)
        out[where, 0:16, :] = block[:16] + zone[16 * n : 16 * n + 16]
        out[where, 16:32, :] = block[16:]


def finish_kernel(place, terms, eta, phi, eta_next, phi_next):
    for z in range(4):
        rows = slice(8 * z, 8 * z + 8)
        own = 4 * (place[1] >> 1) + 2 * place[2] + (place[1] & 1)
        wave_x = wave_of(256 * own + iota((8, 256), 1)) * TURN_X
        wave_y = wave_of(32 * place[0] + 8 * z + iota((8, 256), 0)) * TURN_Y
        kappa = time_step * jnp.sqrt(wave_x * wave_x + wave_y * wave_y)
        for a in range(2):
            surface = eta[a, rows, :]
            potential = phi[a, rows, :]
            part_of = slice(8 * a, 8 * a + 8)
            added = terms[z, part_of, :] + terms[4 + z, part_of, :]
            eta_next[a, rows, :] = surface + kappa * potential + added
            part_of = slice(16 + 8 * a, 24 + 8 * a)
            added = terms[z, part_of, :] + terms[4 + z, part_of, :]
            phi_next[a, rows, :] = potential - (time_step * gravity) * surface + added


def call(kernel, shapes, scalars, arrays, flops=0, limit=24, types=None):
    single = isinstance(shapes, tuple)
    shapes = [shapes] if single else shapes
    types = [f32] * len(shapes) if types is None else types
    vmem = pl.BlockSpec(memory_space=pltpu.VMEM)
    smem = pl.BlockSpec(memory_space=pltpu.SMEM)
    moved = sum(4 * math.prod(s) for s in shapes) + sum(x.size * x.dtype.itemsize for x in arrays)
    result = pl.pallas_call(
        kernel,
        out_shape=[jax.ShapeDtypeStruct(s, t) for s, t in zip(shapes, types)],
        in_specs=[smem] * len(scalars) + [vmem] * len(arrays),
        out_specs=[vmem] * len(shapes),
        compiler_params=pltpu.CompilerParams(vmem_limit_bytes=limit * 1024 * 1024),
        cost_estimate=pl.CostEstimate(flops=flops, bytes_accessed=moved, transcendentals=0),
        name=kernel.__name__,
    )(*scalars, *arrays)
    return result[0] if single else result


def stage_deal(eta, phi):
    return call(deal_kernel, (8, 32, 256), [], [eta, phi], limit=56, flops=2**33)


def stage_source(place, offsets, zone):
    shapes = [(256, 256), (512, 256), (128, 256)]
    types = [f32, bf16, f32]
    return call(source_kernel, shapes, [place, offsets], [zone], flops=2**26, types=types)


def stage_rows(place, modes):
    t = tables()
    arrays = [modes, t["rows_mix"], t["rows_turn"], t["turn"]]
    return call(rows_kernel, (768, 128), [place], arrays, flops=2**30)


def stage_columns(terms, source):
    t = tables()
    arrays = [terms, source, t["turn"], t["y_turn"], t["gather"], t["deal"]]
    return call(columns_kernel, (768, 128), [], arrays, flops=2**30)


def stage_rows_back(place, terms, places, beyond):
    t = tables()
    arrays = [terms, places, beyond, t["turn"], t["main_turn"], t["zone_turn"]]
    arrays += [t["main_mix"], t["zone_mix"]]
    return call(rows_back_kernel, (8, 32, 256), [place], arrays, flops=2**29)


def stage_finish(place, terms, eta, phi):
    return call(finish_kernel, [(2, 32, 256)] * 2, [place], [terms, eta, phi])


def local(eta_modes, phi_modes, zone_field, offsets):
    w, h, c, core = (lax.axis_index(axis) for axis in ("wide", "high", "half", "core"))
    place = jnp.stack([w, 2 * h + core, c]).astype(jnp.int32)
    swap = functools.partial(lax.all_to_all, split_axis=0, concat_axis=0, tiled=True)

    def turn(words):
        return swap(words.reshape(256, 1, 384), ("wide", "high", "core")).reshape(768, 128)

    modes = swap(stage_deal(eta_modes, phi_modes), ("half", "high", "core"))
    ready = stage_source(place, offsets, zone_field)
    modes, (source, places, beyond) = lax.optimization_barrier((modes, ready))
    columns = turn(stage_rows(place, modes))
    rows = turn(stage_columns(columns, source))
    terms = swap(stage_rows_back(place, rows, places, beyond), ("half", "high", "core"))
    return tuple(stage_finish(place, terms, eta_modes, phi_modes))


def solution(mesh):
    wide, narrow = mesh.devices.shape
    shape = (wide, narrow // 4, 2, 2)
    chips = Mesh(mesh.devices.reshape(shape), ("wide", "high", "half", "core"))
    modes = P(None, "wide", ("high", "half", "core"))
    in_specs = (modes, modes, P("wide", None), P())
    return jax.shard_map(
        local, mesh=chips, in_specs=in_specs, out_specs=(modes, modes), check_vma=False
    )
```

```python
import functools
import math

import jax
import jax.numpy as jnp
import ml_dtypes
import numpy as np
from jax import lax
from jax.experimental import pallas as pl
from jax.experimental.pallas import tpu as pltpu
from jax.sharding import Mesh
from jax.sharding import PartitionSpec as P

NX = 2048
NY = 2048
FINE = 4096
TURN_X = 2.0 * math.pi / NX
TURN_Y = 2.0 * math.pi / NY
time_step = 0.04
gravity = 9.81
spread = 1.0 / math.sqrt(NX * NY)
zone_scale = 1.0 / math.sqrt(4096 * 128)
f32 = jnp.float32
bf16 = jnp.bfloat16


def part(value, which):
    return np.where(which == 0, np.real(value), np.imag(value))


def angles(ints, period):
    return 2.0 * np.pi * (np.asarray(ints) % period) / period


def pair(matrix):
    high = matrix.astype(np.float32).astype(ml_dtypes.bfloat16)
    low = (matrix - high.astype(np.float64)).astype(np.float32).astype(ml_dtypes.bfloat16)
    return np.stack([high, low])


def circle(phase):
    return np.stack([np.cos(phase), np.sin(phase)]).astype(np.float32)


@functools.cache
def tables():
    out = {}
    k256 = np.arange(256)
    phase = angles(k256[:, None] * k256[None, :], 256)
    out["turn"] = pair(np.concatenate([np.cos(phase), np.sin(phase)], 1))
    row = np.arange(64)
    i, a, jj = row // 16, row // 8 % 2, row % 8
    col = np.arange(128)
    n, ca, cj = col // 16, col // 8 % 2, col % 8
    base = np.exp(1j * angles(i[:, None] * n[None, :], 8)) * (1j ** ca)[None, :]
    same = jj[:, None] == cj[None, :]
    halves = [np.where(same, part(base * s, a[:, None]), 0.0) for s in (1j, -1, 1, 1j)]
    out["rows_mix"] = pair(np.concatenate(halves, 0))
    x0 = 4 * np.arange(2)[:, None] + np.arange(64)[None, :] // 16
    out["rows_turn"] = circle(angles(x0[:, :, None] * k256, NX))
    lane = np.arange(128)
    out["y_turn"] = circle(angles(k256[:, None] * (lane % 8)[None, :], NY))
    y0 = np.arange(8)
    turn = np.exp(1j * angles((lane % 8)[:, None] * y0[None, :], 8)) * spread
    gather = np.zeros((2, 128, 4, 128))
    gather_lift = np.zeros((128, 128))
    for k in range(128):
        f, i = k // 32, k // 8 % 4
        gather[0, k, f, y0 * 4 + i] = turn[k].real
        gather[1, k, f, y0 * 4 + i] = -turn[k].imag
        if k < 64:
            gather_lift[k, y0 * 4 + i] = turn[k].real if k < 32 else -turn[k].imag
    gather = np.concatenate([gather.reshape(256, 512), np.zeros((256, 128))], 1)
    gather[:128, 512:] = gather_lift
    out["gather"] = pair(gather)
    deal = np.zeros((2, 128, 2, 128))
    for k in range(128):
        f, a, i, jj = k // 64, k // 32 % 2, k // 8 % 4, k % 8
        turn = np.exp(-1j * angles(jj * y0, 8))
        deal[f, y0 * 4 + i, 0, k] = part(turn, a)
        deal[f, y0 * 4 + i, 1, k] = part(-1j * turn, a)
    out["deal"] = pair(deal.reshape(256, 256))
    x0 = 4 * np.arange(2)[:, None] + np.arange(32)[None, :] // 8
    out["main_turn"] = circle(angles(x0[:, :, None] * k256, NX))
    cell = np.arange(128) // 8
    out["zone_turn"] = circle(angles(cell[:, None] * k256, FINE))
    row = np.arange(256)
    n, of, oa, oj = row // 32, row // 16 % 2, row // 8 % 2, row % 8
    col = np.arange(128)
    f, a, i, jj = col // 64, col // 32 % 2, col // 8 % 4, col % 8
    turn = np.exp(-1j * angles(n[:, None] * i[None, :], 8)) * (1j ** a)[None, :]
    same = (of[:, None] == f[None, :]) & (oj[:, None] == jj[None, :])
    halves = [np.where(same, part(turn * s, oa[:, None]), 0.0) for s in (1, -1j)]
    out["main_mix"] = pair(np.concatenate(halves, 1))
    row = np.arange(128)
    n, oa, oj = row // 16, row // 8 % 2, row % 8
    a, p, jj = np.arange(256) // 128, np.arange(256) // 8 % 16, np.arange(256) % 8
    signed = np.where(n < 4, n, n - 8)
    turn = np.exp(-1j * angles(signed[:, None] * p[None, :], 16)) * (1j ** a)[None, :]
    same = oj[:, None] == jj[None, :]
    halves = [np.where(same, part(turn * s, oa[:, None]), 0.0) for s in (1, -1j)]
    out["zone_mix"] = pair(np.concatenate(halves, 1))
    return out


def split(value):
    high = value.astype(bf16)
    return high, (value - high.astype(f32)).astype(bf16)


def dot(left, right, dims=((1,), (0,))):
    return lax.dot_general(left, right, (dims, ((), ())), preferred_element_type=f32)


def dot3(left, right, dims=((1,), (0,))):
    along = dims[0][0], dims[1][0]
    left = jnp.concatenate([left[0], left[0], left[1]], along[0])
    right = jnp.concatenate([right[0], right[1], right[0]], along[1])
    return dot(left, right, dims)


def iota(shape, dim):
    return lax.broadcasted_iota(jnp.int32, shape, dim)


def cos_of(phase):
    moved = phase + 512
    quarter = (moved >> 10) & 3
    angle = ((moved & 1023) - 512).astype(f32) * (2.0 * math.pi / FINE)
    square = angle * angle
    cosine = 1.0 + square * (-0.5 + square * (1.0 / 24 + square * (-1.0 / 720 + square * (1.0 / 40320))))
    sine = angle * (
        1.0 + square * (-1.0 / 6 + square * (1.0 / 120 + square * (-1.0 / 5040 + square * (1.0 / 362880))))
    )
    size = jnp.where((quarter & 1) == 0, cosine, sine)
    return jnp.where((quarter == 1) | (quarter == 2), -size, size)


def wave_of(index):
    return jnp.where(index < 1024, index, index - 2048).astype(f32)


def deal_kernel(eta, phi, out):
    for z in range(4):
        for source, base in ((eta, 0), (phi, 16)):
            for a in range(2):
                rows = source[a, 8 * z : 8 * z + 8, :]
                for c in range(2):
                    out[2 * z + c, base + 8 * a : base + 8 * a + 8, :] = rows


def source_kernel(place, offsets, zone, out, places, beyond):
    tile = place[0]
    core = place[2]
    own = 4 * core + place[1]
    ox = offsets[tile, 0]
    oy = offsets[tile, 1]
    lane = iota((128, 128), 1)
    wanted = (16 * own + (lane >> 3) - 2 * (ox & 7)) & 127
    pick = jnp.where(iota((128, 128), 0) == wanted, 1.0, 0.0).astype(bf16)
    high, low = split(zone[...] * zone_scale)
    cells = dot(high, pick) + dot(low, pick)
    phase = (iota((64, 128), 1) & 7) * (2 * oy + iota((64, 128), 0))
    real = cells * cos_of(phase)
    imag = cells * cos_of(phase + 1024)
    right = jnp.concatenate(
        [jnp.concatenate([real, imag], 1), jnp.concatenate([-imag, real], 1)], 0
    )
    lane = iota((256, 128), 1)
    g = iota((256, 128), 0)
    g = jnp.where(g < 128, g, g - 256)
    left = cos_of(8 * g * (2 * oy + (lane & 63)) + jnp.where(lane < 64, 0, 1024))
    out[...] = dot3(split(left), split(right))
    row = iota((16, 256), 0)
    spot = iota((16, 256), 1)
    edge = jnp.zeros((8, 256), jnp.int32)
    tile_of = iota((8, 256), 1) >> 2
    for t in range(0, 64, 4):
        target = jnp.zeros((16, 256), jnp.int32)
        for k in range(4):
            x = offsets[t + k, 0]
            target = jnp.where((row >> 2) == k, x >> 3, target)
            edge = jnp.where(tile_of == t + k, 2 * (x & 7), edge)
        near = (target + (row & 3) + 4 * core) & 255
        far = (target + 8) & 255
        places[4 * t : 4 * t + 16, :] = jnp.where(spot == near, 1.0, 0.0).astype(bf16)
        places[256 + 4 * t : 272 + 4 * t, :] = jnp.where(spot == far, 1.0, 0.0).astype(bf16)
    edge = jnp.where(((iota((8, 256), 1) & 3) == 0) & (core == 0), edge, 0)
    for p in range(16):
        beyond[8 * p : 8 * p + 8, :] = jnp.where(edge > p, 1.0, 0.0)


def rows_kernel(place, modes, mix, turn, circles, out):
    first_ky = 32 * place[0] + 8 * place[1]
    core = place[2]
    odd = 1.0 - 2.0 * core.astype(f32)
    wave_y = wave_of(first_ky + (iota((16, 256), 0) & 7)) * TURN_Y
    tiles = [[], [], [], [], []]
    for n in range(8):
        wave_x = wave_of(256 * n + iota((16, 256), 1)) * TURN_X
        kappa = jnp.sqrt(wave_x * wave_x + wave_y * wave_y)
        eta = modes[n, 0:16, :]
        phi = modes[n, 16:32, :]
        if n % 2:
            eta = eta * odd
            phi = phi * odd
        terms = (wave_x * eta, wave_y * eta, wave_x * phi, wave_y * phi, kappa * phi)
        for f in range(5):
            tiles[f].append(terms[f])
    cosine = turn[0, core]
    sine = turn[1, core]
    parts = [[], []]
    for f in range(5):
        rows = split(jnp.concatenate(tiles[f], 0))
        kind = slice(0, 128) if f < 4 else slice(128, 256)
        both = dot3((mix[0, kind], mix[1, kind]), rows)
        first = both[:64]
        second = both[64:]
        turned = (first * cosine + second * sine).reshape(4, 2, 8, 256)
        quarter = (second * cosine - first * sine).reshape(4, 2, 8, 256)
        for a in range(2):
            parts[a].append(
                jnp.concatenate(
                    [turned[:, a].reshape(32, 256), quarter[:, a].reshape(32, 256)], 1
                )
            )
    real, imag = parts
    words = real[:4] + imag[:4] + [real[4], imag[4], -imag[4], real[4]]
    result = dot3(circles, split(jnp.concatenate(words, 0)), ((1,), (1,)))
    for q in range(3):
        out[pl.ds(q, 256, stride=3), :] = result[:, 128 * q : 128 * q + 128]


def columns_kernel(terms, source, circles, turn, gather, deal, out):
    words = split(
        jnp.concatenate([terms[pl.ds(q, 256, stride=3), :] for q in range(3)], 1)
    )
    with_cos = dot3((circles[0, :, :256], circles[1, :, :256]), words)
    with_sin = dot3((circles[0, :, 256:], circles[1, :, 256:]), words)
    real = with_cos[:, :128] - with_sin[:, 128:256]
    imag = with_sin[:, :128] + with_cos[:, 128:256]
    lane = iota((256, 128), 1)
    rolled = pltpu.roll(with_sin[:, 256:], 64, 1)
    lift = with_cos[:, 256:] + jnp.where(lane < 64, rolled, -rolled)
    cosine = turn[0]
    sine = turn[1]
    slopes = split(
        jnp.concatenate([real * cosine - imag * sine, real * sine + imag * cosine], 1)
    )
    lift = split(lift * cosine + pltpu.roll(lift, 64, 1) * sine)
    fields = dot3(slopes, (gather[0, :, :512], gather[1, :, :512]))
    lift = dot3(lift, (gather[0, :128, 512:], gather[1, :128, 512:]))
    slope_ex, slope_ey, slope_px, slope_py = (
        fields[:, 128 * k : 128 * k + 128] for k in range(4)
    )
    first_order = lift * (slope_ex * slope_ex + slope_ey * slope_ey) - (
        slope_px * slope_ex + slope_py * slope_ey
    )
    second_term = 0.5 * (lift * lift - slope_px * slope_px - slope_py * slope_py)
    products = jnp.concatenate([first_order, second_term], 1) * (time_step * spread)
    both = dot3(split(products), deal)
    first = both[:, :128]
    second = both[:, 128:]
    turned = jnp.concatenate([first * cosine + second * sine, second * cosine - first * sine], 0)
    out[pl.ds(0, 256, stride=3), :] = dot3(circles, split(turned))
    out[pl.ds(1, 256, stride=3), :] = source[:, :128]
    out[pl.ds(2, 256, stride=3), :] = source[:, 128:]


def rows_back_kernel(
    place, terms, places, beyond, circles, main_turn, zone_turn, main_mix, zone_mix, out
):
    core = place[2]
    cells = jnp.concatenate(
        [terms[pl.ds(1, 256, stride=3), :], terms[pl.ds(2, 256, stride=3), :]], 1
    ).T
    far = cells * jnp.concatenate([beyond[...], beyond[...]], 0)
    cells = jnp.concatenate(split(jnp.concatenate([cells - far, far], 1)), 1)
    grid = dot(cells, jnp.concatenate([places[...], places[...]], 0))
    main = terms[pl.ds(0, 256, stride=3), :].T
    both = dot3(split(jnp.concatenate([main, grid], 0)), circles)

    def turned(lines, cosine, sine):
        with_cos = lines[:, :, :256]
        with_sin = lines[:, :, 256:]
        real = with_cos * cosine - with_sin * sine
        imag = with_cos * sine + with_sin * cosine
        count = lines.shape[0] * lines.shape[1]
        return split(
            jnp.concatenate([real.reshape(count, 256), imag.reshape(count, 256)], 0)
        )

    main = turned(both[:128].reshape(4, 32, 512), main_turn[0, core][None], main_turn[1, core][None])
    zone = turned(both[128:].reshape(2, 128, 512), zone_turn[0][None], zone_turn[1][None])
    main = dot3(main_mix, main)
    zone = dot3(zone_mix, zone)
    odd = 1.0 - 2.0 * core.astype(f32)
    for n in range(8):
        block = main[32 * n : 32 * n + 32]
        if n % 2:
            block = block * odd
        out[n, 0:16, :] = block[:16] + zone[16 * n : 16 * n + 16]
        out[n, 16:32, :] = block[16:]


def finish_kernel(place, terms, eta, phi, eta_next, phi_next):
    for z in range(4):
        rows = slice(8 * z, 8 * z + 8)
        wave_x = wave_of(256 * (2 * place[1] + place[2]) + iota((8, 256), 1)) * TURN_X
        wave_y = wave_of(32 * place[0] + 8 * z + iota((8, 256), 0)) * TURN_Y
        kappa = time_step * jnp.sqrt(wave_x * wave_x + wave_y * wave_y)
        for a in range(2):
            surface = eta[a, rows, :]
            potential = phi[a, rows, :]
            part_of = slice(8 * a, 8 * a + 8)
            added = terms[2 * z, part_of, :] + terms[2 * z + 1, part_of, :]
            eta_next[a, rows, :] = surface + kappa * potential + added
            part_of = slice(16 + 8 * a, 24 + 8 * a)
            added = terms[2 * z, part_of, :] + terms[2 * z + 1, part_of, :]
            phi_next[a, rows, :] = potential - (time_step * gravity) * surface + added


def call(kernel, shapes, scalars, arrays, flops=0, limit=24, types=None):
    single = isinstance(shapes, tuple)
    shapes = [shapes] if single else shapes
    types = [f32] * len(shapes) if types is None else types
    vmem = pl.BlockSpec(memory_space=pltpu.VMEM)
    smem = pl.BlockSpec(memory_space=pltpu.SMEM)
    moved = sum(4 * math.prod(s) for s in shapes) + sum(x.size * x.dtype.itemsize for x in arrays)
    result = pl.pallas_call(
        kernel,
        out_shape=[jax.ShapeDtypeStruct(s, t) for s, t in zip(shapes, types)],
        in_specs=[smem] * len(scalars) + [vmem] * len(arrays),
        out_specs=[vmem] * len(shapes),
        compiler_params=pltpu.CompilerParams(vmem_limit_bytes=limit * 1024 * 1024),
        cost_estimate=pl.CostEstimate(flops=flops, bytes_accessed=moved, transcendentals=0),
        name=kernel.__name__,
    )(*scalars, *arrays)
    return result[0] if single else result


def stage_deal(eta, phi):
    return call(deal_kernel, (8, 32, 256), [], [eta, phi], limit=56, flops=2**33)


def stage_source(place, offsets, zone):
    shapes = [(256, 256), (512, 256), (128, 256)]
    types = [f32, bf16, f32]
    return call(source_kernel, shapes, [place, offsets], [zone], flops=2**26, types=types)


def stage_rows(place, modes):
    t = tables()
    arrays = [modes, t["rows_mix"], t["rows_turn"], t["turn"]]
    return call(rows_kernel, (768, 128), [place], arrays, flops=2**30)


def stage_columns(terms, source):
    t = tables()
    arrays = [terms, source, t["turn"], t["y_turn"], t["gather"], t["deal"]]
    return call(columns_kernel, (768, 128), [], arrays, flops=2**30)


def stage_rows_back(place, terms, places, beyond):
    t = tables()
    arrays = [terms, places, beyond, t["turn"], t["main_turn"], t["zone_turn"]]
    arrays += [t["main_mix"], t["zone_mix"]]
    return call(rows_back_kernel, (8, 32, 256), [place], arrays, flops=2**29)


def stage_finish(place, terms, eta, phi):
    return call(finish_kernel, [(2, 32, 256)] * 2, [place], [terms, eta, phi])


def local(eta_modes, phi_modes, zone_field, offsets):
    place = jnp.stack([lax.axis_index(axis) for axis in ("wide", "lane", "core")]).astype(jnp.int32)
    swap = functools.partial(lax.all_to_all, split_axis=0, concat_axis=0, tiled=True)

    def turn(words):
        return swap(words.reshape(256, 1, 384), ("wide", "lane")).reshape(768, 128)

    modes = swap(stage_deal(eta_modes, phi_modes), ("lane", "core"))
    ready = stage_source(place, offsets, zone_field)
    modes, (source, places, beyond) = lax.optimization_barrier((modes, ready))
    columns = turn(stage_rows(place, modes))
    rows = turn(stage_columns(columns, source))
    terms = swap(stage_rows_back(place, rows, places, beyond), ("lane", "core"))
    return tuple(stage_finish(place, terms, eta_modes, phi_modes))


def solution(mesh):
    wide, narrow = mesh.devices.shape
    chips = Mesh(mesh.devices.reshape(wide, narrow // 2, 2), ("wide", "lane", "core"))
    modes = P(None, "wide", ("lane", "core"))
    in_specs = (modes, modes, P("wide", None), P())
    return jax.shard_map(
        local, mesh=chips, in_specs=in_specs, out_specs=(modes, modes), check_vma=False
    )
```

```python
import functools
import math

import jax
import jax.numpy as jnp
import ml_dtypes
import numpy as np
from jax import lax
from jax.experimental import pallas as pl
from jax.experimental.pallas import tpu as pltpu
from jax.sharding import Mesh
from jax.sharding import PartitionSpec as P

NX = 2048
NY = 2048
FINE = 4096
TURN_X = 2.0 * math.pi / NX
TURN_Y = 2.0 * math.pi / NY
time_step = 0.04
gravity = 9.81
spread = 1.0 / math.sqrt(NX * NY)
zone_scale = 1.0 / math.sqrt(4096 * 128)
f32 = jnp.float32
bf16 = jnp.bfloat16


def part(value, which):
    return np.where(which == 0, np.real(value), np.imag(value))


def angles(ints, period):
    return 2.0 * np.pi * (np.asarray(ints) % period) / period


def pair(matrix):
    high = matrix.astype(np.float32).astype(ml_dtypes.bfloat16)
    low = (matrix - high.astype(np.float64)).astype(np.float32).astype(ml_dtypes.bfloat16)
    return np.stack([high, low])


def circle(phase):
    return np.stack([np.cos(phase), np.sin(phase)]).astype(np.float32)


@functools.cache
def tables():
    out = {}
    k256 = np.arange(256)
    phase = angles(k256[:, None] * k256[None, :], 256)
    out["turn"] = pair(np.concatenate([np.cos(phase), np.sin(phase)], 1))
    row = np.arange(64)
    i, a, jj = row // 16, row // 8 % 2, row % 8
    col = np.arange(128)
    n, ca, cj = col // 16, col // 8 % 2, col % 8
    base = np.exp(1j * angles(i[:, None] * n[None, :], 8)) * (1j ** ca)[None, :]
    same = jj[:, None] == cj[None, :]
    halves = [np.where(same, part(base * s, a[:, None]), 0.0) for s in (1j, -1, 1, 1j)]
    out["rows_mix"] = pair(np.concatenate(halves, 0))
    x0 = 4 * np.arange(2)[:, None] + np.arange(64)[None, :] // 16
    out["rows_turn"] = circle(angles(x0[:, :, None] * k256, NX))
    lane = np.arange(128)
    out["y_turn"] = circle(angles(k256[:, None] * (lane % 8)[None, :], NY))
    y0 = np.arange(8)
    turn = np.exp(1j * angles((lane % 8)[:, None] * y0[None, :], 8)) * spread
    gather = np.zeros((2, 128, 4, 128))
    gather_lift = np.zeros((128, 128))
    for k in range(128):
        f, i = k // 32, k // 8 % 4
        gather[0, k, f, y0 * 4 + i] = turn[k].real
        gather[1, k, f, y0 * 4 + i] = -turn[k].imag
        if k < 64:
            gather_lift[k, y0 * 4 + i] = turn[k].real if k < 32 else -turn[k].imag
    gather = np.concatenate([gather.reshape(256, 512), np.zeros((256, 128))], 1)
    gather[:128, 512:] = gather_lift
    out["gather"] = pair(gather)
    deal = np.zeros((2, 128, 2, 128))
    for k in range(128):
        f, a, i, jj = k // 64, k // 32 % 2, k // 8 % 4, k % 8
        turn = np.exp(-1j * angles(jj * y0, 8))
        deal[f, y0 * 4 + i, 0, k] = part(turn, a)
        deal[f, y0 * 4 + i, 1, k] = part(-1j * turn, a)
    out["deal"] = pair(deal.reshape(256, 256))
    x0 = 4 * np.arange(2)[:, None] + np.arange(32)[None, :] // 8
    out["main_turn"] = circle(angles(x0[:, :, None] * k256, NX))
    cell = np.arange(128) // 8
    out["zone_turn"] = circle(angles(cell[:, None] * k256, FINE))
    row = np.arange(256)
    n, of, oa, oj = row // 32, row // 16 % 2, row // 8 % 2, row % 8
    col = np.arange(128)
    f, a, i, jj = col // 64, col // 32 % 2, col // 8 % 4, col % 8
    turn = np.exp(-1j * angles(n[:, None] * i[None, :], 8)) * (1j ** a)[None, :]
    same = (of[:, None] == f[None, :]) & (oj[:, None] == jj[None, :])
    halves = [np.where(same, part(turn * s, oa[:, None]), 0.0) for s in (1, -1j)]
    out["main_mix"] = pair(np.concatenate(halves, 1))
    row = np.arange(128)
    n, oa, oj = row // 16, row // 8 % 2, row % 8
    a, p, jj = np.arange(256) // 128, np.arange(256) // 8 % 16, np.arange(256) % 8
    signed = np.where(n < 4, n, n - 8)
    turn = np.exp(-1j * angles(signed[:, None] * p[None, :], 16)) * (1j ** a)[None, :]
    same = oj[:, None] == jj[None, :]
    halves = [np.where(same, part(turn * s, oa[:, None]), 0.0) for s in (1, -1j)]
    out["zone_mix"] = pair(np.concatenate(halves, 1))
    return out


def split(value):
    high = value.astype(bf16)
    return high, (value - high.astype(f32)).astype(bf16)


def dot(left, right, dims=((1,), (0,))):
    return lax.dot_general(left, right, (dims, ((), ())), preferred_element_type=f32)


def dot3(left, right, dims=((1,), (0,))):
    along = dims[0][0], dims[1][0]
    left = jnp.concatenate([left[0], left[0], left[1]], along[0])
    right = jnp.concatenate([right[0], right[1], right[0]], along[1])
    return dot(left, right, dims)


def iota(shape, dim):
    return lax.broadcasted_iota(jnp.int32, shape, dim)


def cos_of(phase):
    moved = phase + 512
    quarter = (moved >> 10) & 3
    angle = ((moved & 1023) - 512).astype(f32) * (2.0 * math.pi / FINE)
    square = angle * angle
    cosine = 1.0 + square * (-0.5 + square * (1.0 / 24 + square * (-1.0 / 720 + square * (1.0 / 40320))))
    sine = angle * (
        1.0 + square * (-1.0 / 6 + square * (1.0 / 120 + square * (-1.0 / 5040 + square * (1.0 / 362880))))
    )
    size = jnp.where((quarter & 1) == 0, cosine, sine)
    return jnp.where((quarter == 1) | (quarter == 2), -size, size)


def wave_of(index):
    return jnp.where(index < 1024, index, index - 2048).astype(f32)


def deal_kernel(eta, phi, out):
    for z in range(4):
        for source, base in ((eta, 0), (phi, 16)):
            for a in range(2):
                rows = source[a, 8 * z : 8 * z + 8, :]
                for c in range(2):
                    out[2 * z + c, base + 8 * a : base + 8 * a + 8, :] = rows


def source_kernel(place, offsets, zone, out, places, beyond):
    tile = place[0]
    core = place[2]
    own = 4 * core + place[1]
    ox = offsets[tile, 0]
    oy = offsets[tile, 1]
    lane = iota((128, 128), 1)
    wanted = (16 * own + (lane >> 3) - 2 * (ox & 7)) & 127
    pick = jnp.where(iota((128, 128), 0) == wanted, 1.0, 0.0).astype(bf16)
    high, low = split(zone[...] * zone_scale)
    cells = dot(high, pick) + dot(low, pick)
    phase = (iota((64, 128), 1) & 7) * (2 * oy + iota((64, 128), 0))
    real = cells * cos_of(phase)
    imag = cells * cos_of(phase + 1024)
    right = jnp.concatenate(
        [jnp.concatenate([real, imag], 1), jnp.concatenate([-imag, real], 1)], 0
    )
    lane = iota((256, 128), 1)
    g = iota((256, 128), 0)
    g = jnp.where(g < 128, g, g - 256)
    left = cos_of(8 * g * (2 * oy + (lane & 63)) + jnp.where(lane < 64, 0, 1024))
    out[...] = dot3(split(left), split(right))
    row = iota((16, 256), 0)
    spot = iota((16, 256), 1)
    edge = jnp.zeros((8, 256), jnp.int32)
    tile_of = iota((8, 256), 1) >> 2
    for t in range(0, 64, 4):
        target = jnp.zeros((16, 256), jnp.int32)
        for k in range(4):
            x = offsets[t + k, 0]
            target = jnp.where((row >> 2) == k, x >> 3, target)
            edge = jnp.where(tile_of == t + k, 2 * (x & 7), edge)
        near = (target + (row & 3) + 4 * core) & 255
        far = (target + 8) & 255
        places[4 * t : 4 * t + 16, :] = jnp.where(spot == near, 1.0, 0.0).astype(bf16)
        places[256 + 4 * t : 272 + 4 * t, :] = jnp.where(spot == far, 1.0, 0.0).astype(bf16)
    edge = jnp.where(((iota((8, 256), 1) & 3) == 0) & (core == 0), edge, 0)
    for p in range(16):
        beyond[8 * p : 8 * p + 8, :] = jnp.where(edge > p, 1.0, 0.0)


def rows_kernel(place, modes, mix, turn, circles, out):
    first_ky = 32 * place[0] + 8 * place[1]
    core = place[2]
    odd = 1.0 - 2.0 * core.astype(f32)
    wave_y = wave_of(first_ky + (iota((16, 256), 0) & 7)) * TURN_Y
    tiles = [[], [], [], [], []]
    for n in range(8):
        wave_x = wave_of(256 * n + iota((16, 256), 1)) * TURN_X
        kappa = jnp.sqrt(wave_x * wave_x + wave_y * wave_y)
        eta = modes[n, 0:16, :]
        phi = modes[n, 16:32, :]
        if n % 2:
            eta = eta * odd
            phi = phi * odd
        terms = (wave_x * eta, wave_y * eta, wave_x * phi, wave_y * phi, kappa * phi)
        for f in range(5):
            tiles[f].append(terms[f])
    cosine = turn[0, core]
    sine = turn[1, core]
    parts = [[], []]
    for f in range(5):
        rows = split(jnp.concatenate(tiles[f], 0))
        kind = slice(0, 128) if f < 4 else slice(128, 256)
        both = dot3((mix[0, kind], mix[1, kind]), rows)
        first = both[:64]
        second = both[64:]
        turned = (first * cosine + second * sine).reshape(4, 2, 8, 256)
        quarter = (second * cosine - first * sine).reshape(4, 2, 8, 256)
        for a in range(2):
            parts[a].append(
                jnp.concatenate(
                    [turned[:, a].reshape(32, 256), quarter[:, a].reshape(32, 256)], 1
                )
            )
    real, imag = parts
    words = real[:4] + imag[:4] + [real[4], imag[4], -imag[4], real[4]]
    result = dot3(circles, split(jnp.concatenate(words, 0)), ((1,), (1,)))
    for q in range(3):
        out[pl.ds(q, 256, stride=3), :] = result[:, 128 * q : 128 * q + 128]


def columns_kernel(terms, source, circles, turn, gather, deal, out):
    words = split(
        jnp.concatenate([terms[pl.ds(q, 256, stride=3), :] for q in range(3)], 1)
    )
    with_cos = dot3((circles[0, :, :256], circles[1, :, :256]), words)
    with_sin = dot3((circles[0, :, 256:], circles[1, :, 256:]), words)
    real = with_cos[:, :128] - with_sin[:, 128:256]
    imag = with_sin[:, :128] + with_cos[:, 128:256]
    lane = iota((256, 128), 1)
    rolled = pltpu.roll(with_sin[:, 256:], 64, 1)
    lift = with_cos[:, 256:] + jnp.where(lane < 64, rolled, -rolled)
    cosine = turn[0]
    sine = turn[1]
    slopes = split(
        jnp.concatenate([real * cosine - imag * sine, real * sine + imag * cosine], 1)
    )
    lift = split(lift * cosine + pltpu.roll(lift, 64, 1) * sine)
    fields = dot3(slopes, (gather[0, :, :512], gather[1, :, :512]))
    lift = dot3(lift, (gather[0, :128, 512:], gather[1, :128, 512:]))
    slope_ex, slope_ey, slope_px, slope_py = (
        fields[:, 128 * k : 128 * k + 128] for k in range(4)
    )
    first_order = lift * (slope_ex * slope_ex + slope_ey * slope_ey) - (
        slope_px * slope_ex + slope_py * slope_ey
    )
    second_term = 0.5 * (lift * lift - slope_px * slope_px - slope_py * slope_py)
    products = jnp.concatenate([first_order, second_term], 1) * (time_step * spread)
    both = dot3(split(products), deal)
    first = both[:, :128]
    second = both[:, 128:]
    turned = jnp.concatenate([first * cosine + second * sine, second * cosine - first * sine], 0)
    out[pl.ds(0, 256, stride=3), :] = dot3(circles, split(turned))
    out[pl.ds(1, 256, stride=3), :] = source[:, :128]
    out[pl.ds(2, 256, stride=3), :] = source[:, 128:]


def rows_back_kernel(
    place, terms, places, beyond, circles, main_turn, zone_turn, main_mix, zone_mix, out
):
    core = place[2]
    cells = jnp.concatenate(
        [terms[pl.ds(1, 256, stride=3), :], terms[pl.ds(2, 256, stride=3), :]], 1
    ).T
    far = cells * jnp.concatenate([beyond[...], beyond[...]], 0)
    cells = jnp.concatenate(split(jnp.concatenate([cells - far, far], 1)), 1)
    grid = dot(cells, jnp.concatenate([places[...], places[...]], 0))
    main = terms[pl.ds(0, 256, stride=3), :].T
    both = dot3(split(jnp.concatenate([main, grid], 0)), circles)

    def turned(lines, cosine, sine):
        with_cos = lines[:, :, :256]
        with_sin = lines[:, :, 256:]
        real = with_cos * cosine - with_sin * sine
        imag = with_cos * sine + with_sin * cosine
        count = lines.shape[0] * lines.shape[1]
        return split(
            jnp.concatenate([real.reshape(count, 256), imag.reshape(count, 256)], 0)
        )

    main = turned(both[:128].reshape(4, 32, 512), main_turn[0, core][None], main_turn[1, core][None])
    zone = turned(both[128:].reshape(2, 128, 512), zone_turn[0][None], zone_turn[1][None])
    main = dot3(main_mix, main)
    zone = dot3(zone_mix, zone)
    odd = 1.0 - 2.0 * core.astype(f32)
    for n in range(8):
        block = main[32 * n : 32 * n + 32]
        if n % 2:
            block = block * odd
        where = 4 * (n % 2) + n // 2
        out[where, 0:16, :] = block[:16] + zone[16 * n : 16 * n + 16]
        out[where, 16:32, :] = block[16:]


def finish_kernel(place, terms, eta, phi, eta_next, phi_next):
    for z in range(4):
        rows = slice(8 * z, 8 * z + 8)
        wave_x = wave_of(256 * (2 * place[1] + place[2]) + iota((8, 256), 1)) * TURN_X
        wave_y = wave_of(32 * place[0] + 8 * z + iota((8, 256), 0)) * TURN_Y
        kappa = time_step * jnp.sqrt(wave_x * wave_x + wave_y * wave_y)
        for a in range(2):
            surface = eta[a, rows, :]
            potential = phi[a, rows, :]
            part_of = slice(8 * a, 8 * a + 8)
            added = terms[z, part_of, :] + terms[4 + z, part_of, :]
            eta_next[a, rows, :] = surface + kappa * potential + added
            part_of = slice(16 + 8 * a, 24 + 8 * a)
            added = terms[z, part_of, :] + terms[4 + z, part_of, :]
            phi_next[a, rows, :] = potential - (time_step * gravity) * surface + added


def call(kernel, shapes, scalars, arrays, flops=0, limit=24, types=None):
    single = isinstance(shapes, tuple)
    shapes = [shapes] if single else shapes
    types = [f32] * len(shapes) if types is None else types
    vmem = pl.BlockSpec(memory_space=pltpu.VMEM)
    smem = pl.BlockSpec(memory_space=pltpu.SMEM)
    moved = sum(4 * math.prod(s) for s in shapes) + sum(x.size * x.dtype.itemsize for x in arrays)
    result = pl.pallas_call(
        kernel,
        out_shape=[jax.ShapeDtypeStruct(s, t) for s, t in zip(shapes, types)],
        in_specs=[smem] * len(scalars) + [vmem] * len(arrays),
        out_specs=[vmem] * len(shapes),
        compiler_params=pltpu.CompilerParams(vmem_limit_bytes=limit * 1024 * 1024),
        cost_estimate=pl.CostEstimate(flops=flops, bytes_accessed=moved, transcendentals=0),
        name=kernel.__name__,
    )(*scalars, *arrays)
    return result[0] if single else result


def stage_deal(eta, phi):
    return call(deal_kernel, (8, 32, 256), [], [eta, phi], limit=56, flops=2**33)


def stage_source(place, offsets, zone):
    shapes = [(256, 256), (512, 256), (128, 256)]
    types = [f32, bf16, f32]
    return call(source_kernel, shapes, [place, offsets], [zone], flops=2**26, types=types)


def stage_rows(place, modes):
    t = tables()
    arrays = [modes, t["rows_mix"], t["rows_turn"], t["turn"]]
    return call(rows_kernel, (768, 128), [place], arrays, flops=2**30)


def stage_columns(terms, source):
    t = tables()
    arrays = [terms, source, t["turn"], t["y_turn"], t["gather"], t["deal"]]
    return call(columns_kernel, (768, 128), [], arrays, flops=2**30)


def stage_rows_back(place, terms, places, beyond):
    t = tables()
    arrays = [terms, places, beyond, t["turn"], t["main_turn"], t["zone_turn"]]
    arrays += [t["main_mix"], t["zone_mix"]]
    return call(rows_back_kernel, (8, 32, 256), [place], arrays, flops=2**29)


def stage_finish(place, terms, eta, phi):
    return call(finish_kernel, [(2, 32, 256)] * 2, [place], [terms, eta, phi])


def local(eta_modes, phi_modes, zone_field, offsets):
    place = jnp.stack([lax.axis_index(axis) for axis in ("wide", "lane", "core")]).astype(jnp.int32)
    swap = functools.partial(lax.all_to_all, split_axis=0, concat_axis=0, tiled=True)

    def turn(words):
        return swap(words.reshape(256, 1, 384), ("wide", "lane")).reshape(768, 128)

    modes = swap(stage_deal(eta_modes, phi_modes), ("lane", "core"))
    ready = stage_source(place, offsets, zone_field)
    modes, (source, places, beyond) = lax.optimization_barrier((modes, ready))
    columns = turn(stage_rows(place, modes))
    rows = turn(stage_columns(columns, source))
    terms = swap(stage_rows_back(place, rows, places, beyond), ("core", "lane"))
    return tuple(stage_finish(place, terms, eta_modes, phi_modes))


def solution(mesh):
    wide, narrow = mesh.devices.shape
    chips = Mesh(mesh.devices.reshape(wide, narrow // 2, 2), ("wide", "lane", "core"))
    modes = P(None, "wide", ("lane", "core"))
    in_specs = (modes, modes, P("wide", None), P())
    return jax.shard_map(
        local, mesh=chips, in_specs=in_specs, out_specs=(modes, modes), check_vma=False
    )
```

```python
import functools
import math

import jax
import jax.numpy as jnp
import ml_dtypes
import numpy as np
from jax import lax
from jax.experimental import pallas as pl
from jax.experimental.pallas import tpu as pltpu
from jax.sharding import Mesh
from jax.sharding import PartitionSpec as P

NX = 2048
NY = 2048
FINE = 4096
TURN_X = 2.0 * math.pi / NX
TURN_Y = 2.0 * math.pi / NY
time_step = 0.04
gravity = 9.81
spread = 1.0 / math.sqrt(NX * NY)
zone_scale = 1.0 / math.sqrt(4096 * 128)
f32 = jnp.float32
bf16 = jnp.bfloat16


def part(value, which):
    return np.where(which == 0, np.real(value), np.imag(value))


def angles(ints, period):
    return 2.0 * np.pi * (np.asarray(ints) % period) / period


def pair(matrix):
    high = matrix.astype(np.float32).astype(ml_dtypes.bfloat16)
    low = (matrix - high.astype(np.float64)).astype(np.float32).astype(ml_dtypes.bfloat16)
    return np.stack([high, low])


def circle(phase):
    return np.stack([np.cos(phase), np.sin(phase)]).astype(np.float32)


@functools.cache
def tables():
    out = {}
    k256 = np.arange(256)
    phase = angles(k256[:, None] * k256[None, :], 256)
    out["turn"] = pair(np.concatenate([np.cos(phase), np.sin(phase)], 1))
    row = np.arange(64)
    i, a, jj = row // 16, row // 8 % 2, row % 8
    col = np.arange(128)
    n, ca, cj = col // 16, col // 8 % 2, col % 8
    base = np.exp(1j * angles(i[:, None] * n[None, :], 8)) * (1j ** ca)[None, :]
    same = jj[:, None] == cj[None, :]
    halves = [np.where(same, part(base * s, a[:, None]), 0.0) for s in (1j, -1, 1, 1j)]
    out["rows_mix"] = pair(np.concatenate(halves, 0))
    x0 = 4 * np.arange(2)[:, None] + np.arange(64)[None, :] // 16
    out["rows_turn"] = circle(angles(x0[:, :, None] * k256, NX))
    lane = np.arange(128)
    out["y_turn"] = circle(angles(k256[:, None] * (lane % 8)[None, :], NY))
    y0 = np.arange(8)
    turn = np.exp(1j * angles((lane % 8)[:, None] * y0[None, :], 8)) * spread
    gather = np.zeros((2, 128, 4, 128))
    gather_lift = np.zeros((128, 128))
    for k in range(128):
        f, i = k // 32, k // 8 % 4
        gather[0, k, f, y0 * 4 + i] = turn[k].real
        gather[1, k, f, y0 * 4 + i] = -turn[k].imag
        if k < 64:
            gather_lift[k, y0 * 4 + i] = turn[k].real if k < 32 else -turn[k].imag
    gather = np.concatenate([gather.reshape(256, 512), np.zeros((256, 128))], 1)
    gather[:128, 512:] = gather_lift
    out["gather"] = pair(gather)
    deal = np.zeros((2, 128, 2, 128))
    for k in range(128):
        f, a, i, jj = k // 64, k // 32 % 2, k // 8 % 4, k % 8
        turn = np.exp(-1j * angles(jj * y0, 8))
        deal[f, y0 * 4 + i, 0, k] = part(turn, a)
        deal[f, y0 * 4 + i, 1, k] = part(-1j * turn, a)
    out["deal"] = pair(deal.reshape(256, 256))
    x0 = 4 * np.arange(2)[:, None] + np.arange(32)[None, :] // 8
    out["main_turn"] = circle(angles(x0[:, :, None] * k256, NX))
    cell = np.arange(128) // 8
    out["zone_turn"] = circle(angles(cell[:, None] * k256, FINE))
    row = np.arange(256)
    n, of, oa, oj = row // 32, row // 16 % 2, row // 8 % 2, row % 8
    col = np.arange(128)
    f, a, i, jj = col // 64, col // 32 % 2, col // 8 % 4, col % 8
    turn = np.exp(-1j * angles(n[:, None] * i[None, :], 8)) * (1j ** a)[None, :]
    same = (of[:, None] == f[None, :]) & (oj[:, None] == jj[None, :])
    halves = [np.where(same, part(turn * s, oa[:, None]), 0.0) for s in (1, -1j)]
    out["main_mix"] = pair(np.concatenate(halves, 1))
    row = np.arange(128)
    n, oa, oj = row // 16, row // 8 % 2, row % 8
    a, p, jj = np.arange(256) // 128, np.arange(256) // 8 % 16, np.arange(256) % 8
    signed = np.where(n < 4, n, n - 8)
    turn = np.exp(-1j * angles(signed[:, None] * p[None, :], 16)) * (1j ** a)[None, :]
    same = oj[:, None] == jj[None, :]
    halves = [np.where(same, part(turn * s, oa[:, None]), 0.0) for s in (1, -1j)]
    out["zone_mix"] = pair(np.concatenate(halves, 1))
    return out


def split(value):
    high = value.astype(bf16)
    return high, (value - high.astype(f32)).astype(bf16)


def dot(left, right, dims=((1,), (0,))):
    return lax.dot_general(left, right, (dims, ((), ())), preferred_element_type=f32)


def dot3(left, right, dims=((1,), (0,))):
    along = dims[0][0], dims[1][0]
    left = jnp.concatenate([left[0], left[0], left[1]], along[0])
    right = jnp.concatenate([right[0], right[1], right[0]], along[1])
    return dot(left, right, dims)


def iota(shape, dim):
    return lax.broadcasted_iota(jnp.int32, shape, dim)


def cos_of(phase):
    moved = phase + 512
    quarter = (moved >> 10) & 3
    angle = ((moved & 1023) - 512).astype(f32) * (2.0 * math.pi / FINE)
    square = angle * angle
    cosine = 1.0 + square * (-0.5 + square * (1.0 / 24 + square * (-1.0 / 720 + square * (1.0 / 40320))))
    sine = angle * (
        1.0 + square * (-1.0 / 6 + square * (1.0 / 120 + square * (-1.0 / 5040 + square * (1.0 / 362880))))
    )
    size = jnp.where((quarter & 1) == 0, cosine, sine)
    return jnp.where((quarter == 1) | (quarter == 2), -size, size)


def wave_of(index):
    return jnp.where(index < 1024, index, index - 2048).astype(f32)


def deal_kernel(eta, phi, out):
    for z in range(4):
        for source, base in ((eta, 0), (phi, 16)):
            for a in range(2):
                rows = source[a, 8 * z : 8 * z + 8, :]
                for c in range(2):
                    out[2 * z + c, base + 8 * a : base + 8 * a + 8, :] = rows


def source_kernel(place, offsets, zone, out, places, beyond):
    tile = place[0]
    core = place[2]
    own = 4 * core + place[1]
    ox = offsets[tile, 0]
    oy = offsets[tile, 1]
    lane = iota((128, 128), 1)
    wanted = (16 * own + (lane >> 3) - 2 * (ox & 7)) & 127
    pick = jnp.where(iota((128, 128), 0) == wanted, 1.0, 0.0).astype(bf16)
    high, low = split(zone[...] * zone_scale)
    cells = dot(high, pick) + dot(low, pick)
    phase = (iota((64, 128), 1) & 7) * (2 * oy + iota((64, 128), 0))
    real = cells * cos_of(phase)
    imag = cells * cos_of(phase + 1024)
    right = jnp.concatenate(
        [jnp.concatenate([real, imag], 1), jnp.concatenate([-imag, real], 1)], 0
    )
    lane = iota((256, 128), 1)
    g = iota((256, 128), 0)
    g = jnp.where(g < 128, g, g - 256)
    left = cos_of(8 * g * (2 * oy + (lane & 63)) + jnp.where(lane < 64, 0, 1024))
    out[...] = dot3(split(left), split(right))
    row = iota((16, 256), 0)
    spot = iota((16, 256), 1)
    edge = jnp.zeros((8, 256), jnp.int32)
    tile_of = iota((8, 256), 1) >> 2
    for t in range(0, 64, 4):
        target = jnp.zeros((16, 256), jnp.int32)
        for k in range(4):
            x = offsets[t + k, 0]
            target = jnp.where((row >> 2) == k, x >> 3, target)
            edge = jnp.where(tile_of == t + k, 2 * (x & 7), edge)
        near = (target + (row & 3) + 4 * core) & 255
        far = (target + 8) & 255
        places[4 * t : 4 * t + 16, :] = jnp.where(spot == near, 1.0, 0.0).astype(bf16)
        places[256 + 4 * t : 272 + 4 * t, :] = jnp.where(spot == far, 1.0, 0.0).astype(bf16)
    edge = jnp.where(((iota((8, 256), 1) & 3) == 0) & (core == 0), edge, 0)
    for p in range(16):
        beyond[8 * p : 8 * p + 8, :] = jnp.where(edge > p, 1.0, 0.0)


def rows_kernel(place, modes, mix, turn, circles, out):
    first_ky = 32 * place[0] + 8 * place[1]
    core = place[2]
    odd = 1.0 - 2.0 * core.astype(f32)
    wave_y = wave_of(first_ky + (iota((16, 256), 0) & 7)) * TURN_Y
    tiles = [[], [], [], [], []]
    for n in range(8):
        wave_x = wave_of(256 * n + iota((16, 256), 1)) * TURN_X
        kappa = jnp.sqrt(wave_x * wave_x + wave_y * wave_y)
        eta = modes[n, 0:16, :]
        phi = modes[n, 16:32, :]
        if n % 2:
            eta = eta * odd
            phi = phi * odd
        terms = (wave_x * eta, wave_y * eta, wave_x * phi, wave_y * phi, kappa * phi)
        for f in range(5):
            tiles[f].append(terms[f])
    cosine = turn[0, core]
    sine = turn[1, core]
    parts = [[], []]
    for f in range(5):
        rows = split(jnp.concatenate(tiles[f], 0))
        kind = slice(0, 128) if f < 4 else slice(128, 256)
        both = dot3((mix[0, kind], mix[1, kind]), rows)
        first = both[:64]
        second = both[64:]
        turned = (first * cosine + second * sine).reshape(4, 2, 8, 256)
        quarter = (second * cosine - first * sine).reshape(4, 2, 8, 256)
        for a in range(2):
            parts[a].append(
                jnp.concatenate(
                    [turned[:, a].reshape(32, 256), quarter[:, a].reshape(32, 256)], 1
                )
            )
    real, imag = parts
    words = real[:4] + imag[:4] + [real[4], imag[4], -imag[4], real[4]]
    result = dot3(circles, split(jnp.concatenate(words, 0)), ((1,), (1,)))
    for q in range(3):
        out[pl.ds(q, 256, stride=3), :] = result[:, 128 * q : 128 * q + 128]


def columns_kernel(terms, source, circles, turn, gather, deal, out):
    words = split(
        jnp.concatenate([terms[pl.ds(q, 256, stride=3), :] for q in range(3)], 1)
    )
    with_cos = dot3((circles[0, :, :256], circles[1, :, :256]), words)
    with_sin = dot3((circles[0, :, 256:], circles[1, :, 256:]), words)
    real = with_cos[:, :128] - with_sin[:, 128:256]
    imag = with_sin[:, :128] + with_cos[:, 128:256]
    lane = iota((256, 128), 1)
    rolled = pltpu.roll(with_sin[:, 256:], 64, 1)
    lift = with_cos[:, 256:] + jnp.where(lane < 64, rolled, -rolled)
    cosine = turn[0]
    sine = turn[1]
    slopes = split(
        jnp.concatenate([real * cosine - imag * sine, real * sine + imag * cosine], 1)
    )
    lift = split(lift * cosine + pltpu.roll(lift, 64, 1) * sine)
    fields = dot3(slopes, (gather[0, :, :512], gather[1, :, :512]))
    lift = dot3(lift, (gather[0, :128, 512:], gather[1, :128, 512:]))
    slope_ex, slope_ey, slope_px, slope_py = (
        fields[:, 128 * k : 128 * k + 128] for k in range(4)
    )
    first_order = lift * (slope_ex * slope_ex + slope_ey * slope_ey) - (
        slope_px * slope_ex + slope_py * slope_ey
    )
    second_term = 0.5 * (lift * lift - slope_px * slope_px - slope_py * slope_py)
    products = jnp.concatenate([first_order, second_term], 1) * (time_step * spread)
    both = dot3(split(products), deal)
    first = both[:, :128]
    second = both[:, 128:]
    turned = jnp.concatenate([first * cosine + second * sine, second * cosine - first * sine], 0)
    out[pl.ds(0, 256, stride=3), :] = dot3(circles, split(turned))
    out[pl.ds(1, 256, stride=3), :] = source[:, :128]
    out[pl.ds(2, 256, stride=3), :] = source[:, 128:]


def rows_back_kernel(
    place, terms, places, beyond, circles, main_turn, zone_turn, main_mix, zone_mix, out
):
    core = place[2]
    cells = jnp.concatenate(
        [terms[pl.ds(1, 256, stride=3), :], terms[pl.ds(2, 256, stride=3), :]], 1
    ).T
    far = cells * jnp.concatenate([beyond[...], beyond[...]], 0)
    cells = jnp.concatenate(split(jnp.concatenate([cells - far, far], 1)), 1)
    grid = dot(cells, jnp.concatenate([places[...], places[...]], 0))
    main = terms[pl.ds(0, 256, stride=3), :].T
    both = dot3(split(jnp.concatenate([main, grid], 0)), circles)

    def turned(lines, cosine, sine):
        with_cos = lines[:, :, :256]
        with_sin = lines[:, :, 256:]
        real = with_cos * cosine - with_sin * sine
        imag = with_cos * sine + with_sin * cosine
        count = lines.shape[0] * lines.shape[1]
        return split(
            jnp.concatenate([real.reshape(count, 256), imag.reshape(count, 256)], 0)
        )

    main = turned(both[:128].reshape(4, 32, 512), main_turn[0, core][None], main_turn[1, core][None])
    zone = turned(both[128:].reshape(2, 128, 512), zone_turn[0][None], zone_turn[1][None])
    main = dot3(main_mix, main)
    zone = dot3(zone_mix, zone)
    odd = 1.0 - 2.0 * core.astype(f32)
    for n in range(8):
        block = main[32 * n : 32 * n + 32]
        if n % 2:
            block = block * odd
        out[n, 0:16, :] = block[:16] + zone[16 * n : 16 * n + 16]
        out[n, 16:32, :] = block[16:]


def finish_kernel(place, terms, eta, phi, eta_next, phi_next, held, done):
    copies = []
    for k, out in enumerate((eta_next, phi_next)):
        for z in range(4):
            rows = slice(8 * z, 8 * z + 8)
            wave_x = wave_of(256 * (2 * place[1] + place[2]) + iota((8, 256), 1)) * TURN_X
            wave_y = wave_of(32 * place[0] + 8 * z + iota((8, 256), 0)) * TURN_Y
            kappa = time_step * jnp.sqrt(wave_x * wave_x + wave_y * wave_y)
            for a in range(2):
                surface = eta[a, rows, :]
                potential = phi[a, rows, :]
                part_of = slice(16 * k + 8 * a, 16 * k + 8 * a + 8)
                added = terms[2 * z, part_of, :] + terms[2 * z + 1, part_of, :]
                if k == 0:
                    held[k, a, rows, :] = surface + kappa * potential + added
                else:
                    held[k, a, rows, :] = potential - (time_step * gravity) * surface + added
        copies.append(pltpu.make_async_copy(held.at[k], out, done.at[k]))
        copies[-1].start()
    for copy in copies:
        copy.wait()


def call(kernel, shapes, scalars, arrays, flops=0, limit=24, types=None):
    single = isinstance(shapes, tuple)
    shapes = [shapes] if single else shapes
    types = [f32] * len(shapes) if types is None else types
    vmem = pl.BlockSpec(memory_space=pltpu.VMEM)
    smem = pl.BlockSpec(memory_space=pltpu.SMEM)
    moved = sum(4 * math.prod(s) for s in shapes) + sum(x.size * x.dtype.itemsize for x in arrays)
    result = pl.pallas_call(
        kernel,
        out_shape=[jax.ShapeDtypeStruct(s, t) for s, t in zip(shapes, types)],
        in_specs=[smem] * len(scalars) + [vmem] * len(arrays),
        out_specs=[vmem] * len(shapes),
        compiler_params=pltpu.CompilerParams(vmem_limit_bytes=limit * 1024 * 1024),
        cost_estimate=pl.CostEstimate(flops=flops, bytes_accessed=moved, transcendentals=0),
        name=kernel.__name__,
    )(*scalars, *arrays)
    return result[0] if single else result


def stage_deal(eta, phi):
    return call(deal_kernel, (8, 32, 256), [], [eta, phi], limit=56, flops=2**33)


def stage_source(place, offsets, zone):
    shapes = [(256, 256), (512, 256), (128, 256)]
    types = [f32, bf16, f32]
    return call(source_kernel, shapes, [place, offsets], [zone], flops=2**26, types=types)


def stage_rows(place, modes):
    t = tables()
    arrays = [modes, t["rows_mix"], t["rows_turn"], t["turn"]]
    return call(rows_kernel, (768, 128), [place], arrays, flops=2**30)


def stage_columns(terms, source):
    t = tables()
    arrays = [terms, source, t["turn"], t["y_turn"], t["gather"], t["deal"]]
    return call(columns_kernel, (768, 128), [], arrays, flops=2**30)


def stage_rows_back(place, terms, places, beyond):
    t = tables()
    arrays = [terms, places, beyond, t["turn"], t["main_turn"], t["zone_turn"]]
    arrays += [t["main_mix"], t["zone_mix"]]
    return call(rows_back_kernel, (8, 32, 256), [place], arrays, flops=2**29)


def stage_finish(place, terms, eta, phi):
    vmem = pl.BlockSpec(memory_space=pltpu.VMEM)
    return pl.pallas_call(
        finish_kernel,
        out_shape=[jax.ShapeDtypeStruct((2, 32, 256), f32)] * 2,
        in_specs=[pl.BlockSpec(memory_space=pltpu.SMEM), vmem, vmem, vmem],
        out_specs=[pl.BlockSpec(memory_space=pl.ANY)] * 2,
        scratch_shapes=[pltpu.VMEM((2, 2, 32, 256), f32), pltpu.SemaphoreType.DMA((2,))],
        compiler_params=pltpu.CompilerParams(vmem_limit_bytes=24 * 1024 * 1024),
        cost_estimate=pl.CostEstimate(flops=2**19, bytes_accessed=2**20, transcendentals=0),
        name="finish_kernel",
    )(place, terms, eta, phi)


def local(eta_modes, phi_modes, zone_field, offsets):
    place = jnp.stack([lax.axis_index(axis) for axis in ("wide", "lane", "core")]).astype(jnp.int32)
    swap = functools.partial(lax.all_to_all, split_axis=0, concat_axis=0, tiled=True)

    def turn(words):
        return swap(words.reshape(256, 1, 384), ("wide", "lane")).reshape(768, 128)

    modes = swap(stage_deal(eta_modes, phi_modes), ("lane", "core"))
    ready = stage_source(place, offsets, zone_field)
    modes, (source, places, beyond) = lax.optimization_barrier((modes, ready))
    columns = turn(stage_rows(place, modes))
    rows = turn(stage_columns(columns, source))
    terms = swap(stage_rows_back(place, rows, places, beyond), ("lane", "core"))
    return tuple(stage_finish(place, terms, eta_modes, phi_modes))


def solution(mesh):
    wide, narrow = mesh.devices.shape
    chips = Mesh(mesh.devices.reshape(wide, narrow // 2, 2), ("wide", "lane", "core"))
    modes = P(None, "wide", ("lane", "core"))
    in_specs = (modes, modes, P("wide", None), P())
    return jax.shard_map(
        local, mesh=chips, in_specs=in_specs, out_specs=(modes, modes), check_vma=False
    )
```

```python
import functools
import math

import jax
import jax.numpy as jnp
import ml_dtypes
import numpy as np
from jax import lax
from jax.experimental import pallas as pl
from jax.experimental.pallas import tpu as pltpu
from jax.sharding import Mesh
from jax.sharding import PartitionSpec as P

NX = 2048
NY = 2048
FINE = 4096
TURN_X = 2.0 * math.pi / NX
TURN_Y = 2.0 * math.pi / NY
time_step = 0.04
gravity = 9.81
spread = 1.0 / math.sqrt(NX * NY)
zone_scale = 1.0 / math.sqrt(4096 * 128)
f32 = jnp.float32
bf16 = jnp.bfloat16


def part(value, which):
    return np.where(which == 0, np.real(value), np.imag(value))


def angles(ints, period):
    return 2.0 * np.pi * (np.asarray(ints) % period) / period


def pair(matrix):
    high = matrix.astype(np.float32).astype(ml_dtypes.bfloat16)
    low = (matrix - high.astype(np.float64)).astype(np.float32).astype(ml_dtypes.bfloat16)
    return np.stack([high, low])


def circle(phase):
    return np.stack([np.cos(phase), np.sin(phase)]).astype(np.float32)


@functools.cache
def tables():
    out = {}
    k256 = np.arange(256)
    phase = angles(k256[:, None] * k256[None, :], 256)
    out["turn"] = pair(np.concatenate([np.cos(phase), np.sin(phase)], 1))
    row = np.arange(64)
    i, a, jj = row // 16, row // 8 % 2, row % 8
    col = np.arange(128)
    n, ca, cj = col // 16, col // 8 % 2, col % 8
    base = np.exp(1j * angles(i[:, None] * n[None, :], 8)) * (1j ** ca)[None, :]
    same = jj[:, None] == cj[None, :]
    halves = [np.where(same, part(base * s, a[:, None]), 0.0) for s in (1j, -1, 1, 1j)]
    out["rows_mix"] = pair(np.concatenate(halves, 0))
    x0 = 4 * np.arange(2)[:, None] + np.arange(64)[None, :] // 16
    out["rows_turn"] = circle(angles(x0[:, :, None] * k256, NX))
    lane = np.arange(128)
    out["y_turn"] = circle(angles(k256[:, None] * (lane % 8)[None, :], NY))
    y0 = np.arange(8)
    turn = np.exp(1j * angles((lane % 8)[:, None] * y0[None, :], 8)) * spread
    gather = np.zeros((2, 128, 4, 128))
    gather_lift = np.zeros((128, 128))
    for k in range(128):
        f, i = k // 32, k // 8 % 4
        gather[0, k, f, y0 * 4 + i] = turn[k].real
        gather[1, k, f, y0 * 4 + i] = -turn[k].imag
        if k < 64:
            gather_lift[k, y0 * 4 + i] = turn[k].real if k < 32 else -turn[k].imag
    gather = np.concatenate([gather.reshape(256, 512), np.zeros((256, 128))], 1)
    gather[:128, 512:] = gather_lift
    out["gather"] = pair(gather)
    deal = np.zeros((2, 128, 2, 128))
    for k in range(128):
        f, a, i, jj = k // 64, k // 32 % 2, k // 8 % 4, k % 8
        turn = np.exp(-1j * angles(jj * y0, 8))
        deal[f, y0 * 4 + i, 0, k] = part(turn, a)
        deal[f, y0 * 4 + i, 1, k] = part(-1j * turn, a)
    out["deal"] = pair(deal.reshape(256, 256))
    x0 = 4 * np.arange(2)[:, None] + np.arange(32)[None, :] // 8
    out["main_turn"] = circle(angles(x0[:, :, None] * k256, NX))
    cell = np.arange(128) // 8
    out["zone_turn"] = circle(angles(cell[:, None] * k256, FINE))
    row = np.arange(256)
    n, of, oa, oj = row // 32, row // 16 % 2, row // 8 % 2, row % 8
    col = np.arange(128)
    f, a, i, jj = col // 64, col // 32 % 2, col // 8 % 4, col % 8
    turn = np.exp(-1j * angles(n[:, None] * i[None, :], 8)) * (1j ** a)[None, :]
    same = (of[:, None] == f[None, :]) & (oj[:, None] == jj[None, :])
    halves = [np.where(same, part(turn * s, oa[:, None]), 0.0) for s in (1, -1j)]
    out["main_mix"] = pair(np.concatenate(halves, 1))
    row = np.arange(128)
    n, oa, oj = row // 16, row // 8 % 2, row % 8
    a, p, jj = np.arange(256) // 128, np.arange(256) // 8 % 16, np.arange(256) % 8
    signed = np.where(n < 4, n, n - 8)
    turn = np.exp(-1j * angles(signed[:, None] * p[None, :], 16)) * (1j ** a)[None, :]
    same = oj[:, None] == jj[None, :]
    halves = [np.where(same, part(turn * s, oa[:, None]), 0.0) for s in (1, -1j)]
    out["zone_mix"] = pair(np.concatenate(halves, 1))
    return out


def split(value):
    high = value.astype(bf16)
    return high, (value - high.astype(f32)).astype(bf16)


def dot(left, right, dims=((1,), (0,))):
    return lax.dot_general(left, right, (dims, ((), ())), preferred_element_type=f32)


def dot3(left, right, dims=((1,), (0,))):
    along = dims[0][0], dims[1][0]
    left = jnp.concatenate([left[0], left[0], left[1]], along[0])
    right = jnp.concatenate([right[0], right[1], right[0]], along[1])
    return dot(left, right, dims)


def iota(shape, dim):
    return lax.broadcasted_iota(jnp.int32, shape, dim)


def cos_of(phase):
    moved = phase + 512
    quarter = (moved >> 10) & 3
    angle = ((moved & 1023) - 512).astype(f32) * (2.0 * math.pi / FINE)
    square = angle * angle
    cosine = 1.0 + square * (-0.5 + square * (1.0 / 24 + square * (-1.0 / 720 + square * (1.0 / 40320))))
    sine = angle * (
        1.0 + square * (-1.0 / 6 + square * (1.0 / 120 + square * (-1.0 / 5040 + square * (1.0 / 362880))))
    )
    size = jnp.where((quarter & 1) == 0, cosine, sine)
    return jnp.where((quarter == 1) | (quarter == 2), -size, size)


def wave_of(index):
    return jnp.where(index < 1024, index, index - 2048).astype(f32)


def deal_kernel(eta, phi, out):
    for z in range(4):
        for source, base in ((eta, 0), (phi, 16)):
            for a in range(2):
                rows = source[a, 8 * z : 8 * z + 8, :]
                for c in range(2):
                    out[2 * z + c, base + 8 * a : base + 8 * a + 8, :] = rows


def source_kernel(place, offsets, zone, out, places, beyond):
    tile = place[0]
    core = place[2]
    own = 4 * core + place[1]
    ox = offsets[tile, 0]
    oy = offsets[tile, 1]
    lane = iota((128, 128), 1)
    wanted = (16 * own + (lane >> 3) - 2 * (ox & 7)) & 127
    pick = jnp.where(iota((128, 128), 0) == wanted, 1.0, 0.0).astype(bf16)
    high, low = split(zone[...] * zone_scale)
    cells = dot(high, pick) + dot(low, pick)
    phase = (iota((64, 128), 1) & 7) * (2 * oy + iota((64, 128), 0))
    real = cells * cos_of(phase)
    imag = cells * cos_of(phase + 1024)
    right = jnp.concatenate(
        [jnp.concatenate([real, imag], 1), jnp.concatenate([-imag, real], 1)], 0
    )
    lane = iota((256, 128), 1)
    g = iota((256, 128), 0)
    g = jnp.where(g < 128, g, g - 256)
    left = cos_of(8 * g * (2 * oy + (lane & 63)) + jnp.where(lane < 64, 0, 1024))
    out[...] = dot3(split(left), split(right))
    row = iota((16, 256), 0)
    spot = iota((16, 256), 1)
    edge = jnp.zeros((8, 256), jnp.int32)
    tile_of = iota((8, 256), 1) >> 2
    for t in range(0, 64, 4):
        target = jnp.zeros((16, 256), jnp.int32)
        for k in range(4):
            x = offsets[t + k, 0]
            target = jnp.where((row >> 2) == k, x >> 3, target)
            edge = jnp.where(tile_of == t + k, 2 * (x & 7), edge)
        near = (target + (row & 3) + 4 * core) & 255
        far = (target + 8) & 255
        places[4 * t : 4 * t + 16, :] = jnp.where(spot == near, 1.0, 0.0).astype(bf16)
        places[256 + 4 * t : 272 + 4 * t, :] = jnp.where(spot == far, 1.0, 0.0).astype(bf16)
    edge = jnp.where(((iota((8, 256), 1) & 3) == 0) & (core == 0), edge, 0)
    for p in range(16):
        beyond[8 * p : 8 * p + 8, :] = jnp.where(edge > p, 1.0, 0.0)


def rows_kernel(place, modes, mix, turn, circles, out):
    first_ky = 32 * place[0] + 8 * place[1]
    core = place[2]
    odd = 1.0 - 2.0 * core.astype(f32)
    wave_y = wave_of(first_ky + (iota((16, 256), 0) & 7)) * TURN_Y
    tiles = [[], [], [], [], []]
    for n in range(8):
        wave_x = wave_of(256 * n + iota((16, 256), 1)) * TURN_X
        kappa = jnp.sqrt(wave_x * wave_x + wave_y * wave_y)
        eta = modes[n, 0:16, :]
        phi = modes[n, 16:32, :]
        if n % 2:
            eta = eta * odd
            phi = phi * odd
        terms = (wave_x * eta, wave_y * eta, wave_x * phi, wave_y * phi, kappa * phi)
        for f in range(5):
            tiles[f].append(terms[f])
    cosine = turn[0, core]
    sine = turn[1, core]
    parts = [[], []]
    fields = [jnp.concatenate(tile, 0) for tile in tiles]
    slopes = dot3((mix[0, :128], mix[1, :128]), split(jnp.concatenate(fields[:4], 1)))
    lift = dot3((mix[0, 128:], mix[1, 128:]), split(fields[4]))
    for f in range(5):
        both = slopes[:, 256 * f : 256 * f + 256] if f < 4 else lift
        first = both[:64]
        second = both[64:]
        turned = (first * cosine + second * sine).reshape(4, 2, 8, 256)
        quarter = (second * cosine - first * sine).reshape(4, 2, 8, 256)
        for a in range(2):
            parts[a].append(
                jnp.concatenate(
                    [turned[:, a].reshape(32, 256), quarter[:, a].reshape(32, 256)], 1
                )
            )
    real, imag = parts
    words = real[:4] + imag[:4] + [real[4], imag[4], -imag[4], real[4]]
    result = dot3(circles, split(jnp.concatenate(words, 0)), ((1,), (1,)))
    for q in range(3):
        out[pl.ds(q, 256, stride=3), :] = result[:, 128 * q : 128 * q + 128]


def columns_kernel(terms, source, circles, turn, gather, deal, out):
    words = split(
        jnp.concatenate([terms[pl.ds(q, 256, stride=3), :] for q in range(3)], 1)
    )
    with_cos = dot3((circles[0, :, :256], circles[1, :, :256]), words)
    with_sin = dot3((circles[0, :, 256:], circles[1, :, 256:]), words)
    real = with_cos[:, :128] - with_sin[:, 128:256]
    imag = with_sin[:, :128] + with_cos[:, 128:256]
    lane = iota((256, 128), 1)
    rolled = pltpu.roll(with_sin[:, 256:], 64, 1)
    lift = with_cos[:, 256:] + jnp.where(lane < 64, rolled, -rolled)
    cosine = turn[0]
    sine = turn[1]
    slopes = split(
        jnp.concatenate([real * cosine - imag * sine, real * sine + imag * cosine], 1)
    )
    lift = split(lift * cosine + pltpu.roll(lift, 64, 1) * sine)
    fields = dot3(slopes, (gather[0, :, :512], gather[1, :, :512]))
    lift = dot3(lift, (gather[0, :128, 512:], gather[1, :128, 512:]))
    slope_ex, slope_ey, slope_px, slope_py = (
        fields[:, 128 * k : 128 * k + 128] for k in range(4)
    )
    first_order = lift * (slope_ex * slope_ex + slope_ey * slope_ey) - (
        slope_px * slope_ex + slope_py * slope_ey
    )
    second_term = 0.5 * (lift * lift - slope_px * slope_px - slope_py * slope_py)
    products = jnp.concatenate([first_order, second_term], 1) * (time_step * spread)
    both = dot3(split(products), deal)
    first = both[:, :128]
    second = both[:, 128:]
    turned = jnp.concatenate([first * cosine + second * sine, second * cosine - first * sine], 0)
    out[pl.ds(0, 256, stride=3), :] = dot3(circles, split(turned))
    out[pl.ds(1, 256, stride=3), :] = source[:, :128]
    out[pl.ds(2, 256, stride=3), :] = source[:, 128:]


def rows_back_kernel(
    place, terms, places, beyond, circles, main_turn, zone_turn, main_mix, zone_mix, out
):
    core = place[2]
    cells = jnp.concatenate(
        [terms[pl.ds(1, 256, stride=3), :], terms[pl.ds(2, 256, stride=3), :]], 1
    ).T
    far = cells * jnp.concatenate([beyond[...], beyond[...]], 0)
    cells = jnp.concatenate(split(jnp.concatenate([cells - far, far], 1)), 1)
    grid = dot(cells, jnp.concatenate([places[...], places[...]], 0))
    main = terms[pl.ds(0, 256, stride=3), :].T
    both = dot3(split(jnp.concatenate([main, grid], 0)), circles)

    def turned(lines, cosine, sine):
        with_cos = lines[:, :, :256]
        with_sin = lines[:, :, 256:]
        real = with_cos * cosine - with_sin * sine
        imag = with_cos * sine + with_sin * cosine
        count = lines.shape[0] * lines.shape[1]
        return split(
            jnp.concatenate([real.reshape(count, 256), imag.reshape(count, 256)], 0)
        )

    main = turned(both[:128].reshape(4, 32, 512), main_turn[0, core][None], main_turn[1, core][None])
    zone = turned(both[128:].reshape(2, 128, 512), zone_turn[0][None], zone_turn[1][None])
    main = dot3(main_mix, main)
    zone = dot3(zone_mix, zone)
    odd = 1.0 - 2.0 * core.astype(f32)
    for n in range(8):
        block = main[32 * n : 32 * n + 32]
        if n % 2:
            block = block * odd
        out[n, 0:16, :] = block[:16] + zone[16 * n : 16 * n + 16]
        out[n, 16:32, :] = block[16:]


def finish_kernel(place, terms, eta, phi, eta_next, phi_next):
    for z in range(4):
        rows = slice(8 * z, 8 * z + 8)
        wave_x = wave_of(256 * (2 * place[1] + place[2]) + iota((8, 256), 1)) * TURN_X
        wave_y = wave_of(32 * place[0] + 8 * z + iota((8, 256), 0)) * TURN_Y
        kappa = time_step * jnp.sqrt(wave_x * wave_x + wave_y * wave_y)
        for a in range(2):
            surface = eta[a, rows, :]
            potential = phi[a, rows, :]
            part_of = slice(8 * a, 8 * a + 8)
            added = terms[2 * z, part_of, :] + terms[2 * z + 1, part_of, :]
            eta_next[a, rows, :] = surface + kappa * potential + added
            part_of = slice(16 + 8 * a, 24 + 8 * a)
            added = terms[2 * z, part_of, :] + terms[2 * z + 1, part_of, :]
            phi_next[a, rows, :] = potential - (time_step * gravity) * surface + added


def call(kernel, shapes, scalars, arrays, flops=0, limit=24, types=None):
    single = isinstance(shapes, tuple)
    shapes = [shapes] if single else shapes
    types = [f32] * len(shapes) if types is None else types
    vmem = pl.BlockSpec(memory_space=pltpu.VMEM)
    smem = pl.BlockSpec(memory_space=pltpu.SMEM)
    moved = sum(4 * math.prod(s) for s in shapes) + sum(x.size * x.dtype.itemsize for x in arrays)
    result = pl.pallas_call(
        kernel,
        out_shape=[jax.ShapeDtypeStruct(s, t) for s, t in zip(shapes, types)],
        in_specs=[smem] * len(scalars) + [vmem] * len(arrays),
        out_specs=[vmem] * len(shapes),
        compiler_params=pltpu.CompilerParams(vmem_limit_bytes=limit * 1024 * 1024),
        cost_estimate=pl.CostEstimate(flops=flops, bytes_accessed=moved, transcendentals=0),
        name=kernel.__name__,
    )(*scalars, *arrays)
    return result[0] if single else result


def stage_deal(eta, phi):
    return call(deal_kernel, (8, 32, 256), [], [eta, phi], limit=56, flops=2**33)


def stage_source(place, offsets, zone):
    shapes = [(256, 256), (512, 256), (128, 256)]
    types = [f32, bf16, f32]
    return call(source_kernel, shapes, [place, offsets], [zone], flops=2**26, types=types)


def stage_rows(place, modes):
    t = tables()
    arrays = [modes, t["rows_mix"], t["rows_turn"], t["turn"]]
    return call(rows_kernel, (768, 128), [place], arrays, flops=2**30)


def stage_columns(terms, source):
    t = tables()
    arrays = [terms, source, t["turn"], t["y_turn"], t["gather"], t["deal"]]
    return call(columns_kernel, (768, 128), [], arrays, flops=2**30)


def stage_rows_back(place, terms, places, beyond):
    t = tables()
    arrays = [terms, places, beyond, t["turn"], t["main_turn"], t["zone_turn"]]
    arrays += [t["main_mix"], t["zone_mix"]]
    return call(rows_back_kernel, (8, 32, 256), [place], arrays, flops=2**29)


def stage_finish(place, terms, eta, phi):
    return call(finish_kernel, [(2, 32, 256)] * 2, [place], [terms, eta, phi])


def local(eta_modes, phi_modes, zone_field, offsets):
    place = jnp.stack([lax.axis_index(axis) for axis in ("wide", "lane", "core")]).astype(jnp.int32)
    swap = functools.partial(lax.all_to_all, split_axis=0, concat_axis=0, tiled=True)

    def turn(words):
        return swap(words.reshape(256, 1, 384), ("wide", "lane")).reshape(768, 128)

    modes = swap(stage_deal(eta_modes, phi_modes), ("lane", "core"))
    ready = stage_source(place, offsets, zone_field)
    modes, (source, places, beyond) = lax.optimization_barrier((modes, ready))
    columns = turn(stage_rows(place, modes))
    rows = turn(stage_columns(columns, source))
    terms = swap(stage_rows_back(place, rows, places, beyond), ("lane", "core"))
    return tuple(stage_finish(place, terms, eta_modes, phi_modes))


def solution(mesh):
    wide, narrow = mesh.devices.shape
    chips = Mesh(mesh.devices.reshape(wide, narrow // 2, 2), ("wide", "lane", "core"))
    modes = P(None, "wide", ("lane", "core"))
    in_specs = (modes, modes, P("wide", None), P())
    return jax.shard_map(
        local, mesh=chips, in_specs=in_specs, out_specs=(modes, modes), check_vma=False
    )
```

```python
import functools
import math

import jax
import jax.numpy as jnp
import ml_dtypes
import numpy as np
from jax import lax
from jax.experimental import pallas as pl
from jax.experimental.pallas import tpu as pltpu
from jax.sharding import Mesh
from jax.sharding import PartitionSpec as P

NX = 2048
NY = 2048
FINE = 4096
TURN_X = 2.0 * math.pi / NX
TURN_Y = 2.0 * math.pi / NY
time_step = 0.04
gravity = 9.81
spread = 1.0 / math.sqrt(NX * NY)
zone_scale = 1.0 / math.sqrt(4096 * 128)
f32 = jnp.float32
bf16 = jnp.bfloat16


def part(value, which):
    return np.where(which == 0, np.real(value), np.imag(value))


def angles(ints, period):
    return 2.0 * np.pi * (np.asarray(ints) % period) / period


def pair(matrix):
    high = matrix.astype(np.float32).astype(ml_dtypes.bfloat16)
    low = (matrix - high.astype(np.float64)).astype(np.float32).astype(ml_dtypes.bfloat16)
    return np.stack([high, low])


def circle(phase):
    return np.stack([np.cos(phase), np.sin(phase)]).astype(np.float32)


@functools.cache
def tables():
    out = {}
    k256 = np.arange(256)
    phase = angles(k256[:, None] * k256[None, :], 256)
    out["turn"] = pair(np.concatenate([np.cos(phase), np.sin(phase)], 1))
    row = np.arange(64)
    i, a, jj = row // 16, row // 8 % 2, row % 8
    col = np.arange(128)
    n, ca, cj = col // 16, col // 8 % 2, col % 8
    base = np.exp(1j * angles(i[:, None] * n[None, :], 8)) * (1j ** ca)[None, :]
    same = jj[:, None] == cj[None, :]
    halves = [np.where(same, part(base * s, a[:, None]), 0.0) for s in (1j, -1, 1, 1j)]
    out["rows_mix"] = pair(np.concatenate(halves, 0))
    x0 = 4 * np.arange(2)[:, None] + np.arange(64)[None, :] // 16
    out["rows_turn"] = circle(angles(x0[:, :, None] * k256, NX))
    lane = np.arange(128)
    out["y_turn"] = circle(angles(k256[:, None] * (lane % 8)[None, :], NY))
    y0 = np.arange(8)
    turn = np.exp(1j * angles((lane % 8)[:, None] * y0[None, :], 8)) * spread
    gather = np.zeros((2, 128, 4, 128))
    gather_lift = np.zeros((128, 128))
    for k in range(128):
        f, i = k // 32, k // 8 % 4
        gather[0, k, f, y0 * 4 + i] = turn[k].real
        gather[1, k, f, y0 * 4 + i] = -turn[k].imag
        if k < 64:
            gather_lift[k, y0 * 4 + i] = turn[k].real if k < 32 else -turn[k].imag
    gather = np.concatenate([gather.reshape(256, 512), np.zeros((256, 128))], 1)
    gather[:128, 512:] = gather_lift
    out["gather"] = pair(gather)
    deal = np.zeros((2, 128, 2, 128))
    for k in range(128):
        f, a, i, jj = k // 64, k // 32 % 2, k // 8 % 4, k % 8
        turn = np.exp(-1j * angles(jj * y0, 8))
        deal[f, y0 * 4 + i, 0, k] = part(turn, a)
        deal[f, y0 * 4 + i, 1, k] = part(-1j * turn, a)
    out["deal"] = pair(deal.reshape(256, 256))
    x0 = 4 * np.arange(2)[:, None] + np.arange(32)[None, :] // 8
    out["main_turn"] = circle(angles(x0[:, :, None] * k256, NX))
    cell = np.arange(128) // 8
    out["zone_turn"] = circle(angles(cell[:, None] * k256, FINE))
    row = np.arange(256)
    n, of, oa, oj = row // 32, row // 16 % 2, row // 8 % 2, row % 8
    col = np.arange(128)
    f, a, i, jj = col // 64, col // 32 % 2, col // 8 % 4, col % 8
    turn = np.exp(-1j * angles(n[:, None] * i[None, :], 8)) * (1j ** a)[None, :]
    same = (of[:, None] == f[None, :]) & (oj[:, None] == jj[None, :])
    halves = [np.where(same, part(turn * s, oa[:, None]), 0.0) for s in (1, -1j)]
    out["main_mix"] = pair(np.concatenate(halves, 1))
    row = np.arange(128)
    n, oa, oj = row // 16, row // 8 % 2, row % 8
    a, p, jj = np.arange(256) // 128, np.arange(256) // 8 % 16, np.arange(256) % 8
    signed = np.where(n < 4, n, n - 8)
    turn = np.exp(-1j * angles(signed[:, None] * p[None, :], 16)) * (1j ** a)[None, :]
    same = oj[:, None] == jj[None, :]
    halves = [np.where(same, part(turn * s, oa[:, None]), 0.0) for s in (1, -1j)]
    out["zone_mix"] = pair(np.concatenate(halves, 1))
    return out


def split(value):
    high = value.astype(bf16)
    return high, (value - high.astype(f32)).astype(bf16)


def dot(left, right, dims=((1,), (0,))):
    return lax.dot_general(left, right, (dims, ((), ())), preferred_element_type=f32)


def dot3(left, right, dims=((1,), (0,))):
    along = dims[0][0], dims[1][0]
    left = jnp.concatenate([left[0], left[0], left[1]], along[0])
    right = jnp.concatenate([right[0], right[1], right[0]], along[1])
    return dot(left, right, dims)


def iota(shape, dim):
    return lax.broadcasted_iota(jnp.int32, shape, dim)


def cos_of(phase):
    moved = phase + 512
    quarter = (moved >> 10) & 3
    angle = ((moved & 1023) - 512).astype(f32) * (2.0 * math.pi / FINE)
    square = angle * angle
    cosine = 1.0 + square * (-0.5 + square * (1.0 / 24 + square * (-1.0 / 720 + square * (1.0 / 40320))))
    sine = angle * (
        1.0 + square * (-1.0 / 6 + square * (1.0 / 120 + square * (-1.0 / 5040 + square * (1.0 / 362880))))
    )
    size = jnp.where((quarter & 1) == 0, cosine, sine)
    return jnp.where((quarter == 1) | (quarter == 2), -size, size)


def wave_of(index):
    return jnp.where(index < 1024, index, index - 2048).astype(f32)


def deal_kernel(eta, phi, out):
    for z in range(4):
        for source, base in ((eta, 0), (phi, 16)):
            for a in range(2):
                rows = source[a, 8 * z : 8 * z + 8, :]
                for c in range(2):
                    out[2 * z + c, base + 8 * a : base + 8 * a + 8, :] = rows


def source_kernel(place, offsets, zone, out, places, beyond):
    tile = place[0]
    core = place[2]
    own = 4 * core + place[1]
    ox = offsets[tile, 0]
    oy = offsets[tile, 1]
    lane = iota((128, 128), 1)
    wanted = (16 * own + (lane >> 3) - 2 * (ox & 7)) & 127
    pick = jnp.where(iota((128, 128), 0) == wanted, 1.0, 0.0).astype(bf16)
    high, low = split(zone[...] * zone_scale)
    cells = dot(high, pick) + dot(low, pick)
    phase = (iota((64, 128), 1) & 7) * (2 * oy + iota((64, 128), 0))
    real = cells * cos_of(phase)
    imag = cells * cos_of(phase + 1024)
    right = jnp.concatenate(
        [jnp.concatenate([real, imag], 1), jnp.concatenate([-imag, real], 1)], 0
    )
    lane = iota((256, 128), 1)
    g = iota((256, 128), 0)
    g = jnp.where(g < 128, g, g - 256)
    left = cos_of(8 * g * (2 * oy + (lane & 63)) + jnp.where(lane < 64, 0, 1024))
    out[...] = dot3(split(left), split(right))
    row = iota((16, 256), 0)
    spot = iota((16, 256), 1)
    edge = jnp.zeros((8, 256), jnp.int32)
    tile_of = iota((8, 256), 1) >> 2
    for t in range(0, 64, 4):
        target = jnp.zeros((16, 256), jnp.int32)
        for k in range(4):
            x = offsets[t + k, 0]
            target = jnp.where((row >> 2) == k, x >> 3, target)
            edge = jnp.where(tile_of == t + k, 2 * (x & 7), edge)
        near = (target + (row & 3) + 4 * core) & 255
        far = (target + 8) & 255
        places[4 * t : 4 * t + 16, :] = jnp.where(spot == near, 1.0, 0.0).astype(bf16)
        places[256 + 4 * t : 272 + 4 * t, :] = jnp.where(spot == far, 1.0, 0.0).astype(bf16)
    edge = jnp.where(((iota((8, 256), 1) & 3) == 0) & (core == 0), edge, 0)
    for p in range(16):
        beyond[8 * p : 8 * p + 8, :] = jnp.where(edge > p, 1.0, 0.0)


def rows_kernel(place, modes, mix, turn, circles, out):
    first_ky = 32 * place[0] + 8 * place[1]
    core = place[2]
    odd = 1.0 - 2.0 * core.astype(f32)
    wave_y = wave_of(first_ky + (iota((16, 256), 0) & 7)) * TURN_Y
    tiles = [[], [], [], [], []]
    for n in range(8):
        wave_x = wave_of(256 * n + iota((16, 256), 1)) * TURN_X
        kappa = jnp.sqrt(wave_x * wave_x + wave_y * wave_y)
        eta = modes[n, 0:16, :]
        phi = modes[n, 16:32, :]
        if n % 2:
            eta = eta * odd
            phi = phi * odd
        terms = (wave_x * eta, wave_y * eta, wave_x * phi, wave_y * phi, kappa * phi)
        for f in range(5):
            tiles[f].append(terms[f])
    cosine = turn[0, core]
    sine = turn[1, core]
    parts = [[], []]
    fields = [jnp.concatenate(tile, 0) for tile in tiles]
    slopes = dot3((mix[0, :128], mix[1, :128]), split(jnp.concatenate(fields[:4], 1)))
    lift = dot3((mix[0, 128:], mix[1, 128:]), split(fields[4]))
    for f in range(5):
        both = slopes[:, 256 * f : 256 * f + 256] if f < 4 else lift
        first = both[:64]
        second = both[64:]
        turned = (first * cosine + second * sine).reshape(4, 2, 8, 256)
        quarter = (second * cosine - first * sine).reshape(4, 2, 8, 256)
        for a in range(2):
            parts[a].append(
                jnp.concatenate(
                    [turned[:, a].reshape(32, 256), quarter[:, a].reshape(32, 256)], 1
                )
            )
    real, imag = parts
    words = real[:4] + imag[:4] + [real[4], imag[4], -imag[4], real[4]]
    result = dot3(circles, split(jnp.concatenate(words, 0)), ((1,), (1,)))
    for q in range(3):
        out[pl.ds(q, 256, stride=3), :] = result[:, 128 * q : 128 * q + 128]


def columns_kernel(terms, source, circles, turn, gather, deal, out):
    words = split(
        jnp.concatenate([terms[pl.ds(q, 256, stride=3), :] for q in range(3)], 1)
    )
    stacked = [jnp.concatenate([circles[k, :, :256], circles[k, :, 256:]], 0) for k in range(2)]
    both = dot3(stacked, words)
    with_cos = both[:256]
    with_sin = both[256:]
    real = with_cos[:, :128] - with_sin[:, 128:256]
    imag = with_sin[:, :128] + with_cos[:, 128:256]
    lane = iota((256, 128), 1)
    rolled = pltpu.roll(with_sin[:, 256:], 64, 1)
    lift = with_cos[:, 256:] + jnp.where(lane < 64, rolled, -rolled)
    cosine = turn[0]
    sine = turn[1]
    slopes = split(
        jnp.concatenate([real * cosine - imag * sine, real * sine + imag * cosine], 1)
    )
    lift = split(lift * cosine + pltpu.roll(lift, 64, 1) * sine)
    fields = dot3(slopes, (gather[0, :, :512], gather[1, :, :512]))
    lift = dot3(lift, (gather[0, :128, 512:], gather[1, :128, 512:]))
    slope_ex, slope_ey, slope_px, slope_py = (
        fields[:, 128 * k : 128 * k + 128] for k in range(4)
    )
    first_order = lift * (slope_ex * slope_ex + slope_ey * slope_ey) - (
        slope_px * slope_ex + slope_py * slope_ey
    )
    second_term = 0.5 * (lift * lift - slope_px * slope_px - slope_py * slope_py)
    products = jnp.concatenate([first_order, second_term], 1) * (time_step * spread)
    both = dot3(split(products), deal)
    first = both[:, :128]
    second = both[:, 128:]
    turned = jnp.concatenate([first * cosine + second * sine, second * cosine - first * sine], 0)
    out[pl.ds(0, 256, stride=3), :] = dot3(circles, split(turned))
    out[pl.ds(1, 256, stride=3), :] = source[:, :128]
    out[pl.ds(2, 256, stride=3), :] = source[:, 128:]


def rows_back_kernel(
    place, terms, places, beyond, circles, main_turn, zone_turn, main_mix, zone_mix, out
):
    core = place[2]
    cells = jnp.concatenate(
        [terms[pl.ds(1, 256, stride=3), :], terms[pl.ds(2, 256, stride=3), :]], 1
    ).T
    far = cells * jnp.concatenate([beyond[...], beyond[...]], 0)
    cells = jnp.concatenate(split(jnp.concatenate([cells - far, far], 1)), 1)
    grid = dot(cells, jnp.concatenate([places[...], places[...]], 0))
    main = terms[pl.ds(0, 256, stride=3), :].T
    both = dot3(split(jnp.concatenate([main, grid], 0)), circles)

    def turned(lines, cosine, sine):
        with_cos = lines[:, :, :256]
        with_sin = lines[:, :, 256:]
        real = with_cos * cosine - with_sin * sine
        imag = with_cos * sine + with_sin * cosine
        count = lines.shape[0] * lines.shape[1]
        return split(
            jnp.concatenate([real.reshape(count, 256), imag.reshape(count, 256)], 0)
        )

    main = turned(both[:128].reshape(4, 32, 512), main_turn[0, core][None], main_turn[1, core][None])
    zone = turned(both[128:].reshape(2, 128, 512), zone_turn[0][None], zone_turn[1][None])
    main = dot3(main_mix, main)
    zone = dot3(zone_mix, zone)
    odd = 1.0 - 2.0 * core.astype(f32)
    for n in range(8):
        block = main[32 * n : 32 * n + 32]
        if n % 2:
            block = block * odd
        out[n, 0:16, :] = block[:16] + zone[16 * n : 16 * n + 16]
        out[n, 16:32, :] = block[16:]


def finish_kernel(place, terms, eta, phi, eta_next, phi_next):
    for z in range(4):
        rows = slice(8 * z, 8 * z + 8)
        wave_x = wave_of(256 * (2 * place[1] + place[2]) + iota((8, 256), 1)) * TURN_X
        wave_y = wave_of(32 * place[0] + 8 * z + iota((8, 256), 0)) * TURN_Y
        kappa = time_step * jnp.sqrt(wave_x * wave_x + wave_y * wave_y)
        for a in range(2):
            surface = eta[a, rows, :]
            potential = phi[a, rows, :]
            part_of = slice(8 * a, 8 * a + 8)
            added = terms[2 * z, part_of, :] + terms[2 * z + 1, part_of, :]
            eta_next[a, rows, :] = surface + kappa * potential + added
            part_of = slice(16 + 8 * a, 24 + 8 * a)
            added = terms[2 * z, part_of, :] + terms[2 * z + 1, part_of, :]
            phi_next[a, rows, :] = potential - (time_step * gravity) * surface + added


def call(kernel, shapes, scalars, arrays, flops=0, limit=24, types=None):
    single = isinstance(shapes, tuple)
    shapes = [shapes] if single else shapes
    types = [f32] * len(shapes) if types is None else types
    vmem = pl.BlockSpec(memory_space=pltpu.VMEM)
    smem = pl.BlockSpec(memory_space=pltpu.SMEM)
    moved = sum(4 * math.prod(s) for s in shapes) + sum(x.size * x.dtype.itemsize for x in arrays)
    result = pl.pallas_call(
        kernel,
        out_shape=[jax.ShapeDtypeStruct(s, t) for s, t in zip(shapes, types)],
        in_specs=[smem] * len(scalars) + [vmem] * len(arrays),
        out_specs=[vmem] * len(shapes),
        compiler_params=pltpu.CompilerParams(vmem_limit_bytes=limit * 1024 * 1024),
        cost_estimate=pl.CostEstimate(flops=flops, bytes_accessed=moved, transcendentals=0),
        name=kernel.__name__,
    )(*scalars, *arrays)
    return result[0] if single else result


def stage_deal(eta, phi):
    return call(deal_kernel, (8, 32, 256), [], [eta, phi], limit=56, flops=2**33)


def stage_source(place, offsets, zone):
    shapes = [(256, 256), (512, 256), (128, 256)]
    types = [f32, bf16, f32]
    return call(source_kernel, shapes, [place, offsets], [zone], flops=2**26, types=types)


def stage_rows(place, modes):
    t = tables()
    arrays = [modes, t["rows_mix"], t["rows_turn"], t["turn"]]
    return call(rows_kernel, (768, 128), [place], arrays, flops=2**30)


def stage_columns(terms, source):
    t = tables()
    arrays = [terms, source, t["turn"], t["y_turn"], t["gather"], t["deal"]]
    return call(columns_kernel, (768, 128), [], arrays, flops=2**30)


def stage_rows_back(place, terms, places, beyond):
    t = tables()
    arrays = [terms, places, beyond, t["turn"], t["main_turn"], t["zone_turn"]]
    arrays += [t["main_mix"], t["zone_mix"]]
    return call(rows_back_kernel, (8, 32, 256), [place], arrays, flops=2**29)


def stage_finish(place, terms, eta, phi):
    return call(finish_kernel, [(2, 32, 256)] * 2, [place], [terms, eta, phi])


def local(eta_modes, phi_modes, zone_field, offsets):
    place = jnp.stack([lax.axis_index(axis) for axis in ("wide", "lane", "core")]).astype(jnp.int32)
    swap = functools.partial(lax.all_to_all, split_axis=0, concat_axis=0, tiled=True)

    def turn(words):
        return swap(words.reshape(256, 1, 384), ("wide", "lane")).reshape(768, 128)

    modes = swap(stage_deal(eta_modes, phi_modes), ("lane", "core"))
    ready = stage_source(place, offsets, zone_field)
    modes, (source, places, beyond) = lax.optimization_barrier((modes, ready))
    columns = turn(stage_rows(place, modes))
    rows = turn(stage_columns(columns, source))
    terms = swap(stage_rows_back(place, rows, places, beyond), ("lane", "core"))
    return tuple(stage_finish(place, terms, eta_modes, phi_modes))


def solution(mesh):
    wide, narrow = mesh.devices.shape
    chips = Mesh(mesh.devices.reshape(wide, narrow // 2, 2), ("wide", "lane", "core"))
    modes = P(None, "wide", ("lane", "core"))
    in_specs = (modes, modes, P("wide", None), P())
    return jax.shard_map(
        local, mesh=chips, in_specs=in_specs, out_specs=(modes, modes), check_vma=False
    )
```

```python
import functools
import math

import jax
import jax.numpy as jnp
import ml_dtypes
import numpy as np
from jax import lax
from jax.experimental import pallas as pl
from jax.experimental.pallas import tpu as pltpu
from jax.sharding import Mesh
from jax.sharding import PartitionSpec as P

NX = 2048
NY = 2048
FINE = 4096
TURN_X = 2.0 * math.pi / NX
TURN_Y = 2.0 * math.pi / NY
time_step = 0.04
gravity = 9.81
spread = 1.0 / math.sqrt(NX * NY)
zone_scale = 1.0 / math.sqrt(4096 * 128)
f32 = jnp.float32
bf16 = jnp.bfloat16


def part(value, which):
    return np.where(which == 0, np.real(value), np.imag(value))


def angles(ints, period):
    return 2.0 * np.pi * (np.asarray(ints) % period) / period


def pair(matrix):
    high = matrix.astype(np.float32).astype(ml_dtypes.bfloat16)
    low = (matrix - high.astype(np.float64)).astype(np.float32).astype(ml_dtypes.bfloat16)
    return np.stack([high, low])


def circle(phase):
    return np.stack([np.cos(phase), np.sin(phase)]).astype(np.float32)


@functools.cache
def tables():
    out = {}
    k256 = np.arange(256)
    phase = angles(k256[:, None] * k256[None, :], 256)
    out["turn"] = pair(np.concatenate([np.cos(phase), np.sin(phase)], 1))
    row = np.arange(64)
    i, a, jj = row // 16, row // 8 % 2, row % 8
    col = np.arange(128)
    n, ca, cj = col // 16, col // 8 % 2, col % 8
    base = np.exp(1j * angles(i[:, None] * n[None, :], 8)) * (1j ** ca)[None, :]
    same = jj[:, None] == cj[None, :]
    halves = [np.where(same, part(base * s, a[:, None]), 0.0) for s in (1j, -1, 1, 1j)]
    out["rows_mix"] = pair(np.concatenate(halves, 0))
    x0 = 4 * np.arange(2)[:, None] + np.arange(64)[None, :] // 16
    out["rows_turn"] = circle(angles(x0[:, :, None] * k256, NX))
    lane = np.arange(128)
    out["y_turn"] = circle(angles(k256[:, None] * (lane % 8)[None, :], NY))
    y0 = np.arange(8)
    turn = np.exp(1j * angles((lane % 8)[:, None] * y0[None, :], 8)) * spread
    gather = np.zeros((2, 128, 4, 128))
    gather_lift = np.zeros((128, 128))
    for k in range(128):
        f, i = k // 32, k // 8 % 4
        gather[0, k, f, y0 * 4 + i] = turn[k].real
        gather[1, k, f, y0 * 4 + i] = -turn[k].imag
        if k < 64:
            gather_lift[k, y0 * 4 + i] = turn[k].real if k < 32 else -turn[k].imag
    gather = np.concatenate([gather.reshape(256, 512), np.zeros((256, 128))], 1)
    gather[:128, 512:] = gather_lift
    out["gather"] = pair(gather)
    deal = np.zeros((2, 128, 2, 128))
    for k in range(128):
        f, a, i, jj = k // 64, k // 32 % 2, k // 8 % 4, k % 8
        turn = np.exp(-1j * angles(jj * y0, 8))
        deal[f, y0 * 4 + i, 0, k] = part(turn, a)
        deal[f, y0 * 4 + i, 1, k] = part(-1j * turn, a)
    out["deal"] = pair(deal.reshape(256, 256))
    x0 = 4 * np.arange(2)[:, None] + np.arange(32)[None, :] // 8
    out["main_turn"] = circle(angles(x0[:, :, None] * k256, NX))
    cell = np.arange(128) // 8
    out["zone_turn"] = circle(angles(cell[:, None] * k256, FINE))
    row = np.arange(256)
    n, of, oa, oj = row // 32, row // 16 % 2, row // 8 % 2, row % 8
    col = np.arange(128)
    f, a, i, jj = col // 64, col // 32 % 2, col // 8 % 4, col % 8
    turn = np.exp(-1j * angles(n[:, None] * i[None, :], 8)) * (1j ** a)[None, :]
    same = (of[:, None] == f[None, :]) & (oj[:, None] == jj[None, :])
    halves = [np.where(same, part(turn * s, oa[:, None]), 0.0) for s in (1, -1j)]
    out["main_mix"] = pair(np.concatenate(halves, 1))
    row = np.arange(128)
    n, oa, oj = row // 16, row // 8 % 2, row % 8
    a, p, jj = np.arange(256) // 128, np.arange(256) // 8 % 16, np.arange(256) % 8
    signed = np.where(n < 4, n, n - 8)
    turn = np.exp(-1j * angles(signed[:, None] * p[None, :], 16)) * (1j ** a)[None, :]
    same = oj[:, None] == jj[None, :]
    halves = [np.where(same, part(turn * s, oa[:, None]), 0.0) for s in (1, -1j)]
    out["zone_mix"] = pair(np.concatenate(halves, 1))
    return out


def split(value):
    high = value.astype(bf16)
    return high, (value - high.astype(f32)).astype(bf16)


def dot(left, right, dims=((1,), (0,))):
    return lax.dot_general(left, right, (dims, ((), ())), preferred_element_type=f32)


def dot3(left, right, dims=((1,), (0,))):
    along = dims[0][0], dims[1][0]
    left = jnp.concatenate([left[0], left[0], left[1]], along[0])
    right = jnp.concatenate([right[0], right[1], right[0]], along[1])
    return dot(left, right, dims)


def iota(shape, dim):
    return lax.broadcasted_iota(jnp.int32, shape, dim)


def cos_of(phase):
    moved = phase + 512
    quarter = (moved >> 10) & 3
    angle = ((moved & 1023) - 512).astype(f32) * (2.0 * math.pi / FINE)
    square = angle * angle
    cosine = 1.0 + square * (-0.5 + square * (1.0 / 24 + square * (-1.0 / 720 + square * (1.0 / 40320))))
    sine = angle * (
        1.0 + square * (-1.0 / 6 + square * (1.0 / 120 + square * (-1.0 / 5040 + square * (1.0 / 362880))))
    )
    size = jnp.where((quarter & 1) == 0, cosine, sine)
    return jnp.where((quarter == 1) | (quarter == 2), -size, size)


def wave_of(index):
    return jnp.where(index < 1024, index, index - 2048).astype(f32)


def deal_kernel(eta, phi, out):
    for z in range(4):
        for source, base in ((eta, 0), (phi, 16)):
            for a in range(2):
                rows = source[a, 8 * z : 8 * z + 8, :]
                for c in range(2):
                    out[2 * z + c, base + 8 * a : base + 8 * a + 8, :] = rows


def source_kernel(place, offsets, zone, out, places, beyond):
    tile = place[0]
    core = place[2]
    own = 4 * core + place[1]
    ox = offsets[tile, 0]
    oy = offsets[tile, 1]
    lane = iota((128, 128), 1)
    wanted = (16 * own + (lane >> 3) - 2 * (ox & 7)) & 127
    pick = jnp.where(iota((128, 128), 0) == wanted, 1.0, 0.0).astype(bf16)
    high, low = split(zone[...] * zone_scale)
    cells = dot(high, pick) + dot(low, pick)
    phase = (iota((64, 128), 1) & 7) * (2 * oy + iota((64, 128), 0))
    real = cells * cos_of(phase)
    imag = cells * cos_of(phase + 1024)
    right = jnp.concatenate(
        [jnp.concatenate([real, imag], 1), jnp.concatenate([-imag, real], 1)], 0
    )
    lane = iota((256, 128), 1)
    g = iota((256, 128), 0)
    g = jnp.where(g < 128, g, g - 256)
    left = cos_of(8 * g * (2 * oy + (lane & 63)) + jnp.where(lane < 64, 0, 1024))
    out[...] = dot3(split(left), split(right))
    row = iota((16, 256), 0)
    spot = iota((16, 256), 1)
    edge = jnp.zeros((8, 256), jnp.int32)
    tile_of = iota((8, 256), 1) >> 2
    for t in range(0, 64, 4):
        target = jnp.zeros((16, 256), jnp.int32)
        for k in range(4):
            x = offsets[t + k, 0]
            target = jnp.where((row >> 2) == k, x >> 3, target)
            edge = jnp.where(tile_of == t + k, 2 * (x & 7), edge)
        near = (target + (row & 3) + 4 * core) & 255
        far = (target + 8) & 255
        places[4 * t : 4 * t + 16, :] = jnp.where(spot == near, 1.0, 0.0).astype(bf16)
        places[256 + 4 * t : 272 + 4 * t, :] = jnp.where(spot == far, 1.0, 0.0).astype(bf16)
    edge = jnp.where(((iota((8, 256), 1) & 3) == 0) & (core == 0), edge, 0)
    for p in range(16):
        beyond[8 * p : 8 * p + 8, :] = jnp.where(edge > p, 1.0, 0.0)


def rows_kernel(place, modes, mix, turn, circles, out):
    first_ky = 32 * place[0] + 8 * place[1]
    core = place[2]
    odd = 1.0 - 2.0 * core.astype(f32)
    wave_y = wave_of(first_ky + (iota((16, 256), 0) & 7)) * TURN_Y
    tiles = [[], [], [], [], []]
    for n in range(8):
        wave_x = wave_of(256 * n + iota((16, 256), 1)) * TURN_X
        kappa = jnp.sqrt(wave_x * wave_x + wave_y * wave_y)
        eta = modes[n, 0:16, :]
        phi = modes[n, 16:32, :]
        if n % 2:
            eta = eta * odd
            phi = phi * odd
        terms = (wave_x * eta, wave_y * eta, wave_x * phi, wave_y * phi, kappa * phi)
        for f in range(5):
            tiles[f].append(terms[f])
    cosine = turn[0, core]
    sine = turn[1, core]
    parts = [[], []]
    fields = [jnp.concatenate(tile, 0) for tile in tiles]
    slopes = dot3((mix[0, :128], mix[1, :128]), split(jnp.concatenate(fields[:4], 1)))
    lift = dot3((mix[0, 128:], mix[1, 128:]), split(fields[4]))
    for f in range(5):
        both = slopes[:, 256 * f : 256 * f + 256] if f < 4 else lift
        first = both[:64]
        second = both[64:]
        turned = (first * cosine + second * sine).reshape(4, 2, 8, 256)
        quarter = (second * cosine - first * sine).reshape(4, 2, 8, 256)
        for a in range(2):
            parts[a].append(
                jnp.concatenate(
                    [turned[:, a].reshape(32, 256), quarter[:, a].reshape(32, 256)], 1
                )
            )
    real, imag = parts
    words = real[:4] + imag[:4] + [real[4], imag[4], -imag[4], real[4]]
    result = dot3(circles, split(jnp.concatenate(words, 0)), ((1,), (1,)))
    for q in range(3):
        out[pl.ds(q, 256, stride=3), :] = result[:, 128 * q : 128 * q + 128]


def columns_kernel(terms, source, circles, turn, gather, deal, out):
    words = split(
        jnp.concatenate([terms[pl.ds(q, 256, stride=3), :] for q in range(3)], 1)
    )
    with_cos = dot3((circles[0, :, :256], circles[1, :, :256]), words)
    with_sin = dot3((circles[0, :, 256:], circles[1, :, 256:]), words)
    real = with_cos[:, :128] - with_sin[:, 128:256]
    imag = with_sin[:, :128] + with_cos[:, 128:256]
    lane = iota((256, 128), 1)
    rolled = pltpu.roll(with_sin[:, 256:], 64, 1)
    lift = with_cos[:, 256:] + jnp.where(lane < 64, rolled, -rolled)
    cosine = turn[0]
    sine = turn[1]
    slopes = split(
        jnp.concatenate([real * cosine - imag * sine, real * sine + imag * cosine], 1)
    )
    lift = split(lift * cosine + pltpu.roll(lift, 64, 1) * sine)
    fields = dot3(slopes, (gather[0, :, :512], gather[1, :, :512]))
    lift = dot3(lift, (gather[0, :128, 512:], gather[1, :128, 512:]))
    slope_ex, slope_ey, slope_px, slope_py = (
        fields[:, 128 * k : 128 * k + 128] for k in range(4)
    )
    first_order = lift * (slope_ex * slope_ex + slope_ey * slope_ey) - (
        slope_px * slope_ex + slope_py * slope_ey
    )
    second_term = 0.5 * (lift * lift - slope_px * slope_px - slope_py * slope_py)
    products = jnp.concatenate([first_order, second_term], 1) * (time_step * spread)
    both = dot3(split(products), deal)
    first = both[:, :128]
    second = both[:, 128:]
    turned = jnp.concatenate([first * cosine + second * sine, second * cosine - first * sine], 0)
    out[pl.ds(0, 256, stride=3), :] = dot3(circles, split(turned))
    out[pl.ds(1, 256, stride=3), :] = source[:, :128]
    out[pl.ds(2, 256, stride=3), :] = source[:, 128:]


def rows_back_kernel(
    place, terms, places, beyond, circles, main_turn, zone_turn, main_mix, zone_mix, out
):
    core = place[2]
    cells = jnp.concatenate(
        [terms[pl.ds(1, 256, stride=3), :], terms[pl.ds(2, 256, stride=3), :]], 1
    ).T
    far = cells * jnp.concatenate([beyond[...], beyond[...]], 0)
    cells = jnp.concatenate(split(jnp.concatenate([cells - far, far], 1)), 1)
    grid = dot(cells, jnp.concatenate([places[...], places[...]], 0))
    main = terms[pl.ds(0, 256, stride=3), :].T
    both = dot3(split(jnp.concatenate([main, grid], 0)), circles)

    def turned(lines, cosine, sine):
        with_cos = lines[:, :, :256]
        with_sin = lines[:, :, 256:]
        real = with_cos * cosine - with_sin * sine
        imag = with_cos * sine + with_sin * cosine
        count = lines.shape[0] * lines.shape[1]
        return split(
            jnp.concatenate([real.reshape(count, 256), imag.reshape(count, 256)], 0)
        )

    main = turned(both[:128].reshape(4, 32, 512), main_turn[0, core][None], main_turn[1, core][None])
    zone = turned(both[128:].reshape(2, 128, 512), zone_turn[0][None], zone_turn[1][None])
    main = dot3(main_mix, main)
    zone = dot3(zone_mix, zone)
    odd = 1.0 - 2.0 * core.astype(f32)
    for n in range(8):
        block = main[32 * n : 32 * n + 32]
        if n % 2:
            block = block * odd
        out[n, 0:16, :] = block[:16] + zone[16 * n : 16 * n + 16]
        out[n, 16:32, :] = block[16:]


def finish_kernel(place, terms, eta, phi, eta_next, phi_next, held, done):
    copies = []
    for k, out in enumerate((eta_next, phi_next)):
        for z in range(4):
            rows = slice(8 * z, 8 * z + 8)
            wave_x = wave_of(256 * (2 * place[1] + place[2]) + iota((8, 256), 1)) * TURN_X
            wave_y = wave_of(32 * place[0] + 8 * z + iota((8, 256), 0)) * TURN_Y
            kappa = time_step * jnp.sqrt(wave_x * wave_x + wave_y * wave_y)
            for a in range(2):
                surface = eta[a, rows, :]
                potential = phi[a, rows, :]
                part_of = slice(16 * k + 8 * a, 16 * k + 8 * a + 8)
                added = terms[2 * z, part_of, :] + terms[2 * z + 1, part_of, :]
                if k == 0:
                    held[k, a, rows, :] = surface + kappa * potential + added
                else:
                    held[k, a, rows, :] = potential - (time_step * gravity) * surface + added
        copies.append(pltpu.make_async_copy(held.at[k], out, done.at[k]))
        copies[-1].start()
    for copy in copies:
        copy.wait()


def call(kernel, shapes, scalars, arrays, flops=0, limit=24, types=None):
    single = isinstance(shapes, tuple)
    shapes = [shapes] if single else shapes
    types = [f32] * len(shapes) if types is None else types
    vmem = pl.BlockSpec(memory_space=pltpu.VMEM)
    smem = pl.BlockSpec(memory_space=pltpu.SMEM)
    moved = sum(4 * math.prod(s) for s in shapes) + sum(x.size * x.dtype.itemsize for x in arrays)
    result = pl.pallas_call(
        kernel,
        out_shape=[jax.ShapeDtypeStruct(s, t) for s, t in zip(shapes, types)],
        in_specs=[smem] * len(scalars) + [vmem] * len(arrays),
        out_specs=[vmem] * len(shapes),
        compiler_params=pltpu.CompilerParams(vmem_limit_bytes=limit * 1024 * 1024),
        cost_estimate=pl.CostEstimate(flops=flops, bytes_accessed=moved, transcendentals=0),
        name=kernel.__name__,
    )(*scalars, *arrays)
    return result[0] if single else result


def stage_deal(eta, phi):
    return call(deal_kernel, (8, 32, 256), [], [eta, phi], limit=56, flops=2**33)


def stage_source(place, offsets, zone):
    shapes = [(256, 256), (512, 256), (128, 256)]
    types = [f32, bf16, f32]
    return call(source_kernel, shapes, [place, offsets], [zone], flops=2**26, types=types)


def stage_rows(place, modes):
    t = tables()
    arrays = [modes, t["rows_mix"], t["rows_turn"], t["turn"]]
    return call(rows_kernel, (768, 128), [place], arrays, flops=2**30)


def stage_columns(terms, source):
    t = tables()
    arrays = [terms, source, t["turn"], t["y_turn"], t["gather"], t["deal"]]
    return call(columns_kernel, (768, 128), [], arrays, flops=2**30)


def stage_rows_back(place, terms, places, beyond):
    t = tables()
    arrays = [terms, places, beyond, t["turn"], t["main_turn"], t["zone_turn"]]
    arrays += [t["main_mix"], t["zone_mix"]]
    return call(rows_back_kernel, (8, 32, 256), [place], arrays, flops=2**29)


def stage_finish(place, terms, eta, phi):
    vmem = pl.BlockSpec(memory_space=pltpu.VMEM)
    return pl.pallas_call(
        finish_kernel,
        out_shape=[jax.ShapeDtypeStruct((2, 32, 256), f32)] * 2,
        in_specs=[pl.BlockSpec(memory_space=pltpu.SMEM), vmem, vmem, vmem],
        out_specs=[pl.BlockSpec(memory_space=pl.ANY)] * 2,
        scratch_shapes=[pltpu.VMEM((2, 2, 32, 256), f32), pltpu.SemaphoreType.DMA((2,))],
        compiler_params=pltpu.CompilerParams(vmem_limit_bytes=24 * 1024 * 1024),
        cost_estimate=pl.CostEstimate(flops=2**19, bytes_accessed=2**20, transcendentals=0),
        name="finish_kernel",
    )(place, terms, eta, phi)


def local(eta_modes, phi_modes, zone_field, offsets):
    place = jnp.stack([lax.axis_index(axis) for axis in ("wide", "lane", "core")]).astype(jnp.int32)
    swap = functools.partial(lax.all_to_all, split_axis=0, concat_axis=0, tiled=True)

    def turn(words):
        return swap(words.reshape(256, 1, 384), ("wide", "lane")).reshape(768, 128)

    modes = swap(stage_deal(eta_modes, phi_modes), ("lane", "core"))
    ready = stage_source(place, offsets, zone_field)
    modes, (source, places, beyond) = lax.optimization_barrier((modes, ready))
    columns = turn(stage_rows(place, modes))
    rows = turn(stage_columns(columns, source))
    terms = swap(stage_rows_back(place, rows, places, beyond), ("lane", "core"))
    return tuple(stage_finish(place, terms, eta_modes, phi_modes))


def solution(mesh):
    wide, narrow = mesh.devices.shape
    chips = Mesh(mesh.devices.reshape(wide, narrow // 2, 2), ("wide", "lane", "core"))
    modes = P(None, "wide", ("lane", "core"))
    in_specs = (modes, modes, P("wide", None), P())
    return jax.shard_map(
        local, mesh=chips, in_specs=in_specs, out_specs=(modes, modes), check_vma=False
    )
```
